32 devices in a mesh: dp: 8 (over z, y), vocab: 4 (over x, core).
Axes of the slice: x: 2, y: 2, z: 4, core: 2. Of those that a mesh axis runs over, the one named last changes fastest.
Arguments:
- features: bfloat16 [32, 384, 32], P(('dp', 'vocab')), may hold values from -6 to 6
- scale_ids: int32 [32, 384], P(('dp', 'vocab')), may hold values from 0 to 10, as said below
- class_ids: int32 [32, 8], P(('dp', 'vocab')), may hold values from 0 to 1000
- code_targets: int32 [32, 384], P(('dp', 'vocab')), may hold values from 0 to 4095
- token_weights: float32 [32, 384], P(('dp', 'vocab')), may hold values from 0.5 to 2
- attn_weight: float32 [1024, 4096], P(('dp', 'vocab')), may hold values from -0.1875 to 0.1875
- attn_moment: float32 [1024, 4096], P(('dp', 'vocab')), may hold values from -1.1920929e-07 to 1.1920929e-07
- attn_square: float32 [1024, 4096], P(('dp', 'vocab')), may hold values from 1.9514925e-15 to 7.79113e-15
- mlp_weight: float32 [2, 1024, 4096], P(None, ('dp', 'vocab')), may hold values from -0.125 to 0.125
- mlp_moment: float32 [2, 1024, 4096], P(None, ('dp', 'vocab')), may hold values from -1.1920929e-07 to 1.1920929e-07
- mlp_square: float32 [2, 1024, 4096], P(None, ('dp', 'vocab')), may hold values from 1.9514925e-15 to 7.79113e-15
- ada_weight: float32 [1024, 8192], P(('dp', 'vocab')), may hold values from -0.1875 to 0.1875
- ada_moment: float32 [1024, 8192], P(('dp', 'vocab')), may hold values from -1.3038516e-08 to 1.3038516e-08
- ada_square: float32 [1024, 8192], P(('dp', 'vocab')), may hold values from 2.9680494e-17 to 1.1872198e-16
- embed_weight: float32 [1723, 1024], P(None, ('dp', 'vocab')), may hold values from -0.625 to 0.625
- embed_moment: float32 [1723, 1024], P(None, ('dp', 'vocab')), may hold values from -3.7252903e-08 to 3.7252903e-08
- embed_square: float32 [1723, 1024], P(None, ('dp', 'vocab')), may hold values from 1.7437292e-16 to 7.049118e-16
- gains_weight: float32 [23, 1024], P(None, ('dp', 'vocab')), may hold values from -0.8 to 1.5
- gains_moment: float32 [23, 1024], P(None, ('dp', 'vocab')), may hold values from -1.1920929e-06 to 1.1920929e-06
- gains_square: float32 [23, 1024], P(None, ('dp', 'vocab')), may hold values from 1.9514926e-13 to 7.79113e-13
- head_weight: float32 [1024, 4096], P('dp', 'vocab'), may hold values from -0.1875 to 0.1875
- head_moment: float32 [1024, 4096], P('dp', 'vocab'), may hold values from -1.1920929e-07 to 1.1920929e-07
- head_square: float32 [1024, 4096], P('dp', 'vocab'), may hold values from 1.9514925e-15 to 7.79113e-15
Outputs:
- attn_updated: float32 [1024, 4096], P(('dp', 'vocab'))
- attn_moment_new: float32 [1024, 4096], P(('dp', 'vocab'))
- attn_square_new: float32 [1024, 4096], P(('dp', 'vocab'))
- attn_copy: bfloat16 [1024, 4096], P(('dp', 'vocab'))
- mlp_updated: float32 [2, 1024, 4096], P(None, ('dp', 'vocab'))
- mlp_moment_new: float32 [2, 1024, 4096], P(None, ('dp', 'vocab'))
- mlp_square_new: float32 [2, 1024, 4096], P(None, ('dp', 'vocab'))
- mlp_copy: bfloat16 [2, 1024, 4096], P(None, ('dp', 'vocab'))
- ada_updated: float32 [1024, 8192], P(('dp', 'vocab'))
- ada_moment_new: float32 [1024, 8192], P(('dp', 'vocab'))
- ada_square_new: float32 [1024, 8192], P(('dp', 'vocab'))
- ada_copy: bfloat16 [1024, 8192], P(('dp', 'vocab'))
- embed_updated: float32 [1723, 1024], P(None, ('dp', 'vocab'))
- embed_moment_new: float32 [1723, 1024], P(None, ('dp', 'vocab'))
- embed_square_new: float32 [1723, 1024], P(None, ('dp', 'vocab'))
- embed_copy: bfloat16 [1723, 1024], P(None, ('dp', 'vocab'))
- gains_updated: float32 [23, 1024], P(None, ('dp', 'vocab'))
- gains_moment_new: float32 [23, 1024], P(None, ('dp', 'vocab'))
- gains_square_new: float32 [23, 1024], P(None, ('dp', 'vocab'))
- gains_copy: bfloat16 [23, 1024], P(None, ('dp', 'vocab'))
- head_updated: float32 [1024, 4096], P('dp', 'vocab')
- head_moment_new: float32 [1024, 4096], P('dp', 'vocab')
- head_square_new: float32 [1024, 4096], P('dp', 'vocab')
- head_copy: bfloat16 [1024, 4096], P('dp', 'vocab')
- grad_norm: float32 [], replicated
- loss_sum: float32 [], replicated
- token_count: float32 [], replicated
The draws below stay inside these ranges and needn't reach their ends.
Inputs may be any that keep to these rules, and one draw needn't show every extreme that they name: `scale_ids`: each row is packed with whole images followed by padding; an image starts with scale 0 and runs through consecutive scales holding 1, 4, 9, 16, 25, 36, 64, 100, 169, 256 tokens, so its ids never fall; 10 marks padding, and every row ends with padding.
All inputs are finite; a program needn't handle non-finite values.
Results may differ from the reference program's by a relative error of at most 0.017.
Values may be sent and summed in bfloat16 or wider, within the bound.
No kernel may reach another device: no remote copies, remote signals or barrier semaphores. Data moves between devices by JAX's collectives and lax.ppermute only.
A program may use at most 320 MiB of HBM per device.

```python
import math
import jax
import jax.numpy as jnp
from jax import lax

D = 1024
HEADS = 16
HEAD_DIM = 64
FF = 4096
V = 4096
CHANNELS = 32
CLASSES = 1001
POSITIONS = 680
LEVELS = 10
MAXIMG = 8
STEPS = 10
ROW = 384
ROWS = 32
TROWS = 1723
GROWS = 23
N_DP = 8
N_VOCAB = 4


def draw_scale_ids(key, part):
    key = jax.random.fold_in(key, 11)
    key_fill, key_pick = jax.random.split(key)
    level_ends = jnp.array([1, 5, 14, 30, 55, 91, 155, 255, 424, 680], jnp.int32)
    row_index = jnp.arange(ROWS, dtype=jnp.int32)
    data_index = row_index // N_VOCAB
    code_index = row_index % N_VOCAB
    one_third = ROW // 3
    target = one_third + one_third * data_index // max(N_DP - 1, 1) + one_third * code_index // max(N_VOCAB - 1, 1)
    target = target - jax.random.randint(key_fill, (ROWS,), 1, ROW // 16 + 3)
    wanted = jax.random.randint(key_pick, (ROWS, MAXIMG), 5, 11)
    filled = jnp.zeros((ROWS,), jnp.int32)
    lengths_list = []
    for number in range(MAXIMG):
        room_left = target - filled
        fitting = jnp.sum((level_ends[None, :] <= room_left[:, None]).astype(jnp.int32), axis=1)
        levels_used = jnp.minimum(wanted[:, number], fitting)
        image_len = jnp.where(levels_used > 0, level_ends[jnp.maximum(levels_used - 1, 0)], 0)
        lengths_list.append(image_len)
        filled = filled + image_len
    image_ends = jnp.cumsum(jnp.stack(lengths_list, axis=1), axis=1).astype(jnp.int32)
    position = jnp.arange(ROW, dtype=jnp.int32)
    image_id = jnp.sum((position[None, :, None] >= image_ends[:, None, :]).astype(jnp.int32), axis=2)
    previous = jnp.concatenate([jnp.zeros((ROWS, 1), jnp.int32), image_ends], axis=1)
    starts_at = jnp.take_along_axis(previous, jnp.minimum(image_id, MAXIMG), axis=1)
    inside = position[None, :] - starts_at
    scale_row = jnp.sum((level_ends[None, None, :] <= inside[:, :, None]).astype(jnp.int32), axis=2)
    return jnp.where(position[None, :] < filled[:, None], scale_row, LEVELS).astype(jnp.int32)


def draw_gains_weight(key, part):
    key = jax.random.fold_in(key, 5)
    key_one, key_two = jax.random.split(key)
    row_index = lax.broadcasted_iota(jnp.int32, (GROWS, D), 0)
    ff_rows = FF // D
    gate_rows = (row_index == 9 + ff_rows) | (row_index == 12 + ff_rows)
    gain_rows = (row_index == 5) | (row_index == 6)
    offsets = jnp.clip(0.2 * jax.random.normal(key_one, (GROWS, D), jnp.float32), -0.8, 0.8)
    near_one = jax.random.uniform(key_two, (GROWS, D), jnp.float32, 0.6, 1.4)
    return jnp.where(gain_rows | gate_rows, near_one, offsets)


def touch_ends(values, stream_key, smallest, top_value):
    extent = values.shape
    index_at = [jax.random.randint(jax.random.fold_in(stream_key, axis), (), 0, extent[axis]) for axis in range(len(extent))]
    values = values.at[tuple(index_at)].set(smallest)
    longest = extent.index(max(extent))
    index_at[longest] = (index_at[longest] + 1) % extent[longest]
    return values.at[tuple(index_at)].set(top_value)


def block_levels(own_key, extent, shards, smallest, top_value):
    loudness, own = 1.0, jax.random.fold_in(own_key, 6)
    for axis_at, blocks in shards:
        draws = jnp.exp(jax.random.uniform(jax.random.fold_in(own, axis_at), (blocks,), jnp.float32, smallest / len(shards), top_value / len(shards)))
        loudness = loudness * jnp.repeat(draws, extent[axis_at] // blocks).reshape([-1 if axis == axis_at else 1 for axis in range(len(extent))])
    return loudness


def scatter_about(rng, dims, width, most, cuts=(), kind=jnp.bfloat16):
    drawn = jax.random.normal(rng, dims, jnp.float32) * width
    if len(cuts) > 0:
        drawn = block_levels(rng, dims, cuts, -0.22, 0.18) * drawn
    return jnp.clip(drawn, min=-most, max=most).astype(kind)


def setup_inputs(seed: int = 0) -> dict:
    key_list = jax.random.split(jax.random.key(seed), 24)
    features = scatter_about(key_list[0], (ROWS, ROW, CHANNELS), 1.0, 6.0, ((0, 32),))
    scale_ids = draw_scale_ids(jax.random.fold_in(key_list[23], 71), 0)
    class_ids = touch_ends(jax.random.randint(key_list[2], (ROWS, MAXIMG), 0, CLASSES), jax.random.fold_in(key_list[2], 1), 0, CLASSES - 1).astype(jnp.int32)
    code_targets = touch_ends(jax.random.randint(key_list[3], (ROWS, ROW), 0, V), jax.random.fold_in(key_list[3], 1), 0, V - 1).astype(jnp.int32)
    token_weights = jnp.clip(jnp.exp(math.log(2.0) - 1.3862944 * jax.random.uniform(key_list[4], (ROWS, ROW), jnp.float32) ** block_levels(key_list[4], (ROWS, ROW), ((0, 32),), -0.2, 0.2)), 0.5, 2.0)
    attn_weight = scatter_about(key_list[5], (D, 4 * D), D ** -0.5, 0.1875, ((0, 32),), jnp.float32)
    attn_moment = scatter_about(key_list[6], (D, 4 * D), (0.00011 / (12 * D * D + 2 * D * FF + TROWS * D + GROWS * D + D * V) ** 0.5), 1.1920928955078125e-07, ((0, 32),), jnp.float32)
    attn_square = jnp.clip(jnp.exp(math.log(7.791130174556512e-15) - 1.3843914 * jax.random.uniform(key_list[7], (D, 4 * D), jnp.float32) ** block_levels(key_list[7], (D, 4 * D), ((0, 32),), -0.2, 0.2)), 1.951492547948102e-15, 7.791130174556512e-15)
    mlp_weight = scatter_about(key_list[8], (2, D, FF), (2 * D) ** -0.5, 0.125, ((1, 32),), jnp.float32)
    mlp_moment = scatter_about(key_list[9], (2, D, FF), (0.00011 / (12 * D * D + 2 * D * FF + TROWS * D + GROWS * D + D * V) ** 0.5), 1.1920928955078125e-07, ((1, 32),), jnp.float32)
    mlp_square = jnp.clip(jnp.exp(math.log(7.791130174556512e-15) - 1.3843914 * jax.random.uniform(key_list[10], (2, D, FF), jnp.float32) ** block_levels(key_list[10], (2, D, FF), ((1, 32),), -0.2, 0.2)), 1.951492547948102e-15, 7.791130174556512e-15)
    ada_weight = scatter_about(key_list[11], (D, 8 * D), D ** -0.5, 0.1875, ((0, 32),), jnp.float32)
    ada_moment = scatter_about(key_list[12], (D, 8 * D), (0.000011 / (12 * D * D + 2 * D * FF + TROWS * D + GROWS * D + D * V) ** 0.5), 1.30385160446167e-08, ((0, 32),), jnp.float32)
    ada_square = jnp.clip(jnp.exp(math.log(1.1872197753684505e-16) - 1.3862944 * jax.random.uniform(key_list[13], (D, 8 * D), jnp.float32) ** block_levels(key_list[13], (D, 8 * D), ((0, 32),), -0.2, 0.2)), 2.9680494384211263e-17, 1.1872197753684505e-16)
    embed_weight = scatter_about(key_list[14], (TROWS, D), 0.1, 0.625, ((1, 32),), jnp.float32)
    embed_moment = scatter_about(key_list[15], (TROWS, D), (0.000033 / (12 * D * D + 2 * D * FF + TROWS * D + GROWS * D + D * V) ** 0.5), 3.725290298461914e-08, ((1, 32),), jnp.float32)
    embed_square = jnp.clip(jnp.exp(math.log(7.049117771937838e-16) - 1.3968765 * jax.random.uniform(key_list[16], (TROWS, D), jnp.float32) ** block_levels(key_list[16], (TROWS, D), ((1, 32),), -0.2, 0.2)), 1.7437291567417944e-16, 7.049117771937838e-16)
    gains_weight = draw_gains_weight(jax.random.fold_in(key_list[23], 71), 0)
    gains_moment = scatter_about(key_list[18], (GROWS, D), (0.0011 / (12 * D * D + 2 * D * FF + TROWS * D + GROWS * D + D * V) ** 0.5), 1.1920928955078125e-06, ((1, 32),), jnp.float32)
    gains_square = jnp.clip(jnp.exp(math.log(7.791129937387287e-13) - 1.3843914 * jax.random.uniform(key_list[19], (GROWS, D), jnp.float32) ** block_levels(key_list[19], (GROWS, D), ((1, 32),), -0.2, 0.2)), 1.951492624181067e-13, 7.791129937387287e-13)
    head_weight = scatter_about(key_list[20], (D, V), D ** -0.5, 0.1875, ((0, 8), (1, 4)), jnp.float32)
    head_moment = scatter_about(key_list[21], (D, V), (0.00011 / (12 * D * D + 2 * D * FF + TROWS * D + GROWS * D + D * V) ** 0.5), 1.1920928955078125e-07, ((0, 8), (1, 4)), jnp.float32)
    head_square = jnp.clip(jnp.exp(math.log(7.791130174556512e-15) - 1.3843914 * jax.random.uniform(key_list[22], (D, V), jnp.float32) ** block_levels(key_list[22], (D, V), ((0, 8), (1, 4)), -0.2, 0.2)), 1.951492547948102e-15, 7.791130174556512e-15)
    return dict(features=features, scale_ids=scale_ids, class_ids=class_ids, code_targets=code_targets, token_weights=token_weights, attn_weight=attn_weight, attn_moment=attn_moment, attn_square=attn_square, mlp_weight=mlp_weight, mlp_moment=mlp_moment, mlp_square=mlp_square, ada_weight=ada_weight, ada_moment=ada_moment, ada_square=ada_square, embed_weight=embed_weight, embed_moment=embed_moment, embed_square=embed_square, gains_weight=gains_weight, gains_moment=gains_moment, gains_square=gains_square, head_weight=head_weight, head_moment=head_moment, head_square=head_square)


@jax.custom_vjp
def low(v):
    return lax.optimization_barrier(v.astype(jnp.bfloat16)).astype(jnp.float32)

@jax.custom_vjp
def low_back(v):
    return v

def low_keep(v):
    return (low(v), None)

def low_pass(kept, grad):
    return (grad,)

def back_keep(v):
    return (v, None)

def back_low(kept, grad):
    return (low(grad),)
low.defvjp(low_keep, low_pass)
low_back.defvjp(back_keep, back_low)
EPS_NORM = 1e-06
BETA_ONE = 0.9
BETA_TWO = 0.95
ADAM_EPS = 1e-08
DECAY = 0.05
CLIP_NORM = 0.001
RATES = (0.03, 0.03, 0.03, 0.15, 0.4, 0.03)
NEG_FILL = -1e+30

def multiply(left, right):
    return jnp.dot(left, right, precision=lax.Precision.HIGHEST)

def normalize(values):
    center = values - lax.optimization_barrier(jnp.mean(values, axis=-1, keepdims=True))
    return center * lax.rsqrt(lax.optimization_barrier(jnp.mean(center * center, axis=-1, keepdims=True)) + EPS_NORM)

def modulate(values, shifts, scales):
    return normalize(values) * (1.0 + scales) + shifts

def head_norm(values, gain_vec):
    return values * lax.rsqrt(lax.optimization_barrier(jnp.mean(values * values, axis=-1, keepdims=True)) + EPS_NORM) * gain_vec

def layout(scale_row):
    position = jnp.arange(scale_row.shape[0], dtype=jnp.int32)
    opening = scale_row == 0
    image_id = (jnp.cumsum(opening.astype(jnp.int32)) - 1).astype(jnp.int32)
    starts_at = lax.cummax(jnp.where(opening, position, 0), axis=0)
    return (image_id, (position - starts_at).astype(jnp.int32), scale_row < LEVELS)

def row_loss(weights, row_data):
    attn_mats, mlp_mats, ada_mats, embedding, gain_rows, head_table = weights
    features, scale_row, class_row, target_row, weight_row = row_data
    length = scale_row.shape[0]
    model_width = attn_mats.shape[0]
    ff_rows = FF // model_width
    ada_at = 7 + ff_rows
    head_at = ada_at + 8
    off_level = CLASSES + POSITIONS
    off_word = off_level + LEVELS
    image_id, inside, counted = layout(scale_row)
    resid_in = multiply(features.astype(jnp.float32), embedding[off_word:off_word + CHANNELS]) + gain_rows[0]
    pos_rows = embedding[CLASSES + jnp.minimum(inside, POSITIONS - 1)]
    resid_in = resid_in + jnp.where((inside < POSITIONS)[:, None], pos_rows, 0.0)
    level_rows = embedding[off_level + jnp.minimum(scale_row, LEVELS - 1)]
    resid_in = resid_in + jnp.where(counted[:, None], level_rows, 0.0)
    class_act = low(jax.nn.silu(embedding[class_row]))
    modulation = low_back(multiply(class_act, ada_mats) + gain_rows[ada_at:head_at].reshape(-1))
    pieces = jnp.split(modulation[image_id], 8, axis=1)
    shift_one, scale_one, gate_one, shift_two, scale_two, gate_two, shift_head, scale_head = pieces
    u_in = low(modulate(resid_in, shift_one, scale_one))
    qkv_bias = jnp.concatenate([gain_rows[1], jnp.zeros_like(gain_rows[1]), gain_rows[2]])
    qkv_out = low_back(multiply(u_in, attn_mats[:, :3 * model_width]) + qkv_bias)
    queries, keys, values = jnp.split(qkv_out, 3, axis=1)
    split_shape = (length, HEADS, HEAD_DIM)
    q_norm = low(head_norm(queries.reshape(split_shape), gain_rows[5].reshape(HEADS, HEAD_DIM)))
    k_norm = low(head_norm(keys.reshape(split_shape), gain_rows[6].reshape(HEADS, HEAD_DIM)))
    v_low = low(values.reshape(split_shape))
    scores = low_back(jnp.einsum('qhd,khd->hqk', q_norm, k_norm, precision=lax.Precision.HIGHEST) * HEAD_DIM ** (-0.5))
    allowed = (image_id[:, None] == image_id[None, :]) & (scale_row[None, :] <= scale_row[:, None])
    soft_w = jax.nn.softmax(jnp.where(allowed[None], scores, NEG_FILL), axis=-1)
    mixed_heads = jnp.einsum('hqk,khd->qhd', low(soft_w), v_low, precision=lax.Precision.HIGHEST)
    mixture = low(low_back(mixed_heads)).reshape(length, model_width)
    attn_out = low_back(multiply(mixture, attn_mats[:, 3 * model_width:]) + gain_rows[3])
    resid_mid = resid_in + gate_one * attn_out
    u_two = low(modulate(resid_mid, shift_two, scale_two))
    hidden = low_back(multiply(u_two, mlp_mats[0]) + gain_rows[7:ada_at].reshape(-1))
    active = low(jax.nn.gelu(hidden, approximate=True))
    mlp_out = low_back(multiply(active, mlp_mats[1].T) + gain_rows[4])
    resid_out = resid_mid + gate_two * mlp_out
    head_in = low(modulate(resid_out, shift_head, scale_head))
    logits = low_back(multiply(head_in, head_table) + gain_rows[head_at:].reshape(-1))
    log_total = jax.nn.logsumexp(logits, axis=-1)
    picked = jnp.take_along_axis(logits, target_row[:, None], axis=1)[:, 0]
    return jnp.sum(weight_row * counted * (log_total - picked))

def adam_step(weight, moment, square, gradient, clip_factor, step_rate):
    gradient = gradient * clip_factor
    moment = BETA_ONE * moment + (1.0 - BETA_ONE) * gradient
    square = BETA_TWO * square + (1.0 - BETA_TWO) * gradient * gradient
    first_hat = moment / (1.0 - BETA_ONE ** STEPS)
    second_hat = square / (1.0 - BETA_TWO ** STEPS)
    weight = weight - step_rate * (first_hat / (jnp.sqrt(second_hat) + ADAM_EPS) + DECAY * weight)
    return (weight, moment, square, weight.astype(jnp.bfloat16))

def reference(features, scale_ids, class_ids, code_targets, token_weights, attn_weight, attn_moment, attn_square, mlp_weight, mlp_moment, mlp_square, ada_weight, ada_moment, ada_square, embed_weight, embed_moment, embed_square, gains_weight, gains_moment, gains_square, head_weight, head_moment, head_square):
    masters = (attn_weight, mlp_weight, ada_weight, embed_weight, gains_weight, head_weight)
    moments = (attn_moment, mlp_moment, ada_moment, embed_moment, gains_moment, head_moment)
    squares = (attn_square, mlp_square, ada_square, embed_square, gains_square, head_square)
    token_count = jnp.sum((scale_ids < LEVELS).astype(jnp.float32))
    inputs = (features, scale_ids, class_ids, code_targets, token_weights)

    def objective(params):
        weights = tuple((low(param) for param in params))

        def advance(running, row_data):
            return (running + jax.checkpoint(row_loss)(weights, row_data), None)
        summed, _ = lax.scan(advance, jnp.zeros((), jnp.float32), inputs)
        return (summed / token_count, summed)
    _, pull_back, loss_sum = jax.vjp(objective, masters, has_aux=True)
    gradients = pull_back(jnp.ones((), jnp.float32))[0]
    total_sq = jnp.zeros((), jnp.float32)
    for gradient in gradients:
        total_sq = total_sq + jnp.sum(gradient * gradient)
    grad_norm = jnp.sqrt(total_sq)
    clip_factor = jnp.minimum(1.0, CLIP_NORM / (grad_norm + 1e-06))
    updates = [adam_step(masters[number], moments[number], squares[number], gradients[number], clip_factor, RATES[number]) for number in range(6)]
    return (updates[0][0], updates[0][1], updates[0][2], updates[0][3], updates[1][0], updates[1][1], updates[1][2], updates[1][3], updates[2][0], updates[2][1], updates[2][2], updates[2][3], updates[3][0], updates[3][1], updates[3][2], updates[3][3], updates[4][0], updates[4][1], updates[4][2], updates[4][3], updates[5][0], updates[5][1], updates[5][2], updates[5][3], grad_norm, loss_sum, token_count)
```

```python
import jax
import jax.numpy as jnp
from jax import lax
from jax.sharding import Mesh, PartitionSpec as P

HEADS = 16
HEAD_DIM = 64
FF = 4096
V = 4096
CHANNELS = 32
CLASSES = 1001
POSITIONS = 680
LEVELS = 10
MAXIMG = 8
STEPS = 10


EPS_NORM = 1e-06
BETA_ONE = 0.9
BETA_TWO = 0.95
ADAM_EPS = 1e-08
DECAY = 0.05
CLIP_NORM = 0.001
RATES = (0.03, 0.03, 0.03, 0.15, 0.4, 0.03)
NEG_FILL = -1e30
GROUP_HEADS = 4
BF16 = jnp.bfloat16
F32 = jnp.float32


def matmul(left, right):
    return jnp.dot(left, right, preferred_element_type=F32)


def matmul_tn(left, right):
    return lax.dot_general(left, right, (((0,), (0,)), ((), ())), preferred_element_type=F32)


def matmul_nt(left, right):
    return lax.dot_general(left, right, (((1,), (1,)), ((), ())), preferred_element_type=F32)


def precise(left, right):
    return jnp.dot(left, right, precision=lax.Precision.HIGHEST)


def precise_tn(left, right):
    return lax.dot_general(left, right, (((0,), (0,)), ((), ())), precision=lax.Precision.HIGHEST)


def by_halves(times, values):
    upper = lax.reduce_precision(values, 8, 7)
    return times(upper.astype(BF16)) + times((values - upper).astype(BF16))


def shifted(value, axis, size, shift):
    return lax.ppermute(value, axis, [(i, (i + shift) % size) for i in range(size)])


def gather_axis(value, axis, size):
    return [value] + [shifted(value, axis, size, k) for k in range(1, size)]


def gather(value, order, sizes):
    for axis in order[:-1]:
        value = jnp.concatenate(gather_axis(value, axis, sizes[axis]), axis=0)
    last = order[-1]
    blocks = gather_axis(value, last, sizes[last])
    return blocks + [shifted(block, "c", 2, 1) for block in blocks]


def add_shifts(pieces, axis, size, out):
    total = pieces[0].astype(F32)
    for k in range(1, size):
        total = total + shifted(pieces[k].astype(BF16), axis, size, size - k).astype(F32)
    return total.astype(out)


def scatter(blocks, order, sizes):
    count = len(blocks) // 2
    kept = [
        add_shifts([blocks[k], blocks[count + k]], "c", 2, BF16) for k in reversed(range(count))
    ][::-1]
    axes = list(reversed(order))
    value = add_shifts(kept, axes[0], sizes[axes[0]], BF16)
    for axis in axes[1:]:
        pieces = jnp.split(value, sizes[axis], axis=0)
        value = add_shifts(pieces, axis, sizes[axis], F32 if axis == axes[-1] else BF16)
    return value


def sum_all(value, sizes):
    for axis in ("c", "x", "y", "z"):
        value = sum(gather_axis(value, axis, sizes[axis]))
    return value


def source_rows(order, sizes, rows):
    places = sizes["z"] * sizes["y"] * sizes["x"] * 2 * rows
    place = jnp.arange(places, dtype=jnp.int32)
    row, rest = place % rows, place // rows
    at = {}
    for axis in tuple(order) + ("c",):
        at[axis] = (lax.axis_index(axis) - rest % sizes[axis]) % sizes[axis]
        rest = rest // sizes[axis]
    device = ((at["z"] * sizes["y"] + at["y"]) * sizes["x"] + at["x"]) * 2 + at["c"]
    return device * rows + row


def hot_rows(source):
    width = source.shape[0]
    return (source[:, None] == jnp.arange(width, dtype=jnp.int32)[None, :]).astype(BF16)


def normalize(values):
    center = values - jnp.mean(values, axis=-1, keepdims=True)
    return center * lax.rsqrt(jnp.mean(center * center, axis=-1, keepdims=True) + EPS_NORM)


def modulate(values, shifts, scales):
    return normalize(values) * (1.0 + scales) + shifts


def head_norm(values, gain_vec):
    return (
        values * lax.rsqrt(jnp.mean(values * values, axis=-1, keepdims=True) + EPS_NORM) * gain_vec
    )


def gelu_tanh(values):
    return jax.nn.gelu(values, approximate=True)


def layout(scale_row):
    position = jnp.arange(scale_row.shape[0], dtype=jnp.int32)
    opening = scale_row == 0
    image_id = jnp.cumsum(opening.astype(jnp.int32)) - 1
    starts_at = lax.cummax(jnp.where(opening, position, 0), axis=0)
    return (image_id, position - starts_at, scale_row < LEVELS)


def split_groups(values):
    length = values.shape[0]
    return jnp.moveaxis(values.reshape(length, HEADS // GROUP_HEADS, GROUP_HEADS, HEAD_DIM), 1, 0)


def join_groups(values):
    return jnp.moveaxis(values, 0, 1).reshape(values.shape[1], HEADS, HEAD_DIM)


def soft_block(q_group, k_group, allowed):
    scores = jnp.einsum(
        "qhd,khd->hqk", q_group, k_group, preferred_element_type=F32
    ) * HEAD_DIM ** (-0.5)
    scores = jnp.where(allowed[None], scores, NEG_FILL)
    exp_terms = jnp.exp(scores - jnp.max(scores, axis=-1, keepdims=True))
    return exp_terms / jnp.sum(exp_terms, axis=-1, keepdims=True)


def mix_heads(q_norm, k_norm, v_low, allowed):
    def mix_block(item):
        q_group, k_group, v_group = item
        soft_w = soft_block(q_group, k_group, allowed)
        return jnp.einsum(
            "hqk,khd->qhd", soft_w.astype(BF16), v_group, preferred_element_type=F32
        )

    mixed = lax.map(mix_block, (split_groups(q_norm), split_groups(k_norm), split_groups(v_low)))
    return join_groups(mixed)


def mix_heads_back(q_norm, k_norm, v_low, d_mix, allowed):
    def back_block(item):
        q_group, k_group, v_group, dm_group = item
        soft_w = soft_block(q_group, k_group, allowed)
        soft_low = soft_w.astype(BF16)
        d_values = jnp.einsum("hqk,qhd->khd", soft_low, dm_group, preferred_element_type=F32)
        d_soft = jnp.einsum("qhd,khd->hqk", dm_group, v_group, preferred_element_type=F32)
        d_scores = (soft_w * (d_soft - jnp.sum(d_soft * soft_w, axis=-1, keepdims=True))).astype(
            BF16
        )
        d_qn = jnp.einsum("hqk,khd->qhd", d_scores, k_group, preferred_element_type=F32)
        d_kn = jnp.einsum("hqk,qhd->khd", d_scores, q_group, preferred_element_type=F32)
        return (d_qn * HEAD_DIM ** (-0.5), d_kn * HEAD_DIM ** (-0.5), d_values)

    d_qn, d_kn, d_values = lax.map(
        back_block,
        (split_groups(q_norm), split_groups(k_norm), split_groups(v_low), split_groups(d_mix)),
    )
    return (join_groups(d_qn), join_groups(d_kn), join_groups(d_values))


def adam_step(weight, moment, square, gradient, clip_factor, step_rate):
    gradient = gradient * clip_factor
    moment = BETA_ONE * moment + (1.0 - BETA_ONE) * gradient
    square = BETA_TWO * square + (1.0 - BETA_TWO) * gradient * gradient
    first_hat = moment / (1.0 - BETA_ONE**STEPS)
    second_hat = square / (1.0 - BETA_TWO**STEPS)
    weight = weight - step_rate * (first_hat / (jnp.sqrt(second_hat) + ADAM_EPS) + DECAY * weight)
    return (weight, moment, square, weight.astype(BF16))


def per_device(
    sizes,
    features,
    scale_ids,
    class_ids,
    code_targets,
    token_weights,
    attn_weight,
    attn_moment,
    attn_square,
    mlp_weight,
    mlp_moment,
    mlp_square,
    ada_weight,
    ada_moment,
    ada_square,
    embed_weight,
    embed_moment,
    embed_square,
    gains_weight,
    gains_moment,
    gains_square,
    head_weight,
    head_moment,
    head_square,
):
    path_one, path_two = ("z", "y", "x"), ("z", "x", "y")
    devices = sizes["z"] * sizes["y"] * sizes["x"] * 2
    rows = attn_weight.shape[0]
    width = rows * devices
    ff_rows = FF // width
    ada_at = 7 + ff_rows
    head_at = ada_at + 8
    off_level = CLASSES + POSITIONS
    off_word = off_level + LEVELS
    length = scale_ids.shape[1]
    used = min(POSITIONS, length)
    n_gains = gains_weight.shape[0]

    scale_row = scale_ids[0]
    image_id, inside, counted = layout(scale_row)
    counted = counted.astype(F32)
    facts = jnp.concatenate(
        [class_ids[0], jnp.sum(counted).astype(jnp.int32)[None], jnp.zeros((119,), jnp.int32)]
    )[None]
    facts = jnp.concatenate(gather(facts, path_one, sizes), axis=0)
    total_count = jnp.sum(facts[:, MAXIMG]).astype(F32)
    weighted = token_weights[0] * counted
    row_info = jnp.stack([code_targets[0].astype(F32), weighted])
    row_info = gather_axis(row_info, "x", sizes["x"])
    row_info = row_info + [shifted(part, "c", 2, 1) for part in row_info]
    row_info = jnp.concatenate(row_info, axis=1)

    embed16 = embed_weight.astype(BF16)
    gains16 = gains_weight.astype(BF16)
    slim = jnp.concatenate(
        [
            embed16[CLASSES : CLASSES + used],
            embed16[off_level : off_word + CHANNELS],
            gains16,
        ],
        axis=0,
    )
    n_slim = slim.shape[0]
    fill = -n_slim % 128
    slim = jnp.pad(slim, ((0, fill), (0, 0))).T
    slim_all = jnp.concatenate(gather(slim, path_one, sizes), axis=0)
    perm_one = hot_rows(source_rows(path_one, sizes, rows))
    perm_two = hot_rows(source_rows(path_two, sizes, rows))
    slim_all = matmul_tn(slim_all, perm_one)
    n_embed = used + LEVELS + CHANNELS
    gain_rows = slim_all[n_embed : n_embed + n_gains]

    ids_one = facts[:, :MAXIMG]
    slots = devices * MAXIMG
    class_hot = (
        ids_one.reshape(slots)[:, None] == jnp.arange(CLASSES, dtype=jnp.int32)[None, :]
    ).astype(BF16)
    class_vec = matmul(class_hot, embed16[:CLASSES])
    class_act = jax.nn.silu(class_vec).astype(BF16)

    def to_two(value):
        shaped = value.reshape((2, sizes["x"], sizes["y"], sizes["z"] * MAXIMG) + value.shape[1:])
        return jnp.swapaxes(shaped, 1, 2).reshape(value.shape)

    def to_one(value):
        shaped = value.reshape((2, sizes["y"], sizes["x"], sizes["z"] * MAXIMG) + value.shape[1:])
        return jnp.swapaxes(shaped, 1, 2).reshape(value.shape)

    ada16 = ada_weight.astype(BF16)
    half = ada16.shape[1] // 2
    act_two = to_two(class_act)
    mod_one = matmul(class_act, ada16[:, :half]).astype(BF16)
    mod_two = matmul(act_two, ada16[:, half:]).astype(BF16)
    mod_one = scatter(jnp.split(mod_one, 2 * sizes["x"], axis=0), path_one, sizes)
    mod_two = scatter(jnp.split(mod_two, 2 * sizes["y"], axis=0), path_two, sizes)
    modulation = jnp.concatenate([mod_one, mod_two], axis=1) + gain_rows[ada_at:head_at].reshape(-1)

    attn16 = attn_weight.astype(BF16)
    attn_one = jnp.concatenate(gather(attn16[:, : 2 * width], path_one, sizes), axis=0)
    attn_two = jnp.concatenate(gather(attn16[:, 2 * width :], path_two, sizes), axis=0)
    w_v, w_proj = attn_two[:, :width], attn_two[:, width:]
    mlp16 = mlp_weight.astype(BF16)
    w_up = jnp.concatenate(gather(mlp16[0], path_one, sizes), axis=0)
    w_down = jnp.concatenate(gather(mlp16[1], path_two, sizes), axis=0)
    head16 = head_weight.astype(BF16)
    for axis in ("z", "y"):
        head16 = jnp.concatenate(gather_axis(head16, axis, sizes[axis]), axis=0)
    head_rows = head_weight.shape[0]
    place = jnp.arange(width, dtype=jnp.int32)
    rest = place // head_rows
    z_at = (lax.axis_index("z") - rest % sizes["z"]) % sizes["z"]
    y_at = (lax.axis_index("y") - rest // sizes["z"]) % sizes["y"]
    perm_head = hot_rows((z_at * sizes["y"] + y_at) * head_rows + place % head_rows)

    feat_row = features[0]
    pos_hot = (inside[:, None] == jnp.arange(used, dtype=jnp.int32)[None, :]).astype(BF16)
    level_hot = (scale_row[:, None] == jnp.arange(LEVELS, dtype=jnp.int32)[None, :]).astype(BF16)
    token_hot = jnp.concatenate([pos_hot, level_hot, feat_row], axis=1)
    resid_in = matmul(token_hot, slim_all[:n_embed].astype(BF16)) + gain_rows[0]
    image_hot = (image_id[:, None] == jnp.arange(MAXIMG, dtype=jnp.int32)[None, :]).astype(F32)
    pieces = jnp.split(precise(image_hot, modulation), 8, axis=1)
    allowed = (image_id[:, None] == image_id[None, :]) & (scale_row[None, :] <= scale_row[:, None])
    u_one = modulate(resid_in, pieces[0], pieces[1]).astype(BF16)
    u_rel_one = matmul_nt(u_one, perm_one).astype(BF16)
    u_rel_two = matmul_nt(u_one, perm_two).astype(BF16)
    qk = matmul(u_rel_one, attn_one)
    queries, keys = qk[:, :width] + gain_rows[1], qk[:, width:]
    values = matmul(u_rel_two, w_v) + gain_rows[2]
    split_shape = (length, HEADS, HEAD_DIM)
    queries = queries.reshape(split_shape)
    keys = keys.reshape(split_shape)
    q_gain = gain_rows[5].reshape(HEADS, HEAD_DIM)
    k_gain = gain_rows[6].reshape(HEADS, HEAD_DIM)
    q_norm = head_norm(queries, q_gain).astype(BF16)
    k_norm = head_norm(keys, k_gain).astype(BF16)
    v_low = values.reshape(split_shape).astype(BF16)
    mixture = mix_heads(q_norm, k_norm, v_low, allowed).reshape(length, width).astype(BF16)
    mixture_rel = matmul_nt(mixture, perm_two).astype(BF16)
    attn_out = matmul(mixture_rel, w_proj) + gain_rows[3]
    resid_mid = resid_in + pieces[2] * attn_out
    u_two = modulate(resid_mid, pieces[3], pieces[4]).astype(BF16)
    u_two_rel = matmul_nt(u_two, perm_one).astype(BF16)
    hidden = matmul(u_two_rel, w_up) + gain_rows[7:ada_at].reshape(-1)
    active = gelu_tanh(hidden).astype(BF16)
    mlp_out = by_halves(lambda part: matmul(part, perm_two), matmul_nt(active, w_down)) + gain_rows[4]
    resid_out = resid_mid + pieces[5] * mlp_out
    head_in = modulate(resid_out, pieces[6], pieces[7]).astype(BF16)

    head_rel = matmul_nt(head_in, perm_head).astype(BF16)
    n_x = sizes["x"]
    rows_all = gather_axis(head_rel, "x", n_x)
    rows_all = rows_all + [shifted(part, "c", 2, 1) for part in rows_all]
    rows_all = jnp.concatenate(rows_all, axis=0)
    member = lax.axis_index("x") * 2 + lax.axis_index("c")
    code_span = head_weight.shape[1]
    code_start = member * code_span
    head_bias = gain_rows[head_at:].reshape(-1)
    logits = matmul(rows_all, head16) + lax.dynamic_slice_in_dim(head_bias, code_start, code_span)
    local_max = jnp.max(logits, axis=1)
    exp_sums = jnp.sum(jnp.exp(logits - local_max[:, None]), axis=1)
    is_target = (
        jnp.arange(code_span, dtype=jnp.int32)[None, :] + code_start
        == row_info[0].astype(jnp.int32)[:, None]
    ).astype(F32)
    picked = jnp.sum(is_target * logits, axis=1)
    stats = jnp.stack([local_max, exp_sums, picked]).reshape(3, 2, n_x, length)
    group = [stats]
    for d_c in range(2):
        for d_x in range(n_x):
            if d_c or d_x:
                perm = [
                    (x * 2 + c, ((x + d_x) % n_x) * 2 + (c + d_c) % 2)
                    for x in range(n_x)
                    for c in range(2)
                ]
                group.append(jnp.roll(lax.ppermute(stats, ("x", "c"), perm), (d_c, d_x), (1, 2)))
    row_max = group[0][0]
    for other in group[1:]:
        row_max = jnp.maximum(row_max, other[0])
    totals = sum(other[1] * jnp.exp(other[0] - row_max) for other in group)
    target_logit = sum(other[2] for other in group).reshape(-1)
    log_total = (row_max + jnp.log(totals)).reshape(-1)
    loss_part = jnp.sum((row_info[1] * (log_total - target_logit))[:length])
    row_coef = row_info[1] / total_count
    d_logits = (row_coef[:, None] * (jnp.exp(logits - log_total[:, None]) - is_target)).astype(BF16)
    d_rows = matmul_nt(d_logits, head16).astype(BF16)
    d_rows = jnp.split(d_rows, 2 * n_x, axis=0)
    d_rows = [add_shifts([d_rows[k], d_rows[n_x + k]], "c", 2, BF16) for k in range(n_x)]
    d_head_in = add_shifts(d_rows, "x", n_x, F32)
    d_head_in = by_halves(lambda part: matmul(part, perm_head), d_head_in)
    head_grad = matmul_tn(rows_all, d_logits).astype(BF16)
    head_grad = add_shifts(jnp.split(head_grad, sizes["y"], axis=0), "y", sizes["y"], BF16)
    head_grad = add_shifts(jnp.split(head_grad, sizes["z"], axis=0), "z", sizes["z"], F32)
    bias_grad = lax.dynamic_update_slice(
        jnp.zeros((V,), F32), jnp.sum(d_logits.astype(F32), axis=0), (code_start,)
    )
    _, head_back = jax.vjp(modulate, resid_out, pieces[6], pieces[7])
    d_resid_out, d_shift_head, d_scale_head = head_back(d_head_in)

    d_low = (pieces[5] * d_resid_out).astype(BF16)
    d_low_rel = matmul_nt(d_low, perm_two).astype(BF16)
    d_down = matmul_tn(d_low_rel, active).astype(BF16)
    down_grad = scatter(jnp.split(d_down, 2 * sizes["y"], axis=0), path_two, sizes)
    d_bias_down = jnp.sum(d_low.astype(F32), axis=0)
    d_active = matmul(d_low_rel, w_down)
    _, gelu_back = jax.vjp(gelu_tanh, hidden)
    d_hidden = gelu_back(d_active)[0].astype(BF16)
    d_up = matmul_tn(u_two_rel, d_hidden).astype(BF16)
    up_grad = scatter(jnp.split(d_up, 2 * sizes["x"], axis=0), path_one, sizes)
    d_bias_up = jnp.sum(d_hidden.astype(F32), axis=0)
    d_u = matmul(matmul_nt(d_hidden, w_up).astype(BF16), perm_one)
    _, mod_back = jax.vjp(modulate, resid_mid, pieces[3], pieces[4])
    d_branch, d_shift_two, d_scale_two = mod_back(d_u)
    d_gate_two = d_resid_out * mlp_out
    d_resid_mid = d_resid_out + d_branch

    d_low = (pieces[2] * d_resid_mid).astype(BF16)
    d_proj = matmul_tn(mixture_rel, d_low).astype(BF16)
    proj_grad = scatter(jnp.split(d_proj, 2 * sizes["y"], axis=0), path_two, sizes)
    d_bias_out = jnp.sum(d_low.astype(F32), axis=0)
    d_mix = matmul(matmul_nt(d_low, w_proj).astype(BF16), perm_two).astype(BF16)
    d_qn, d_kn, d_values = mix_heads_back(
        q_norm, k_norm, v_low, d_mix.reshape(split_shape), allowed
    )
    _, q_back = jax.vjp(head_norm, queries, q_gain)
    d_queries, d_qgain = q_back(d_qn)
    _, k_back = jax.vjp(head_norm, keys, k_gain)
    d_keys, d_kgain = k_back(d_kn)
    d_q = d_queries.reshape(length, width).astype(BF16)
    d_k = d_keys.reshape(length, width).astype(BF16)
    d_v = d_values.reshape(length, width).astype(BF16)
    d_qk = jnp.concatenate([d_q, d_k], axis=1)
    d_attn_one = matmul_tn(u_rel_one, d_qk).astype(BF16)
    one_grad = scatter(jnp.split(d_attn_one, 2 * sizes["x"], axis=0), path_one, sizes)
    d_attn_two = matmul_tn(u_rel_two, d_v).astype(BF16)
    v_grad = scatter(jnp.split(d_attn_two, 2 * sizes["y"], axis=0), path_two, sizes)
    d_u = matmul(matmul_nt(d_qk, attn_one).astype(BF16), perm_one)
    d_u = d_u + matmul(matmul_nt(d_v, w_v).astype(BF16), perm_two)
    _, mod_back = jax.vjp(modulate, resid_in, pieces[0], pieces[1])
    d_branch, d_shift_one, d_scale_one = mod_back(d_u)
    d_gate_one = d_resid_mid * attn_out
    d_resid_in = d_resid_mid + d_branch

    d_token = jnp.concatenate(
        [
            d_shift_one,
            d_scale_one,
            d_gate_one,
            d_shift_two,
            d_scale_two,
            d_gate_two,
            d_shift_head,
            d_scale_head,
        ],
        axis=1,
    )
    d_mod = precise_tn(image_hot, d_token).astype(BF16)
    d_ada_bias = jnp.sum(d_mod.astype(F32), axis=0)
    d_mod_one = jnp.concatenate(gather(d_mod[:, :half], path_one, sizes), axis=0)
    d_mod_two = jnp.concatenate(gather(d_mod[:, half:], path_two, sizes), axis=0)
    ada_grad = jnp.concatenate(
        [matmul_tn(class_act, d_mod_one), matmul_tn(act_two, d_mod_two)], axis=1
    )
    d_class_act = matmul_nt(d_mod_one, ada16[:, :half]) + to_one(
        matmul_nt(d_mod_two, ada16[:, half:])
    )
    _, silu_back = jax.vjp(jax.nn.silu, class_vec)
    d_class = precise_tn(class_hot.astype(F32), silu_back(d_class_act)[0])

    d_res16 = d_resid_in.astype(BF16)
    d_gains = jnp.concatenate(
        [
            jnp.sum(d_resid_in, axis=0)[None],
            jnp.sum(d_q.astype(F32), axis=0)[None],
            jnp.sum(d_v.astype(F32), axis=0)[None],
            d_bias_out[None],
            d_bias_down[None],
            d_qgain.reshape(1, width),
            d_kgain.reshape(1, width),
            d_bias_up.reshape(ff_rows, width),
            d_ada_bias.reshape(8, width),
            bias_grad.reshape(-1, width),
        ],
        axis=0,
    ).astype(BF16)
    d_slim = jnp.concatenate(
        [
            matmul_tn(token_hot, d_res16).astype(BF16),
            d_gains,
            jnp.zeros((fill, width), BF16),
        ],
        axis=0,
    )
    d_slim = matmul_nt(perm_one, d_slim).astype(BF16)
    slim_grad = scatter(jnp.split(d_slim, 2 * sizes["x"], axis=0), path_one, sizes).T
    embed_grad = jnp.concatenate(
        [
            d_class,
            slim_grad[:used],
            jnp.zeros((POSITIONS - used, rows), F32),
            slim_grad[used:n_embed],
        ],
        axis=0,
    )
    gains_grad = slim_grad[n_embed : n_embed + n_gains]

    attn_grad = jnp.concatenate([one_grad, v_grad, proj_grad], axis=1)
    mlp_grad = jnp.stack([up_grad, down_grad])
    gradients = (attn_grad, mlp_grad, ada_grad, embed_grad, gains_grad, head_grad)
    squares_local = jnp.zeros((), F32)
    for gradient in gradients:
        squares_local = squares_local + jnp.sum(gradient * gradient)
    sums = sum_all(jnp.stack([squares_local, loss_part])[None], sizes)
    total_sq, loss_sum = sums[0, 0], sums[0, 1]
    grad_norm = jnp.sqrt(total_sq)
    clip_factor = jnp.minimum(1.0, CLIP_NORM / (grad_norm + 1e-06))
    masters = (attn_weight, mlp_weight, ada_weight, embed_weight, gains_weight, head_weight)
    moments = (attn_moment, mlp_moment, ada_moment, embed_moment, gains_moment, head_moment)
    squares = (attn_square, mlp_square, ada_square, embed_square, gains_square, head_square)
    updates = []
    for number in range(6):
        updates.extend(
            adam_step(
                masters[number],
                moments[number],
                squares[number],
                gradients[number],
                clip_factor,
                RATES[number],
            )
        )
    return tuple(updates) + (grad_norm, loss_sum, total_count)


def solution(mesh):
    n_dp, n_vocab = mesh.shape["dp"], mesh.shape["vocab"]
    n_z = 1 << (n_dp.bit_length() // 2)
    sizes = {"z": n_z, "y": n_dp // n_z, "x": n_vocab // 2, "c": 2}
    fine = Mesh(
        mesh.devices.reshape(sizes["z"], sizes["y"], sizes["x"], 2), ("z", "y", "x", "c")
    )
    every, dp, vocab = ("z", "y", "x", "c"), ("z", "y"), ("x", "c")
    by_row = P(every, None)
    by_mid = P(None, every, None)
    by_column = P(None, every)
    head = P(dp, vocab)
    placed = (P(every, None, None), by_row, by_row, by_row, by_row)
    for spec in (by_row, by_mid, by_row, by_column, by_column, head):
        placed = placed + (spec,) * 3
    given = ()
    for spec in (by_row, by_mid, by_row, by_column, by_column, head):
        given = given + (spec,) * 4

    def step(*arrays):
        return per_device(sizes, *arrays)

    return jax.shard_map(
        step, mesh=fine, in_specs=placed, out_specs=given + (P(), P(), P()), check_vma=False
    )
```

```python
import jax
import jax.numpy as jnp
from jax import lax
from jax.experimental import pallas as pl
from jax.experimental.pallas import tpu as pltpu
from jax.sharding import PartitionSpec as P

HEADS = 16
HEAD_DIM = 64
FF = 4096
V = 4096
CHANNELS = 32
CLASSES = 1001
POSITIONS = 680
LEVELS = 10
MAXIMG = 8
STEPS = 10


EPS_NORM = 1e-06
BETA_ONE = 0.9
BETA_TWO = 0.95
ADAM_EPS = 1e-08
DECAY = 0.05
CLIP_NORM = 0.001
RATES = (0.03, 0.03, 0.03, 0.15, 0.4, 0.03)
NEG_FILL = -1e30
BF16 = jnp.bfloat16
F32 = jnp.float32
SPAN = 512
TOKENS = 128
PAIR = 2 * HEAD_DIM


def matmul(left, right):
    return jnp.dot(left, right, preferred_element_type=F32)


def matmul_tn(left, right):
    return lax.dot_general(left, right, (((0,), (0,)), ((), ())), preferred_element_type=F32)


def matmul_nt(left, right):
    return lax.dot_general(left, right, (((1,), (1,)), ((), ())), preferred_element_type=F32)


def precise(left, right):
    return jnp.dot(left, right, precision=lax.Precision.HIGHEST, preferred_element_type=F32)


def precise_tn(left, right):
    return lax.dot_general(left, right, (((0,), (0,)), ((), ())), precision=lax.Precision.HIGHEST)


def in_halves(times, values):
    upper = values.astype(BF16)
    return times(upper) + times((values - upper.astype(F32)).astype(BF16))


def in_halves_outside(times, values):
    upper = lax.reduce_precision(values, 8, 7)
    return times(upper.astype(BF16)) + times((values - upper).astype(BF16))


def swapped(value, mask, devices):
    return lax.ppermute(value, ("dp", "vocab"), [(i, i ^ mask) for i in range(devices)])


def tie(*values):
    return lax.optimization_barrier(values)


def grow(value, mask, devices):
    return jnp.concatenate([value, swapped(value, mask, devices)], axis=0)


def added(mine, theirs, out=BF16):
    return (mine.astype(F32) + theirs.astype(F32)).astype(out)


def keep_half(value, mask, devices, out=BF16):
    half = value.shape[0] // 2
    return added(value[:half], swapped(value[half:].astype(BF16), mask, devices), out)


def keep_all(value, masks, devices):
    for mask in reversed(masks):
        value = keep_half(value, mask, devices, F32 if mask == masks[0] else BF16)
    return value


def halves_of(mine, back, out=BF16):
    half = mine.shape[0] // 2
    return (added(mine[:half], back[:half], out), added(mine[half:], back[half:], out))


def sum_all(value, bits, devices):
    for at in range(0, len(bits), 2):
        masks = bits[at : at + 2]
        if len(masks) == 2:
            masks = masks + [masks[0] ^ masks[1]]
        value = value + sum(swapped(value, mask, devices) for mask in masks)
    return value


def place_masks(masks):
    places = [0]
    for mask in masks:
        places = places + [place ^ mask for place in places]
    return places


def source_rows(masks, me, rows):
    differ = jnp.repeat(jnp.array(place_masks(masks), jnp.int32), rows)
    row = jnp.tile(jnp.arange(rows, dtype=jnp.int32), 1 << len(masks))
    return (differ ^ me) * rows + row


def hot_rows(source):
    place = jnp.arange(source.shape[0], dtype=jnp.int32)
    return (
        (source[:, None] == place[None, :]).astype(BF16),
        (place[:, None] == source[None, :]).astype(BF16),
    )


def run(body, grid, given, specs, outs, out_specs, scratch=(), work=0):
    moved = sum(value.size * value.dtype.itemsize for value in given)
    return pl.pallas_call(
        body,
        grid=grid,
        in_specs=specs,
        out_shape=outs,
        out_specs=out_specs,
        scratch_shapes=scratch,
        compiler_params=pltpu.CompilerParams(vmem_limit_bytes=48 << 20),
        cost_estimate=pl.CostEstimate(flops=work, bytes_accessed=moved, transcendentals=0),
    )(*given)


def whole(value):
    return pl.BlockSpec(value.shape, lambda j: (0,) * value.ndim)


def two_sets(sets):
    first = sets[0][0].shape[1] // SPAN
    specs = [
        pl.BlockSpec((block.shape[0], SPAN), lambda j: (0, jnp.minimum(j, first - 1)))
        for block in sets[0]
    ]
    specs += [
        pl.BlockSpec((block.shape[0], SPAN), lambda j: (0, jnp.maximum(j - first, 0)))
        for block in sets[1]
    ]
    return first, specs


def gelu_parts(value):
    inner = 0.7978845608028654 * (value + 0.044715 * (value * value * value))
    bend = jnp.tanh(inner)
    return bend


def gelu(value):
    return 0.5 * value * (1.0 + gelu_parts(value))


def gelu_slope(value):
    bend = gelu_parts(value)
    rise = 0.7978845608028654 * (1.0 + 3.0 * 0.044715 * value * value)
    return 0.5 * (1.0 + bend) + 0.5 * value * (1.0 - bend * bend) * rise


def times_sets(left, sets, bias=None, hidden=None, bend=False):
    tokens = left[0].shape[0]
    first, specs = two_sets(sets)
    steps = first + sets[1][0].shape[1] // SPAN
    count = len(sets[0])
    extra = [value for value in (bias, hidden) if value is not None]
    column = lambda j: (0, j)
    extra_specs = [pl.BlockSpec((value.shape[0], SPAN), column) for value in extra]

    def body(one_ref, two_ref, *refs):
        extras, blocks = refs[: len(extra)], refs[len(extra) : len(extra) + 2 * count]
        outs = refs[len(extra) + 2 * count :]

        def part(u_ref, blocks):
            total, at = None, 0
            for block in blocks:
                rows = block.shape[0]
                term = matmul(u_ref[:, at : at + rows], block[...])
                total = term if total is None else total + term
                at += rows
            if bias is not None:
                total = total + extras[0][...]
            if hidden is not None:
                slope = gelu_slope(extras[-1][...])
                low = (total * slope).astype(BF16)
                outs[0][...] = low
                outs[1][...] = jnp.sum(low.astype(F32), axis=0, keepdims=True)
            else:
                outs[0][...] = total
                if bend:
                    outs[1][...] = gelu(total).astype(BF16)

        pl.when(pl.program_id(0) < first)(lambda: part(one_ref, blocks[:count]))
        pl.when(pl.program_id(0) >= first)(lambda: part(two_ref, blocks[count:]))

    wide = steps * SPAN
    shape = jax.ShapeDtypeStruct
    outs, out_specs = [shape((tokens, wide), F32)], [pl.BlockSpec((tokens, SPAN), column)]
    if hidden is not None:
        outs = [shape((tokens, wide), BF16), shape((1, wide), F32)]
        out_specs.append(pl.BlockSpec((1, SPAN), column))
    elif bend:
        outs.append(shape((tokens, wide), BF16))
        out_specs.append(pl.BlockSpec((tokens, SPAN), column))
    given = list(left) + extra + list(sets[0]) + list(sets[1])
    specs = [whole(value) for value in left] + extra_specs + specs
    work = 2 * tokens * left[0].shape[1] * wide
    found = run(body, (steps,), given, specs, outs, out_specs, work=work)
    return found if len(outs) > 1 else found[0]


def span_spec(value):
    each = value.shape[2] // SPAN
    return pl.BlockSpec((1, value.shape[1], SPAN), lambda j: (j // each, 0, j % each))


def back_sets(right, sets, perms, bias=None, exact=False, out=F32):
    tokens = right.shape[1]
    first, specs = two_sets(sets)
    steps = first + sets[1][0].shape[1] // SPAN
    count = len(sets[0])
    width = perms[0].shape[0]
    extra = [] if bias is None else [bias]

    def body(right_ref, one_ref, two_ref, *refs):
        extras, blocks = refs[: len(extra)], refs[len(extra) : len(extra) + 2 * count]
        out_ref, one_sum, two_sum = refs[len(extra) + 2 * count :]
        step = pl.program_id(0)

        def part(sums, blocks, start):
            terms = [matmul_nt(right_ref[0], block[...]) for block in blocks]
            term = jnp.concatenate(terms, axis=1)

            @pl.when(step == start)
            def _():
                sums[...] = term

            @pl.when(step > start)
            def _():
                sums[...] += term

        pl.when(step < first)(lambda: part(one_sum, blocks[:count], 0))
        pl.when(step >= first)(lambda: part(two_sum, blocks[count:], first))

        @pl.when(step == steps - 1)
        def _():
            total = None
            for sums, perm in ((one_sum, one_ref), (two_sum, two_ref)):
                if exact:
                    term = in_halves(lambda part: matmul(part, perm[...]), sums[...])
                else:
                    term = matmul(sums[...].astype(BF16), perm[...])
                total = term if total is None else total + term
            if bias is not None:
                total = total + extras[0][...]
            out_ref[...] = total.astype(out)

    given = [right] + list(perms) + extra + list(sets[0]) + list(sets[1])
    specs = [span_spec(right)] + [whole(value) for value in list(perms) + extra] + specs
    outs = jax.ShapeDtypeStruct((tokens, width), out)
    scratch = [pltpu.VMEM((tokens, width), F32)] * 2
    work = 2 * tokens * width * steps * SPAN
    return run(body, (steps,), given, specs, outs, whole(outs), scratch, work)


def grad_rows(left, right, rows, columns, back=None):
    tokens = left.shape[0]
    count = rows[1] - rows[0]
    each = right.shape[2] // SPAN
    start, steps = columns[0] // SPAN, (columns[1] - columns[0]) // SPAN

    def body(left_ref, right_ref, *refs):
        total = matmul_tn(left_ref[...], right_ref[0])
        if back is not None:
            total = total + refs[0][...].astype(F32)
        refs[-1][...] = total.astype(BF16)

    given = [left, right]
    at = rows[0] // count
    specs = [
        pl.BlockSpec((tokens, count), lambda j: (0, at)),
        pl.BlockSpec(
            (1, tokens, SPAN), lambda j: ((j + start) // each, 0, (j + start) % each)
        ),
    ]
    if back is not None:
        given.append(back)
        specs.append(pl.BlockSpec((count, SPAN), lambda j: (at, j)))
    outs = jax.ShapeDtypeStruct((count, steps * SPAN), BF16)
    spec = pl.BlockSpec((count, SPAN), lambda j: (0, j))
    work = 2 * tokens * count * steps * SPAN
    return run(body, (steps,), given, specs, outs, spec, work=work)


def head_scale(value, left_half):
    square = value * value
    one = jnp.sum(jnp.where(left_half, square, 0.0), axis=1, keepdims=True)
    two = jnp.sum(jnp.where(left_half, 0.0, square), axis=1, keepdims=True)
    return jnp.where(
        left_half,
        lax.rsqrt(one * (1.0 / HEAD_DIM) + EPS_NORM),
        lax.rsqrt(two * (1.0 / HEAD_DIM) + EPS_NORM),
    )


def soft_rows(q_norm, k_norm, mask):
    scores = matmul_nt(q_norm, k_norm) * HEAD_DIM ** (-0.5) + mask
    terms = jnp.exp(scores - jnp.max(scores, axis=1, keepdims=True))
    return terms * (1.0 / jnp.sum(terms, axis=1, keepdims=True))


def pair_specs(tokens):
    pairs = HEADS // 2
    return [
        pl.BlockSpec((tokens, PAIR), lambda j: (0, j)),
        pl.BlockSpec((tokens, PAIR), lambda j: (0, pairs + j)),
        pl.BlockSpec((tokens, PAIR), lambda j: (0, 2 * pairs + j)),
        pl.BlockSpec((1, PAIR), lambda j: (0, j)),
        pl.BlockSpec((1, PAIR), lambda j: (0, j)),
        pl.BlockSpec((tokens, tokens), lambda j: (0, 0)),
    ]


def attend(qkv, q_gain, k_gain, mask):
    tokens, width = qkv.shape[0], qkv.shape[1] // 3

    def body(q_ref, k_ref, v_ref, qg_ref, kg_ref, mask_ref, out_ref):
        left_half = lax.broadcasted_iota(jnp.int32, (1, PAIR), 1) < HEAD_DIM
        query, key = q_ref[...], k_ref[...]
        q_norm = (query * head_scale(query, left_half) * qg_ref[...]).astype(BF16)
        k_norm = (key * head_scale(key, left_half) * kg_ref[...]).astype(BF16)
        v_low = v_ref[...].astype(BF16)
        zero = jnp.zeros_like(q_norm)
        mixed = []
        for one in (jnp.where(left_half, q_norm, zero), jnp.where(left_half, zero, q_norm)):
            probs = soft_rows(one, k_norm, mask_ref[...])
            mixed.append(matmul(probs.astype(BF16), v_low))
        out_ref[...] = jnp.where(left_half, mixed[0], mixed[1]).astype(BF16)

    outs = jax.ShapeDtypeStruct((tokens, width), BF16)
    spec = pl.BlockSpec((tokens, PAIR), lambda j: (0, j))
    given = [qkv, qkv, qkv, q_gain, k_gain, mask]
    return run(body, (HEADS // 2,), given, pair_specs(tokens), outs, spec, work=10**10)


def attend_back(qkv, q_gain, k_gain, mask, d_mix):
    tokens, width = qkv.shape[0], qkv.shape[1] // 3

    def body(q_ref, k_ref, v_ref, qg_ref, kg_ref, mask_ref, dm_ref, out_ref, sums_ref):
        left_half = lax.broadcasted_iota(jnp.int32, (1, PAIR), 1) < HEAD_DIM
        query, key = q_ref[...], k_ref[...]
        q_scale, k_scale = head_scale(query, left_half), head_scale(key, left_half)
        q_norm = (query * q_scale * qg_ref[...]).astype(BF16)
        k_norm = (key * k_scale * kg_ref[...]).astype(BF16)
        v_low, d_mix = v_ref[...].astype(BF16), dm_ref[...]
        zero = jnp.zeros_like(q_norm)
        found = []
        for side in range(2):
            own = (lambda v: jnp.where(left_half, v, zero)) if side == 0 else (
                lambda v: jnp.where(left_half, zero, v)
            )
            probs = soft_rows(own(q_norm), k_norm, mask_ref[...])
            d_values = matmul_tn(probs.astype(BF16), d_mix)
            d_probs = matmul_nt(own(d_mix), v_low)
            inner = jnp.sum(d_probs * probs, axis=1, keepdims=True)
            d_scores = (probs * (d_probs - inner)).astype(BF16)
            found.append((matmul(d_scores, k_norm), matmul_tn(d_scores, q_norm), d_values))
        d_qn, d_kn, d_values = (jnp.where(left_half, one, two) for one, two in zip(*found))
        sums = []
        for at, value, scale, gain, d_norm in (
            (0, query, q_scale, qg_ref[...], d_qn * HEAD_DIM ** (-0.5)),
            (1, key, k_scale, kg_ref[...], d_kn * HEAD_DIM ** (-0.5)),
        ):
            product = d_norm * value
            sums.append(jnp.sum(product * scale, axis=0, keepdims=True))
            product = product * gain
            one = jnp.sum(jnp.where(left_half, product, 0.0), axis=1, keepdims=True)
            two = jnp.sum(jnp.where(left_half, 0.0, product), axis=1, keepdims=True)
            mean = jnp.where(left_half, one, two) * (1.0 / HEAD_DIM)
            d_value = scale * (gain * d_norm - value * (scale * scale) * mean)
            out_ref[at] = d_value.astype(BF16)
        out_ref[2] = d_values.astype(BF16)
        sums.append(jnp.sum(out_ref[0].astype(F32), axis=0, keepdims=True))
        sums.append(jnp.sum(out_ref[2].astype(F32), axis=0, keepdims=True))
        sums_ref[...] = jnp.concatenate(sums + [jnp.zeros((4, PAIR), F32)], axis=0)

    outs = [
        jax.ShapeDtypeStruct((3, tokens, width), BF16),
        jax.ShapeDtypeStruct((8, width), F32),
    ]
    out_specs = [
        pl.BlockSpec((3, tokens, PAIR), lambda j: (0, 0, j)),
        pl.BlockSpec((8, PAIR), lambda j: (0, j)),
    ]
    given = [qkv, qkv, qkv, q_gain, k_gain, mask, d_mix]
    specs = pair_specs(tokens) + [pl.BlockSpec((tokens, PAIR), lambda j: (0, j))]
    return run(body, (HEADS // 2,), given, specs, outs, out_specs, work=3 * 10**10)


def row_stats(value):
    center = value - jnp.mean(value, axis=1, keepdims=True)
    return center, lax.rsqrt(jnp.mean(center * center, axis=1, keepdims=True) + EPS_NORM)


def by_tokens(value):
    return pl.BlockSpec((TOKENS, value.shape[1]), lambda j: (j, 0))


def norm_ahead(value, hot, shift, scale, perms, gate=None, branch=None):
    tokens, width = value.shape
    extra = [] if gate is None else [gate, branch]

    def body(value_ref, hot_ref, shift_ref, scale_ref, *refs):
        total = value_ref[...]
        outs = refs[len(extra) + len(perms) :]
        if gate is not None:
            total = total + precise(hot_ref[...], refs[0][...]) * refs[1][...]
            outs[-1][...] = total
        center, inverse = row_stats(total)
        scales = 1.0 + precise(hot_ref[...], scale_ref[...])
        normed = center * inverse * scales + precise(hot_ref[...], shift_ref[...])
        normed = normed.astype(BF16)
        for perm_ref, out_ref in zip(refs[len(extra) : len(extra) + len(perms)], outs):
            out_ref[...] = matmul(normed, perm_ref[...]).astype(BF16)

    given = [value, hot, shift, scale] + extra + list(perms)
    specs = [by_tokens(value), by_tokens(hot), whole(shift), whole(scale)]
    specs += [whole(gate), by_tokens(branch)] if extra else []
    specs += [whole(perm) for perm in perms]
    outs = [jax.ShapeDtypeStruct((tokens, width), BF16) for _ in perms]
    outs += [jax.ShapeDtypeStruct((tokens, width), F32)] if extra else []
    out_specs = [by_tokens(value) for _ in outs]
    return run(body, (tokens // TOKENS,), given, specs, outs, out_specs, work=10**9)


def norm_back(value, d_out, hot, hot_t, scale, beyond=None, gate=None, branch=None, perms=()):
    tokens, width = value.shape
    gated = gate is not None
    tall = [value, d_out] + ([] if beyond is None else [beyond]) + ([branch] if gated else [])
    flat = [scale] + ([gate] if gated else []) + list(perms)

    def body(hot_ref, hot_t_ref, *refs):
        talls, flats = refs[: len(tall)], refs[len(tall) : len(tall) + len(flat)]
        outs = refs[len(tall) + len(flat) :]
        total_ref, shift_ref, scale_ref, column_ref = outs[:4]
        d_out = talls[1][...]
        center, inverse = row_stats(talls[0][...])
        normed = center * inverse
        d_norm = d_out * (1.0 + precise(hot_ref[...], flats[0][...]))
        mean = jnp.mean(d_norm, axis=1, keepdims=True)
        along = jnp.mean(d_norm * normed, axis=1, keepdims=True)
        total = (d_norm - mean - normed * along) * inverse
        if beyond is not None:
            total = total + talls[2][...]
        total_ref[...] = total
        sums = [
            (shift_ref, precise(hot_t_ref[...], d_out)),
            (scale_ref, precise(hot_t_ref[...], d_out * normed)),
        ]
        if gated:
            sums.append((outs[4], precise(hot_t_ref[...], total * talls[-1][...])))
            low = (precise(hot_ref[...], flats[1][...]) * total).astype(BF16)
            column = jnp.sum(low.astype(F32), axis=0, keepdims=True)
        else:
            low = total.astype(BF16)
            column = jnp.sum(total, axis=0, keepdims=True)
        sums.append((column_ref, column))
        lows = outs[5:] if gated else outs[4:]
        if perms:
            for perm_ref, low_ref in zip(flats[2:], lows):
                low_ref[...] = matmul(low, perm_ref[...]).astype(BF16)
        else:
            lows[0][...] = low

        @pl.when(pl.program_id(0) == 0)
        def _():
            for ref, term in sums:
                ref[...] = term

        @pl.when(pl.program_id(0) > 0)
        def _():
            for ref, term in sums:
                ref[...] += term

    given = [hot, hot_t] + tall + flat
    specs = [by_tokens(hot), pl.BlockSpec((hot_t.shape[0], TOKENS), lambda j: (0, j))]
    specs += [by_tokens(part) for part in tall] + [whole(part) for part in flat]
    shape = jax.ShapeDtypeStruct
    image = shape(scale.shape, F32)
    outs = [shape((tokens, width), F32), image, image, shape((1, width), F32)]
    outs += [image] if gated else []
    outs += [shape((tokens, width), BF16) for _ in range(max(len(perms), 1))]
    out_specs = [by_tokens(part) if part.shape[0] == tokens else whole(part) for part in outs]
    return run(body, (tokens // TOKENS,), given, specs, outs, out_specs, work=10**9)


def slim_back(d_resid, token_hot, arrays, plan, perm, n_embed):
    width, wide = perm.shape[0], token_hot.shape[1]
    rows = sum(arrays[which].shape[1] // width for which, _ in plan)
    room = rows + (-rows % 16)

    def body(d_ref, hot_ref, perm_ref, *refs):
        out_ref, gains = refs[-2], refs[-1]
        gains[...] = jnp.zeros_like(gains)
        at = 0
        for which, row in plan:
            for column in range(0, arrays[which].shape[1], width):
                gains[at : at + 1, :] = refs[which][row : row + 1, column : column + width]
                at += 1
        place = lax.broadcasted_iota(jnp.int32, (room, wide), 1)
        own = lax.broadcasted_iota(jnp.int32, (room, wide), 0) + n_embed
        own = jnp.where(own < n_embed + rows, own, -1)
        total = matmul_tn(d_ref[...], hot_ref[...])
        chosen = jnp.where(place == own, 1.0, 0.0).astype(BF16)
        total = total + matmul_tn(gains[...].astype(BF16), chosen)
        out_ref[...] = matmul(perm_ref[...], total.astype(BF16)).astype(BF16)

    given = [d_resid, token_hot, perm] + list(arrays)
    outs = jax.ShapeDtypeStruct((width, wide), BF16)
    specs = [whole(value) for value in given]
    scratch = [pltpu.VMEM((room, width), F32)]
    return run(body, (1,), given, specs, outs, whole(outs), scratch, 3 * 10**9)


def layout(scale_row):
    position = jnp.arange(scale_row.shape[0], dtype=jnp.int32)
    opening = scale_row == 0
    image_id = jnp.cumsum(opening.astype(jnp.int32)) - 1
    starts_at = lax.cummax(jnp.where(opening, position, 0), axis=0)
    return (image_id, position - starts_at, scale_row < LEVELS)


def adam_step(weight, moment, square, gradient, clip_factor, step_rate):
    gradient = gradient * clip_factor
    moment = BETA_ONE * moment + (1.0 - BETA_ONE) * gradient
    square = BETA_TWO * square + (1.0 - BETA_TWO) * gradient * gradient
    first_hat = moment / (1.0 - BETA_ONE**STEPS)
    second_hat = square / (1.0 - BETA_TWO**STEPS)
    weight = weight - step_rate * (first_hat / (jnp.sqrt(second_hat) + ADAM_EPS) + DECAY * weight)
    return (weight, moment, square, weight.astype(BF16))


def per_device(
    ways,
    features,
    scale_ids,
    class_ids,
    code_targets,
    token_weights,
    attn_weight,
    attn_moment,
    attn_square,
    mlp_weight,
    mlp_moment,
    mlp_square,
    ada_weight,
    ada_moment,
    ada_square,
    embed_weight,
    embed_moment,
    embed_square,
    gains_weight,
    gains_moment,
    gains_square,
    head_weight,
    head_moment,
    head_square,
):
    devices, n_vocab = ways["devices"], ways["n_vocab"]
    bits_y, bits_x, bits_z = ways["y"], ways["x"], ways["z"]
    path_one = bits_z + bits_y + bits_x
    path_two = bits_z + bits_x + bits_y
    me = lax.axis_index("dp") * n_vocab + lax.axis_index("vocab")
    rows = attn_weight.shape[0]
    width = rows * devices
    top, quarter = width // 2, width // 4
    ff_rows = FF // width
    ada_at = 7 + ff_rows
    head_at = ada_at + 8
    off_level = CLASSES + POSITIONS
    off_word = off_level + LEVELS
    length = scale_ids.shape[1]
    used = min(POSITIONS, length)
    n_gains = gains_weight.shape[0]
    n_embed = used + LEVELS + CHANNELS
    half_ff, half_qkv = FF // 2, 3 * width // 2

    def swap(value, mask):
        return swapped(value, mask, devices)

    def grown(masks, *values):
        for mask in masks:
            values = [grow(value, mask, devices) for value in values]
        return values if len(values) > 1 else values[0]

    scale_row = scale_ids[0]
    image_id, inside, counted = layout(scale_row)
    counted = counted.astype(F32)
    facts = jnp.concatenate(
        [class_ids[0], jnp.sum(counted).astype(jnp.int32)[None], jnp.zeros((119,), jnp.int32)]
    )[None]
    weighted = token_weights[0] * counted
    row_info = jnp.stack([code_targets[0].astype(F32), weighted])[None]

    embed16 = embed_weight.astype(BF16)
    slim = jnp.concatenate(
        [
            embed16[CLASSES : CLASSES + used],
            embed16[off_level : off_word + CHANNELS],
            gains_weight.astype(BF16),
        ],
        axis=0,
    )
    fill = -slim.shape[0] % 128
    slim = jnp.pad(slim, ((0, fill), (0, 0))).T
    wide = slim.shape[1]
    qkv_one = attn_weight[:, :half_qkv].astype(BF16)
    qkv_two = attn_weight[:, half_qkv : 3 * width].astype(BF16)
    up = jnp.concatenate(
        [
            mlp_weight[0, :, :half_ff],
            attn_weight[:, 3 * width : 3 * width + top],
            mlp_weight[0, :, half_ff:],
            attn_weight[:, 3 * width + top :],
        ],
        axis=1,
    ).astype(BF16)
    down = mlp_weight[1].astype(BF16)
    head16 = head_weight.astype(BF16)
    ada16 = ada_weight.astype(BF16)

    one_y, one_x, two_x, two_y = bits_y, bits_x, bits_x, bits_y
    slots = devices * MAXIMG
    n_x, n_y, n_z = 1 << len(bits_x), 1 << len(bits_y), 1 << len(bits_z)

    def to_two(value):
        shaped = value.reshape((2, n_x, n_y, n_z * MAXIMG) + value.shape[1:])
        return jnp.swapaxes(shaped, 1, 2).reshape(value.shape)

    def to_one(value):
        shaped = value.reshape((2, n_y, n_x, n_z * MAXIMG) + value.shape[1:])
        return jnp.swapaxes(shaped, 1, 2).reshape(value.shape)

    facts = grown(bits_z[:1], facts)
    slim, qkv_one, qkv_two = grown(bits_z[:1], slim, qkv_one, qkv_two)
    facts, slim, qkv_one, qkv_two, up = tie(facts, slim, qkv_one, qkv_two, up)
    facts = grown(bits_z[1:] + bits_y + bits_x + [1], facts)
    slim, qkv_one, qkv_two = grown(bits_z[1:], slim, qkv_one, qkv_two)
    perm_one, perm_one_t = hot_rows(source_rows(path_one + [1], me, rows))
    perm_two, perm_two_t = hot_rows(source_rows(path_two + [1], me, rows))
    facts, slim, qkv_one, qkv_two, up, perm_one, perm_two = tie(
        facts, slim, qkv_one, qkv_two, up, perm_one, perm_two
    )

    total_count = jnp.sum(facts[:, MAXIMG]).astype(F32)
    class_hot = (
        facts[:, :MAXIMG].reshape(slots)[:, None] == jnp.arange(CLASSES, dtype=jnp.int32)[None, :]
    ).astype(BF16)
    class_vec = matmul(class_hot, embed16[:CLASSES])
    class_act = jax.nn.silu(class_vec).astype(BF16)
    cuts = (2 * width, 5 * width)
    act_two = to_two(class_act)
    first = matmul(class_act, ada16[:, : cuts[0]]).astype(BF16)
    up = grown(bits_z[:1], up)
    qkv_one, qkv_two = grown(one_y, qkv_one), grown(two_x, qkv_two)
    slim = grown(bits_y, slim)
    first = keep_half(first, 1, devices)
    for mask in reversed(bits_x):
        first = keep_half(first, mask, devices)
    slim = grown(bits_x, slim)
    first, slim, qkv_one, qkv_two, up, down, head16 = tie(
        first, slim, qkv_one, qkv_two, up, down, head16
    )

    for mask in bits_x[:-1]:
        qkv_one = grown([mask], qkv_one)
    for mask in bits_y[:-1]:
        qkv_two = grown([mask], qkv_two)
    one_far, two_far = swap(qkv_one, bits_x[-1]), swap(qkv_two, bits_y[-1])
    up = grown(bits_z[1:], up)
    slim = grown([1], slim)
    first = keep_all(first, bits_z + bits_y, devices)
    pos_hot = (inside[:, None] == jnp.arange(used, dtype=jnp.int32)[None, :]).astype(BF16)
    level_hot = (scale_row[:, None] == jnp.arange(LEVELS, dtype=jnp.int32)[None, :]).astype(BF16)
    token_hot = jnp.concatenate(
        [pos_hot, level_hot, features[0], jnp.zeros((length, wide - n_embed), BF16)], axis=1
    )
    image = jnp.arange(MAXIMG, dtype=jnp.int32)
    hot = (image_id[:, None] == image[None, :]).astype(F32)
    hot_t = (image[:, None] == image_id[None, :]).astype(F32)
    allowed = (image_id[:, None] == image_id[None, :]) & (scale_row[None, :] <= scale_row[:, None])
    mask_rows = jnp.where(allowed, 0.0, NEG_FILL).astype(F32)
    mod_one = matmul(class_act, ada16[:, cuts[0] : cuts[1]]).astype(BF16)
    mod_two = matmul(act_two, ada16[:, cuts[1] :]).astype(BF16)
    first, slim, token_hot, mask_rows, mod_one, mod_two = tie(
        first, slim, token_hot, mask_rows, mod_one, mod_two
    )

    one_near_c, two_near_c = swap(qkv_one, 1), swap(qkv_two, 1)
    slim = matmul_tn(slim, perm_one)
    gain_rows = slim[n_embed : n_embed + n_gains]
    ada_bias = gain_rows[ada_at:head_at].reshape(1, -1)
    resid_in = matmul(token_hot, slim.astype(BF16)) + gain_rows[0]
    first = first + ada_bias[:, : cuts[0]]
    mods = [first[:, :width], first[:, width:]]
    u_one, u_two = norm_ahead(resid_in, hot, mods[0], mods[1], [perm_one_t, perm_two_t])
    u_one, u_two, one_far, two_far, one_near_c, two_near_c, mod_one, mod_two, up = tie(
        u_one, u_two, one_far, two_far, one_near_c, two_near_c, mod_one, mod_two, up
    )

    one_far_c, two_far_c = swap(one_far, 1), swap(two_far, 1)
    half_up = half_ff + top
    up_one, up_two = grown(one_y, up[:, :half_up]), grown(two_x, up[:, half_up:])
    mod_one, mod_two = keep_half(mod_one, 1, devices), keep_half(mod_two, 1, devices)
    one_far_c, two_far_c, u_one, u_two, mod_one, mod_two, down = tie(
        one_far_c, two_far_c, u_one, u_two, mod_one, mod_two, down
    )

    for mask in reversed(bits_x):
        mod_one = keep_half(mod_one, mask, devices)
    for mask in reversed(bits_y):
        mod_two = keep_half(mod_two, mask, devices)
    down = grown(bits_z[:1], down)
    w_qkv = (
        [qkv_one, one_far, one_near_c, one_far_c],
        [qkv_two, two_far, two_near_c, two_far_c],
    )
    qkv_bias = jnp.concatenate(
        [gain_rows[1:2], jnp.zeros((1, width), F32), gain_rows[2:3]], axis=1
    )
    q_gain, k_gain = gain_rows[5:6], gain_rows[6:7]
    qkv = times_sets([u_one, u_two], w_qkv, qkv_bias)
    mixture = attend(qkv, q_gain, k_gain, mask_rows)
    mixture, up_one, up_two, mod_one, mod_two, down, head16 = tie(
        mixture, up_one, up_two, mod_one, mod_two, down, head16
    )

    for mask in bits_x[:-1]:
        up_one = grown([mask], up_one)
    for mask in bits_y[:-1]:
        up_two = grown([mask], up_two)
    proj_one, proj_two = up_one[:, half_ff:], up_two[:, half_ff:]
    up_one, up_two = up_one[:, :half_ff], up_two[:, :half_ff]
    proj_one_far, proj_two_far = swap(proj_one, bits_x[-1]), swap(proj_two, bits_y[-1])
    for mask in reversed(bits_y):
        mod_one = keep_half(mod_one, mask, devices)
    for mask in reversed(bits_x):
        mod_two = keep_half(mod_two, mask, devices)
    proj_one_c, proj_two_c = swap(proj_one, 1), swap(proj_two, 1)
    mix_one = matmul(mixture, perm_one_t).astype(BF16)
    mix_two = matmul(mixture, perm_two_t).astype(BF16)
    mods_rest = jnp.concatenate([mod_one, mod_two], axis=1)
    (
        mix_one,
        mix_two,
        proj_one_far,
        proj_two_far,
        proj_one_c,
        proj_two_c,
        up_one,
        up_two,
        mods_rest,
        down,
    ) = tie(
        mix_one,
        mix_two,
        proj_one_far,
        proj_two_far,
        proj_one_c,
        proj_two_c,
        up_one,
        up_two,
        mods_rest,
        down,
    )

    up_one_far, up_two_far = swap(up_one, bits_x[-1]), swap(up_two, bits_y[-1])
    w_proj = (
        [proj_one, proj_one_far, proj_one_c, swap(proj_one_far, 1)],
        [proj_two, proj_two_far, proj_two_c, swap(proj_two_far, 1)],
    )
    down = grown(bits_z[1:], down)
    mods_rest = keep_all(mods_rest, bits_z, devices)
    attn_out = times_sets([mix_one, mix_two], w_proj, gain_rows[3:4])
    attn_out, mods_rest, head16 = tie(attn_out, mods_rest, head16)
    mods_rest = mods_rest + ada_bias[:, cuts[0] :]
    mods += [mods_rest[:, at : at + width] for at in range(0, 6 * width, width)]
    u_mid_one, u_mid_two, resid_mid = norm_ahead(
        resid_in, hot, mods[3], mods[4], [perm_one_t, perm_two_t], mods[2], attn_out
    )
    up_one_c, up_two_c = swap(up_one, 1), swap(up_two, 1)
    head16 = grown(bits_y, head16)
    u_mid_one, u_mid_two, up_one_far, up_two_far, up_one_c, up_two_c, down, head16 = tie(
        u_mid_one, u_mid_two, up_one_far, up_two_far, up_one_c, up_two_c, down, head16
    )

    up_one_fc, up_two_fc = swap(up_one_far, 1), swap(up_two_far, 1)
    down_one, down_two = grown(one_y, down[:, :half_ff]), grown(two_x, down[:, half_ff:])
    head16 = grown(bits_z[:1], head16)
    w_up = (
        [up_one, up_one_far, up_one_c, up_one_fc],
        [up_two, up_two_far, up_two_c, up_two_fc],
    )
    up_bias = gain_rows[7:ada_at].reshape(1, -1)
    hidden, active = times_sets([u_mid_one, u_mid_two], w_up, up_bias, bend=True)
    for mask in bits_x[:-1]:
        down_one = grown([mask], down_one)
    for mask in bits_y[:-1]:
        down_two = grown([mask], down_two)
    active, down_one, down_two, row_info = tie(active, down_one, down_two, row_info)

    down_one_far, down_two_far = swap(down_one, bits_x[-1]), swap(down_two, bits_y[-1])
    down_one_c, down_two_c = swap(down_one, 1), swap(down_two, 1)
    for mask in bits_x + [1]:
        row_info = grown([mask], row_info)
    row_info = jnp.swapaxes(row_info, 0, 1).reshape(2, -1)
    active, down_one_far, down_two_far, down_one_c, down_two_c, head16, row_info = tie(
        active, down_one_far, down_two_far, down_one_c, down_two_c, head16, row_info
    )

    head16 = grown(bits_z[1:], head16)
    w_down = (
        [down_one, down_one_far, down_one_c, swap(down_one_far, 1)],
        [down_two, down_two_far, down_two_c, swap(down_two_far, 1)],
    )
    perms = [perm_one, perm_two]
    mlp_out = back_sets(active[None], w_down, perms, gain_rows[4:5], exact=True)
    head_masks = bits_y + bits_z
    perm_head, perm_head_t = hot_rows(
        source_rows(
            [mask // n_vocab for mask in head_masks], lax.axis_index("dp"), head_weight.shape[0]
        )
    )
    head_rel, resid_out = norm_ahead(
        resid_mid, hot, mods[6], mods[7], [perm_head_t], mods[5], mlp_out
    )
    head_rel, head16 = tie(head_rel, head16)

    vocab_masks = bits_x + [1]
    rows_all = grown(bits_x[:-1], head_rel)
    far = swap(rows_all, bits_x[-1])
    near_c = swap(rows_all, 1)
    code_span = head_weight.shape[1]
    code_start = lax.axis_index("vocab") * code_span
    head_bias = lax.dynamic_slice_in_dim(gain_rows[head_at:].reshape(-1), code_start, code_span)
    code = jnp.arange(code_span, dtype=jnp.int32)[None, :] + code_start

    def part_stats(part, info):
        logits = matmul(part, head16) + head_bias
        local_max = jnp.max(logits, axis=1)
        exp_sums = jnp.sum(jnp.exp(logits - local_max[:, None]), axis=1)
        is_target = (code == info[0].astype(jnp.int32)[:, None]).astype(F32)
        picked = jnp.sum(is_target * logits, axis=1)
        return logits, is_target, jnp.stack([local_max, exp_sums, picked])

    each = rows_all.shape[0]
    info_of = [row_info[:, at * each : (at + 1) * each] for at in range(4)]
    near_rows = jnp.concatenate([rows_all, near_c], axis=0)
    near_info = jnp.concatenate([info_of[0], info_of[2]], axis=1)
    far_info = jnp.concatenate([info_of[1], info_of[3]], axis=1)
    near_logits, near_target, near_stats = part_stats(near_rows, near_info)
    near_stats, far = tie(near_stats, far)
    far_rows = jnp.concatenate([far, swap(far, 1)], axis=0)
    far_logits, far_target, far_stats = part_stats(far_rows, far_info)
    places = [x ^ c for x in (0, bits_x[-1]) for c in (0, 1)]
    places = [place ^ other for place in places for other in place_masks(bits_x[:-1])]
    stats = jnp.concatenate([near_stats, far_stats], axis=1)
    group = [stats]
    for other in place_masks(vocab_masks)[1:]:
        their = jnp.split(swap(stats, other), n_vocab, axis=1)
        group.append(
            jnp.concatenate([their[places.index(place ^ other)] for place in places], axis=1)
        )
    row_max = group[0][0]
    for other in group[1:]:
        row_max = jnp.maximum(row_max, other[0])
    totals = sum(other[1] * jnp.exp(other[0] - row_max) for other in group)
    target_logit = sum(other[2] for other in group)
    log_total = row_max + jnp.log(totals)
    loss_part = jnp.sum((near_info[1] * (log_total - target_logit)[: 2 * each])[:length])
    mid = 2 * each

    def part_back(logits, is_target, info, log_total):
        coef = info[1] / total_count
        grad = coef[:, None] * (jnp.exp(logits - log_total[:, None]) - is_target)
        return grad.astype(BF16)

    d_far_logits = part_back(far_logits, far_target, far_info, log_total[mid:])
    d_near_logits = part_back(near_logits, near_target, near_info, log_total[:mid])
    d_far = matmul_nt(d_far_logits, head16).astype(BF16)
    d_near = matmul_nt(d_near_logits, head16).astype(BF16)
    to_core = jnp.concatenate([d_near[each:], d_far[each:]], axis=0)
    back = swap(to_core, 1)
    d_far, d_near = added(d_far[:each], back[each:]), added(d_near[:each], back[:each])
    rows_all = jnp.concatenate([near_rows, far_rows], axis=0)
    d_logits = jnp.concatenate([d_near_logits, d_far_logits], axis=0)
    d_far, head16 = tie(d_far, head16)
    d_head_in = added(d_near, swap(d_far, bits_x[-1]), F32)
    for mask in reversed(bits_x[:-1]):
        d_head_in = keep_half(d_head_in.astype(BF16), mask, devices, F32)
    head_far = matmul_tn(rows_all[:, top:], d_logits).astype(BF16)
    head_near = matmul_tn(rows_all[:, :top], d_logits).astype(BF16)
    bias_grad = lax.dynamic_update_slice(
        jnp.zeros((V,), F32), jnp.sum(d_logits.astype(F32), axis=0), (code_start,)
    )
    d_head_in, head_far, head_near = tie(d_head_in, head_far, head_near)

    def far_rows_of(left, right, columns):
        return grad_rows(left, right, (top, width), columns)

    def meet_far(left, right, columns, back):
        return grad_rows(left, right, (quarter, top), columns, back)

    def meet_near(left, right, columns, back):
        return grad_rows(left, right, (0, quarter), columns, back)

    def cross(one, two):
        return swap(one, bits_x[-1]), swap(two, bits_y[-1])

    def join(one, two, one_back, two_back):
        one, two = added(one, one_back), added(two, two_back)
        for mask in reversed(bits_y[:-1]):
            two = keep_half(two, mask, devices)
        for mask in reversed(bits_x[:-1]):
            one = keep_half(one, mask, devices)
        half = one.shape[0] // 2
        return tuple(
            jnp.concatenate([one[at : at + half], two[at : at + half]], axis=1) for at in (0, half)
        )

    def turn(one, two, one_back, two_back):
        one, one_far = halves_of(one, one_back)
        two, two_far = halves_of(two, two_back)
        for mask in reversed(bits_x[:-1]):
            whole_one = jnp.concatenate([one, one_far], axis=0)
            one, one_far = halves_of(
                whole_one[: whole_one.shape[0] // 2],
                swap(whole_one[whole_one.shape[0] // 2 :], mask),
            )
        for mask in reversed(bits_y[:-1]):
            whole_two = jnp.concatenate([two, two_far], axis=0)
            two, two_far = halves_of(
                whole_two[: whole_two.shape[0] // 2],
                swap(whole_two[whole_two.shape[0] // 2 :], mask),
            )
        return one, one_far, two, two_far

    def cross_back(one_far, two_far):
        return swap(one_far, bits_y[-1]), swap(two_far, bits_x[-1])

    ones, twos = (0, half_ff), (half_ff, FF)
    q_ones, q_twos = (0, half_qkv), (half_qkv, 3 * width)
    active = active[None]
    head_back = swap(head_far, head_masks[-1])
    d_head_in = in_halves_outside(lambda part: matmul(part, perm_head), d_head_in)
    d_resid_out, d_shift_head, d_scale_head, down_bias, d_gate_two, d_low_one, d_low_two = (
        norm_back(
            resid_out,
            d_head_in,
            hot,
            hot_t,
            mods[7],
            gate=mods[5],
            branch=mlp_out,
            perms=[perm_one_t, perm_two_t],
        )
    )
    down_f1, down_f2 = far_rows_of(d_low_one, active, ones), far_rows_of(d_low_two, active, twos)
    d_low_one, d_low_two, down_f1, down_f2 = tie(d_low_one, d_low_two, down_f1, down_f2)
    down_b1, down_b2 = swap(down_f1, 1), swap(down_f2, 1)
    d_hid, up_bias_sum = times_sets([d_low_one, d_low_two], w_down, hidden=hidden)
    d_hid = d_hid[None]
    d_hid, down_b1, down_b2, head_back, head_near = tie(
        d_hid, down_b1, down_b2, head_back, head_near
    )
    head_near, head_far = halves_of(head_near, head_back)
    down_f1 = meet_far(d_low_one, active, ones, down_b1)
    down_f2 = meet_far(d_low_two, active, twos, down_b2)
    d_hid, down_f1, down_f2, head_far = tie(d_hid, down_f1, down_f2, head_far)
    down_x1, down_x2 = cross(down_f1, down_f2)
    head_back = swap(head_far, head_masks[-2])
    up_f1, up_f2 = far_rows_of(u_mid_one, d_hid, ones), far_rows_of(u_mid_two, d_hid, twos)
    up_b1, up_b2 = swap(up_f1, 1), swap(up_f2, 1)
    down_n1 = meet_near(d_low_one, active, ones, down_b1)
    down_n2 = meet_near(d_low_two, active, twos, down_b2)
    d_u = back_sets(d_hid, w_up, perms)
    d_u, down_x1, down_x2, down_n1, down_n2, up_b1, up_b2, head_back, head_near = tie(
        d_u, down_x1, down_x2, down_n1, down_n2, up_b1, up_b2, head_back, head_near
    )
    down_n1, down_f1, down_n2, down_f2 = turn(down_n1, down_n2, down_x1, down_x2)
    head_near = added(head_near, head_back)
    down_x1, down_x2 = cross_back(down_f1, down_f2)
    head_grad = keep_all(head_near, head_masks[:-2], devices)
    up_f1 = meet_far(u_mid_one, d_hid, ones, up_b1)
    up_f2 = meet_far(u_mid_two, d_hid, twos, up_b2)
    d_resid_mid, d_shift_two, d_scale_two, proj_bias, d_gate_one, d_low = norm_back(
        resid_mid, d_u, hot, hot_t, mods[4], beyond=d_resid_out, gate=mods[2], branch=attn_out
    )
    d_mod = jnp.concatenate(
        [d_gate_one, d_shift_two, d_scale_two, d_gate_two, d_shift_head, d_scale_head], axis=1
    ).astype(BF16)
    d_low, d_mod, down_x1, down_x2, down_n1, down_n2, up_f1, up_f2, head_grad = tie(
        d_low, d_mod, down_x1, down_x2, down_n1, down_n2, up_f1, up_f2, head_grad
    )
    up_x1, up_x2 = cross(up_f1, up_f2)
    down_near, down_far = join(down_n1, down_n2, down_x1, down_x2)
    down_back = swap(down_far, bits_z[-1])
    all_mod = grown(bits_z[:1], d_mod)
    d_low3 = d_low[None]
    p_ones, p_twos = (0, top), (top, width)
    proj_f1 = far_rows_of(mix_one, d_low3, p_ones)
    proj_f2 = far_rows_of(mix_two, d_low3, p_twos)
    proj_b1, proj_b2 = swap(proj_f1, 1), swap(proj_f2, 1)
    up_n1 = meet_near(u_mid_one, d_hid, ones, up_b1)
    up_n2 = meet_near(u_mid_two, d_hid, twos, up_b2)
    d_mix = back_sets(d_low3, w_proj, perms, out=BF16)
    d_mix, proj_b1, proj_b2 = tie(d_mix, proj_b1, proj_b2)
    proj_f1 = meet_far(mix_one, d_low3, p_ones, proj_b1)
    proj_f2 = meet_far(mix_two, d_low3, p_twos, proj_b2)
    proj_n1 = meet_near(mix_one, d_low3, p_ones, proj_b1)
    proj_n2 = meet_near(mix_two, d_low3, p_twos, proj_b2)
    d_qkv, attn_sums = attend_back(qkv, q_gain, k_gain, mask_rows, d_mix)
    d_qkv, up_x1, up_x2, up_n1, up_n2, down_back, down_near, all_mod, proj_f1, proj_f2 = tie(
        d_qkv, up_x1, up_x2, up_n1, up_n2, down_back, down_near, all_mod, proj_f1, proj_f2
    )
    up_n1, up_f1, up_n2, up_f2 = turn(up_n1, up_n2, up_x1, up_x2)
    up_x1, up_x2 = cross_back(up_f1, up_f2)
    down_near, down_far = halves_of(down_near, down_back)
    down_back = swap(down_far, bits_z[-2])
    proj_x1, proj_x2 = cross(proj_f1, proj_f2)
    qkv_f1, qkv_f2 = far_rows_of(u_one, d_qkv, q_ones), far_rows_of(u_two, d_qkv, q_twos)
    d_u = back_sets(d_qkv, w_qkv, perms)
    d_u, up_x1, up_x2, up_n1, up_n2, down_back, proj_x1, proj_x2, qkv_f1, qkv_f2, all_mod = tie(
        d_u, up_x1, up_x2, up_n1, up_n2, down_back, proj_x1, proj_x2, qkv_f1, qkv_f2, all_mod
    )
    qkv_b1, qkv_b2 = swap(qkv_f1, 1), swap(qkv_f2, 1)
    up_near, up_far = join(up_n1, up_n2, up_x1, up_x2)
    up_back = swap(up_far, bits_z[-1])
    all_mod = grown(bits_z[1:], all_mod)
    d_resid_in, d_shift_one, d_scale_one, word_bias, d_res16 = norm_back(
        resid_in, d_u, hot, hot_t, mods[1], beyond=d_resid_mid
    )
    d_first = jnp.concatenate([d_shift_one, d_scale_one], axis=1).astype(BF16)
    d_res16, d_first, qkv_b1, qkv_b2 = tie(d_res16, d_first, qkv_b1, qkv_b2)
    qkv_f1 = meet_far(u_one, d_qkv, q_ones, qkv_b1)
    qkv_f2 = meet_far(u_two, d_qkv, q_twos, qkv_b2)
    d_res16, qkv_f1, qkv_f2, d_first = tie(d_res16, qkv_f1, qkv_f2, d_first)
    qkv_x1, qkv_x2 = cross(qkv_f1, qkv_f2)
    all_first = grown(bits_z, d_first)
    ada_sums = jnp.sum(
        jnp.concatenate([d_first, d_mod], axis=1).astype(F32), axis=0, keepdims=True
    )
    arrays = [word_bias, attn_sums, proj_bias, down_bias, up_bias_sum, ada_sums, bias_grad[None]]
    plan = [(0, 0), (1, 2), (1, 3), (2, 0), (3, 0), (1, 0), (1, 1), (4, 0), (5, 0), (6, 0)]
    d_slim = slim_back(d_res16, token_hot, arrays, plan, perm_one, n_embed)
    d_slim = keep_half(d_slim, 1, devices)
    proj_n1, proj_f1, proj_n2, proj_f2 = turn(proj_n1, proj_n2, proj_x1, proj_x2)
    proj_x1, proj_x2 = cross_back(proj_f1, proj_f2)
    qkv_n1 = meet_near(u_one, d_qkv, q_ones, qkv_b1)
    qkv_n2 = meet_near(u_two, d_qkv, q_twos, qkv_b2)
    (
        qkv_x1,
        qkv_x2,
        qkv_n1,
        qkv_n2,
        all_first,
        d_slim,
        proj_x1,
        proj_x2,
        proj_n1,
        proj_n2,
        up_back,
        up_near,
        all_mod,
    ) = tie(
        qkv_x1,
        qkv_x2,
        qkv_n1,
        qkv_n2,
        all_first,
        d_slim,
        proj_x1,
        proj_x2,
        proj_n1,
        proj_n2,
        up_back,
        up_near,
        all_mod,
    )
    qkv_n1, qkv_f1, qkv_n2, qkv_f2 = turn(qkv_n1, qkv_n2, qkv_x1, qkv_x2)
    qkv_x1, qkv_x2 = cross_back(qkv_f1, qkv_f2)
    up_near, up_far = halves_of(up_near, up_back)
    up_back = swap(up_far, bits_z[-2])
    cut = cuts[1] - cuts[0]
    all_first = jnp.concatenate([all_first, all_mod[:, :cut]], axis=1)
    all_first = grown(bits_y, all_first)
    for mask in reversed(bits_x):
        d_slim = keep_half(d_slim, mask, devices)
    qkv_x1, qkv_x2, qkv_n1, qkv_n2, up_back, up_near, all_first, all_mod, d_slim = tie(
        qkv_x1, qkv_x2, qkv_n1, qkv_n2, up_back, up_near, all_first, all_mod, d_slim
    )
    near, far = join(
        jnp.concatenate([qkv_n1, proj_n1], axis=1),
        jnp.concatenate([qkv_n2, proj_n2], axis=1),
        jnp.concatenate([qkv_x1, proj_x1], axis=1),
        jnp.concatenate([qkv_x2, proj_x2], axis=1),
    )
    attn_back = swap(far, bits_z[-1])
    all_two = grown(bits_x, all_mod[:, cut:])
    all_first = grown(bits_x, all_first)
    d_slim = keep_all(d_slim, bits_z + bits_y, devices)
    attn_back, near, all_two, all_first, d_slim = tie(attn_back, near, all_two, all_first, d_slim)
    near, far = halves_of(near, attn_back)
    attn_back = swap(far, bits_z[-2])
    all_two = grown(bits_y + [1], all_two)
    all_first = grown([1], all_first)

    def close(near, back):
        masks = bits_z[:-2]
        near = added(near, back, BF16 if masks else F32)
        return keep_all(near, masks, devices)

    attn_rows, up_rows, down_rows = (
        close(near, attn_back),
        close(up_near, up_back),
        close(down_near, down_back),
    )
    slim_grad = d_slim.T
    half_attn = half_qkv + top
    attn_grad = jnp.concatenate(
        [
            attn_rows[:, :half_qkv],
            attn_rows[:, half_attn : half_attn + half_qkv],
            attn_rows[:, half_qkv:half_attn],
            attn_rows[:, half_attn + half_qkv :],
        ],
        axis=1,
    )
    mlp_grad = jnp.stack([up_rows, down_rows])
    ada_grad = jnp.concatenate([matmul_tn(class_act, all_first), matmul_tn(act_two, all_two)], axis=1)
    d_class_act = matmul_nt(all_first, ada16[:, : cuts[1]]) + to_one(
        matmul_nt(all_two, ada16[:, cuts[1] :])
    )
    _, silu_back = jax.vjp(jax.nn.silu, class_vec)
    d_class = precise_tn(class_hot.astype(F32), silu_back(d_class_act)[0])
    embed_grad = jnp.concatenate(
        [
            d_class,
            slim_grad[:used],
            jnp.zeros((POSITIONS - used, rows), F32),
            slim_grad[used:n_embed],
        ],
        axis=0,
    )
    gains_grad = slim_grad[n_embed : n_embed + n_gains]

    gradients = (attn_grad, mlp_grad, ada_grad, embed_grad, gains_grad, head_grad)
    squares_local = jnp.zeros((), F32)
    for gradient in gradients:
        squares_local = squares_local + jnp.sum(gradient * gradient)
    sums = sum_all(
        jnp.stack([squares_local, loss_part])[None], [1] + bits_x + bits_y + bits_z, devices
    )
    total_sq, loss_sum = sums[0, 0], sums[0, 1]
    grad_norm = jnp.sqrt(total_sq)
    clip_factor = jnp.minimum(1.0, CLIP_NORM / (grad_norm + 1e-06))
    masters = (attn_weight, mlp_weight, ada_weight, embed_weight, gains_weight, head_weight)
    moments = (attn_moment, mlp_moment, ada_moment, embed_moment, gains_moment, head_moment)
    squares = (attn_square, mlp_square, ada_square, embed_square, gains_square, head_square)
    updates = []
    for number in range(6):
        updates.extend(
            adam_step(
                masters[number],
                moments[number],
                squares[number],
                gradients[number],
                clip_factor,
                RATES[number],
            )
        )
    return tuple(updates) + (grad_norm, loss_sum, total_count)


def solution(mesh):
    n_dp, n_vocab = mesh.shape["dp"], mesh.shape["vocab"]
    n_z = 1 << (n_dp.bit_length() // 2)
    devices = n_dp * n_vocab

    def bits(least, top):
        found = []
        while least < top:
            found, least = [least] + found, least * 2
        return found

    ways = {"devices": devices, "n_vocab": n_vocab}
    ways["x"] = bits(2, n_vocab)
    ways["y"] = bits(n_vocab, devices // n_z)
    ways["z"] = bits(devices // n_z, devices)
    every = ("dp", "vocab")
    by_row = P(every, None)
    by_mid = P(None, every, None)
    by_column = P(None, every)
    head = P("dp", "vocab")
    placed = (P(every, None, None), by_row, by_row, by_row, by_row)
    for spec in (by_row, by_mid, by_row, by_column, by_column, head):
        placed = placed + (spec,) * 3
    given = ()
    for spec in (by_row, by_mid, by_row, by_column, by_column, head):
        given = given + (spec,) * 4

    def step(*arrays):
        return per_device(ways, *arrays)

    return jax.shard_map(
        step, mesh=mesh, in_specs=placed, out_specs=given + (P(), P(), P()), check_vma=False
    )
```

```python
import jax
import jax.numpy as jnp
from jax import lax
from jax.experimental import pallas as pl
from jax.experimental.pallas import tpu as pltpu
from jax.sharding import PartitionSpec as P

HEADS = 16
HEAD_DIM = 64
FF = 4096
V = 4096
CHANNELS = 32
CLASSES = 1001
POSITIONS = 680
LEVELS = 10
MAXIMG = 8
STEPS = 10


EPS_NORM = 1e-06
BETA_ONE = 0.9
BETA_TWO = 0.95
ADAM_EPS = 1e-08
DECAY = 0.05
CLIP_NORM = 0.001
RATES = (0.03, 0.03, 0.03, 0.15, 0.4, 0.03)
NEG_FILL = -1e30
BF16 = jnp.bfloat16
F32 = jnp.float32
SPANS = (1024, 512)
TOKENS = 128
PAIR = 2 * HEAD_DIM


def matmul(left, right):
    return jnp.dot(left, right, preferred_element_type=F32)


def matmul_tn(left, right):
    return lax.dot_general(left, right, (((0,), (0,)), ((), ())), preferred_element_type=F32)


def matmul_nt(left, right):
    return lax.dot_general(left, right, (((1,), (1,)), ((), ())), preferred_element_type=F32)


def precise_tn(left, right):
    return lax.dot_general(left, right, (((0,), (0,)), ((), ())), precision=lax.Precision.HIGHEST)


def pick(hot, values):
    return in_halves(lambda part: matmul(hot, part), values)


def in_halves(times, values):
    upper = values.astype(BF16)
    return times(upper) + times((values - upper.astype(F32)).astype(BF16))


def in_halves_outside(times, values):
    upper = lax.reduce_precision(values, 8, 7)
    return times(upper.astype(BF16)) + times((values - upper).astype(BF16))


def swapped(value, mask, devices):
    return lax.ppermute(value, ("dp", "vocab"), [(i, i ^ mask) for i in range(devices)])


def tie(*values):
    return lax.optimization_barrier(values)


def grow(value, mask, devices):
    return jnp.concatenate([value, swapped(value, mask, devices)], axis=0)


def spread(value, masks, devices):
    if len(masks) == 2:
        masks = masks + [masks[0] ^ masks[1]]
    return [value] + [swapped(value, mask, devices) for mask in masks]


def stack(parts):
    return jnp.concatenate(parts, axis=0)


def widen(value, masks, devices):
    for mask in masks[:-1]:
        value = grow(value, mask, devices)
    return [value, swapped(value, masks[-1], devices)]


def added(mine, theirs, out=BF16):
    return (mine.astype(F32) + theirs.astype(F32)).astype(out)


def keep_half(value, mask, devices, out=BF16):
    half = value.shape[0] // 2
    return added(value[:half], swapped(value[half:].astype(BF16), mask, devices), out)


def lend(value, masks, devices):
    for mask in reversed(masks[1:]):
        value = keep_half(value, mask, devices)
    half = value.shape[0] // 2
    return [value[:half], swapped(value[half:].astype(BF16), masks[0], devices)]


def keep_all(value, masks, devices):
    for mask in reversed(masks):
        value = keep_half(value, mask, devices, F32 if mask == masks[0] else BF16)
    return value


def halves_of(mine, back, out=BF16):
    half = mine.shape[0] // 2
    return (added(mine[:half], back[:half], out), added(mine[half:], back[half:], out))


def sum_all(value, bits, devices):
    for at in range(0, len(bits), 2):
        masks = bits[at : at + 2]
        if len(masks) == 2:
            masks = masks + [masks[0] ^ masks[1]]
        value = value + sum(swapped(value, mask, devices) for mask in masks)
    return value


def place_masks(masks):
    places = [0]
    for mask in masks:
        places = places + [place ^ mask for place in places]
    return places


def source_rows(masks, me, rows):
    differ = jnp.repeat(jnp.array(place_masks(masks), jnp.int32), rows)
    row = jnp.tile(jnp.arange(rows, dtype=jnp.int32), 1 << len(masks))
    return (differ ^ me) * rows + row


def hot_rows(source):
    place = jnp.arange(source.shape[0], dtype=jnp.int32)
    return (
        (source[:, None] == place[None, :]).astype(BF16),
        (place[:, None] == source[None, :]).astype(BF16),
    )


def run(body, grid, given, specs, outs, out_specs, scratch=()):
    return pl.pallas_call(
        body,
        grid=grid,
        in_specs=specs,
        out_shape=outs,
        out_specs=out_specs,
        scratch_shapes=scratch,
        compiler_params=pltpu.CompilerParams(vmem_limit_bytes=48 << 20),
        cost_estimate=pl.CostEstimate(flops=1000, bytes_accessed=1000, transcendentals=0),
    )(*given)


def whole(value):
    return pl.BlockSpec(value.shape, lambda j: (0,) * value.ndim)


def span_of(*sizes):
    return [span for span in SPANS if all(size % span == 0 for size in sizes)][0]


def columns_of(sets):
    return [blocks[0].shape[1] if used is None else used for blocks, used in sets]


def two_sets(sets, first, span):
    specs = [
        pl.BlockSpec((block.shape[0], span), lambda j: (0, jnp.minimum(j, first - 1)))
        for block in sets[0][0]
    ]
    specs += [
        pl.BlockSpec((block.shape[0], span), lambda j: (0, jnp.maximum(j - first, 0)))
        for block in sets[1][0]
    ]
    return specs


def gelu_parts(value):
    inner = 0.7978845608028654 * (value + 0.044715 * (value * value * value))
    bend = jnp.tanh(inner)
    return bend


def gelu(value):
    return 0.5 * value * (1.0 + gelu_parts(value))


def gelu_slope(value):
    bend = gelu_parts(value)
    rise = 0.7978845608028654 * (1.0 + 3.0 * 0.044715 * value * value)
    return 0.5 * (1.0 + bend) + 0.5 * value * (1.0 - bend * bend) * rise


def times_sets(left, sets, bias=None, hidden=None, bend=False):
    tokens = left[0].shape[0]
    columns = columns_of(sets)
    span = span_of(*columns)
    first, steps = columns[0] // span, sum(columns) // span
    specs = two_sets(sets, first, span)
    count = len(sets[0][0])
    extra = [value for value in (bias, hidden) if value is not None]
    column = lambda j: (0, j)
    extra_specs = [pl.BlockSpec((value.shape[0], span), column) for value in extra]

    def body(one_ref, two_ref, *refs):
        extras, blocks = refs[: len(extra)], refs[len(extra) : len(extra) + 2 * count]
        outs = refs[len(extra) + 2 * count :]

        def part(u_ref, blocks):
            total, at = None, 0
            for block in blocks:
                rows = block.shape[0]
                term = matmul(u_ref[:, at : at + rows], block[...])
                total = term if total is None else total + term
                at += rows
            if bias is not None:
                total = total + extras[0][...]
            if hidden is not None:
                slope = gelu_slope(extras[-1][...])
                low = (total * slope).astype(BF16)
                outs[0][...] = low
                outs[1][...] = jnp.sum(low.astype(F32), axis=0, keepdims=True)
            else:
                outs[0][...] = total
                if bend:
                    outs[1][...] = gelu(total).astype(BF16)

        pl.when(pl.program_id(0) < first)(lambda: part(one_ref, blocks[:count]))
        pl.when(pl.program_id(0) >= first)(lambda: part(two_ref, blocks[count:]))

    wide = steps * span
    shape = jax.ShapeDtypeStruct
    outs, out_specs = [shape((tokens, wide), F32)], [pl.BlockSpec((tokens, span), column)]
    if hidden is not None:
        outs = [shape((tokens, wide), BF16), shape((1, wide), F32)]
        out_specs.append(pl.BlockSpec((1, span), column))
    elif bend:
        outs.append(shape((tokens, wide), BF16))
        out_specs.append(pl.BlockSpec((tokens, span), column))
    given = list(left) + extra + list(sets[0][0]) + list(sets[1][0])
    specs = [whole(value) for value in left] + extra_specs + specs
    found = run(body, (steps,), given, specs, outs, out_specs)
    return found if len(outs) > 1 else found[0]


def span_spec(value, span):
    each = value.shape[2] // span
    return pl.BlockSpec((1, value.shape[1], span), lambda j: (j // each, 0, j % each))


def back_sets(right, sets, perms, bias=None, exact=False, out=F32):
    tokens = right.shape[1]
    columns = columns_of(sets)
    span = span_of(right.shape[2], *columns)
    first, steps = columns[0] // span, sum(columns) // span
    specs = two_sets(sets, first, span)
    count = len(sets[0][0])
    width = perms[0].shape[0]
    extra = [] if bias is None else [bias]

    def body(right_ref, one_ref, two_ref, *refs):
        extras, blocks = refs[: len(extra)], refs[len(extra) : len(extra) + 2 * count]
        out_ref, one_sum, two_sum = refs[len(extra) + 2 * count :]
        step = pl.program_id(0)

        def part(sums, blocks, start):
            terms = [matmul_nt(right_ref[0], block[...]) for block in blocks]
            term = jnp.concatenate(terms, axis=1)

            @pl.when(step == start)
            def _():
                sums[...] = term

            @pl.when(step > start)
            def _():
                sums[...] += term

        pl.when(step < first)(lambda: part(one_sum, blocks[:count], 0))
        pl.when(step >= first)(lambda: part(two_sum, blocks[count:], first))

        @pl.when(step == steps - 1)
        def _():
            total = None
            for sums, perm in ((one_sum, one_ref), (two_sum, two_ref)):
                if exact:
                    term = in_halves(lambda part: matmul(part, perm[...]), sums[...])
                else:
                    term = matmul(sums[...].astype(BF16), perm[...])
                total = term if total is None else total + term
            if bias is not None:
                total = total + extras[0][...]
            out_ref[...] = total.astype(out)

    given = [right] + list(perms) + extra + list(sets[0][0]) + list(sets[1][0])
    specs = [span_spec(right, span)] + [whole(value) for value in list(perms) + extra] + specs
    outs = jax.ShapeDtypeStruct((tokens, width), out)
    scratch = [pltpu.VMEM((tokens, width), F32)] * 2
    return run(body, (steps,), given, specs, outs, whole(outs), scratch)


def grad_sets(left, right, columns, back=None):
    tokens, width = left[0].shape
    parts = 2 if back is not None else 1
    half = width // 2
    count = half // parts
    wide = [stop - start for start, stop in columns]
    span = span_of(right.shape[2], *wide, *[start for start, _ in columns])
    each = right.shape[2] // span
    first, steps = wide[0] // span, sum(wide) // span
    at = [start // span for start, _ in columns]

    def place(j):
        block = jnp.where(j < first, j + at[0], j - first + at[1])
        return (block // each, 0, block % each)

    def body(one_ref, two_ref, right_ref, *refs):
        def part(left_ref, outs):
            total = matmul_tn(left_ref[...], right_ref[0])
            if back is not None:
                total = total + refs[0][...].astype(F32)
            for which, out in enumerate(outs):
                out[...] = total[which * count : (which + 1) * count].astype(BF16)

        step = pl.program_id(0)
        if back is None:
            pl.when(step < first)(lambda: part(one_ref, refs))
            pl.when(step >= first)(lambda: part(two_ref, refs))
        else:
            pl.when(step < first)(lambda: part(one_ref, refs[1:3]))
            pl.when(step >= first)(lambda: part(two_ref, refs[3:]))

    side = 0 if back is not None else 1
    given = list(left) + [right]
    specs = [pl.BlockSpec((tokens, half), lambda j: (0, side)) for _ in left]
    specs.append(pl.BlockSpec((1, tokens, span), place))
    own = pl.BlockSpec((half, span), lambda j: (0, j))
    if back is None:
        outs = jax.ShapeDtypeStruct((half, sum(wide)), BF16)
        return run(body, (steps,), given, specs, outs, own)
    outs, out_specs = [], []
    indices = (lambda j: (0, jnp.minimum(j, first - 1)), lambda j: (0, jnp.maximum(j - first, 0)))
    for size, index in zip(wide, indices):
        outs += [jax.ShapeDtypeStruct((count, size), BF16)] * 2
        out_specs += [pl.BlockSpec((count, span), index)] * 2
    return run(body, (steps,), given + [back], specs + [own], outs, out_specs)


def head_scale(value, left_half):
    square = value * value
    one = jnp.sum(jnp.where(left_half, square, 0.0), axis=1, keepdims=True)
    two = jnp.sum(jnp.where(left_half, 0.0, square), axis=1, keepdims=True)
    return jnp.where(
        left_half,
        lax.rsqrt(one * (1.0 / HEAD_DIM) + EPS_NORM),
        lax.rsqrt(two * (1.0 / HEAD_DIM) + EPS_NORM),
    )


def soft_rows(q_norm, k_norm, mask):
    scores = matmul_nt(q_norm, k_norm) * HEAD_DIM ** (-0.5) + mask
    terms = jnp.exp(scores - jnp.max(scores, axis=1, keepdims=True))
    return terms * (1.0 / jnp.sum(terms, axis=1, keepdims=True))


def pair_specs(tokens):
    pairs = HEADS // 2
    return [
        pl.BlockSpec((tokens, PAIR), lambda j: (0, j)),
        pl.BlockSpec((tokens, PAIR), lambda j: (0, pairs + j)),
        pl.BlockSpec((tokens, PAIR), lambda j: (0, 2 * pairs + j)),
        pl.BlockSpec((1, PAIR), lambda j: (0, j)),
        pl.BlockSpec((1, PAIR), lambda j: (0, j)),
        pl.BlockSpec((tokens, tokens), lambda j: (0, 0)),
    ]


def attend(qkv, q_gain, k_gain, mask):
    tokens, width = qkv.shape[0], qkv.shape[1] // 3

    def body(q_ref, k_ref, v_ref, qg_ref, kg_ref, mask_ref, out_ref):
        left_half = lax.broadcasted_iota(jnp.int32, (1, PAIR), 1) < HEAD_DIM
        query, key = q_ref[...], k_ref[...]
        q_norm = (query * head_scale(query, left_half) * qg_ref[...]).astype(BF16)
        k_norm = (key * head_scale(key, left_half) * kg_ref[...]).astype(BF16)
        v_low = v_ref[...].astype(BF16)
        zero = jnp.zeros_like(q_norm)
        mixed = []
        for one in (jnp.where(left_half, q_norm, zero), jnp.where(left_half, zero, q_norm)):
            probs = soft_rows(one, k_norm, mask_ref[...])
            mixed.append(matmul(probs.astype(BF16), v_low))
        out_ref[...] = jnp.where(left_half, mixed[0], mixed[1]).astype(BF16)

    outs = jax.ShapeDtypeStruct((tokens, width), BF16)
    spec = pl.BlockSpec((tokens, PAIR), lambda j: (0, j))
    given = [qkv, qkv, qkv, q_gain, k_gain, mask]
    return run(body, (HEADS // 2,), given, pair_specs(tokens), outs, spec)


def attend_back(qkv, q_gain, k_gain, mask, d_mix):
    tokens, width = qkv.shape[0], qkv.shape[1] // 3

    def body(q_ref, k_ref, v_ref, qg_ref, kg_ref, mask_ref, dm_ref, out_ref, sums_ref):
        left_half = lax.broadcasted_iota(jnp.int32, (1, PAIR), 1) < HEAD_DIM
        query, key = q_ref[...], k_ref[...]
        q_scale, k_scale = head_scale(query, left_half), head_scale(key, left_half)
        q_norm = (query * q_scale * qg_ref[...]).astype(BF16)
        k_norm = (key * k_scale * kg_ref[...]).astype(BF16)
        v_low, d_mix = v_ref[...].astype(BF16), dm_ref[...]
        zero = jnp.zeros_like(q_norm)
        found = []
        for side in range(2):
            own = (lambda v: jnp.where(left_half, v, zero)) if side == 0 else (
                lambda v: jnp.where(left_half, zero, v)
            )
            probs = soft_rows(own(q_norm), k_norm, mask_ref[...])
            d_values = matmul_tn(probs.astype(BF16), d_mix)
            d_probs = matmul_nt(own(d_mix), v_low)
            inner = jnp.sum(d_probs * probs, axis=1, keepdims=True)
            d_scores = (probs * (d_probs - inner)).astype(BF16)
            found.append((matmul(d_scores, k_norm), matmul_tn(d_scores, q_norm), d_values))
        d_qn, d_kn, d_values = (jnp.where(left_half, one, two) for one, two in zip(*found))
        sums = []
        for at, value, scale, gain, d_norm in (
            (0, query, q_scale, qg_ref[...], d_qn * HEAD_DIM ** (-0.5)),
            (1, key, k_scale, kg_ref[...], d_kn * HEAD_DIM ** (-0.5)),
        ):
            product = d_norm * value
            sums.append(jnp.sum(product * scale, axis=0, keepdims=True))
            product = product * gain
            one = jnp.sum(jnp.where(left_half, product, 0.0), axis=1, keepdims=True)
            two = jnp.sum(jnp.where(left_half, 0.0, product), axis=1, keepdims=True)
            mean = jnp.where(left_half, one, two) * (1.0 / HEAD_DIM)
            d_value = scale * (gain * d_norm - value * (scale * scale) * mean)
            out_ref[at] = d_value.astype(BF16)
        out_ref[2] = d_values.astype(BF16)
        sums.append(jnp.sum(out_ref[0].astype(F32), axis=0, keepdims=True))
        sums.append(jnp.sum(out_ref[2].astype(F32), axis=0, keepdims=True))
        sums_ref[...] = jnp.concatenate(sums + [jnp.zeros((4, PAIR), F32)], axis=0)

    outs = [
        jax.ShapeDtypeStruct((3, tokens, width), BF16),
        jax.ShapeDtypeStruct((8, width), F32),
    ]
    out_specs = [
        pl.BlockSpec((3, tokens, PAIR), lambda j: (0, 0, j)),
        pl.BlockSpec((8, PAIR), lambda j: (0, j)),
    ]
    given = [qkv, qkv, qkv, q_gain, k_gain, mask, d_mix]
    specs = pair_specs(tokens) + [pl.BlockSpec((tokens, PAIR), lambda j: (0, j))]
    return run(body, (HEADS // 2,), given, specs, outs, out_specs)


def row_stats(value):
    center = value - jnp.mean(value, axis=1, keepdims=True)
    return center, lax.rsqrt(jnp.mean(center * center, axis=1, keepdims=True) + EPS_NORM)


def by_tokens(value):
    return pl.BlockSpec((TOKENS, value.shape[1]), lambda j: (j, 0))


def norm_ahead(value, hot, shift, scale, perms, gate=None, branch=None):
    tokens, width = value.shape
    extra = [] if gate is None else [gate, branch]

    def body(value_ref, hot_ref, shift_ref, scale_ref, *refs):
        total = value_ref[...]
        outs = refs[len(extra) + len(perms) :]
        if gate is not None:
            total = total + pick(hot_ref[...], refs[0][...]) * refs[1][...]
            outs[-1][...] = total
        center, inverse = row_stats(total)
        scales = 1.0 + pick(hot_ref[...], scale_ref[...])
        normed = center * inverse * scales + pick(hot_ref[...], shift_ref[...])
        normed = normed.astype(BF16)
        for perm_ref, out_ref in zip(refs[len(extra) : len(extra) + len(perms)], outs):
            out_ref[...] = matmul(normed, perm_ref[...]).astype(BF16)

    given = [value, hot, shift, scale] + extra + list(perms)
    specs = [by_tokens(value), by_tokens(hot), whole(shift), whole(scale)]
    specs += [whole(gate), by_tokens(branch)] if extra else []
    specs += [whole(perm) for perm in perms]
    outs = [jax.ShapeDtypeStruct((tokens, width), BF16) for _ in perms]
    outs += [jax.ShapeDtypeStruct((tokens, width), F32)] if extra else []
    out_specs = [by_tokens(value) for _ in outs]
    return run(body, (tokens // TOKENS,), given, specs, outs, out_specs)


def norm_back(value, d_out, hot, hot_t, scale, beyond=None, gate=None, branch=None, perms=()):
    tokens, width = value.shape
    gated = gate is not None
    tall = [value, d_out] + ([] if beyond is None else [beyond]) + ([branch] if gated else [])
    flat = [scale] + ([gate] if gated else []) + list(perms)

    def body(hot_ref, hot_t_ref, *refs):
        talls, flats = refs[: len(tall)], refs[len(tall) : len(tall) + len(flat)]
        outs = refs[len(tall) + len(flat) :]
        total_ref, shift_ref, scale_ref, column_ref = outs[:4]
        d_out = talls[1][...]
        center, inverse = row_stats(talls[0][...])
        normed = center * inverse
        d_norm = d_out * (1.0 + pick(hot_ref[...], flats[0][...]))
        mean = jnp.mean(d_norm, axis=1, keepdims=True)
        along = jnp.mean(d_norm * normed, axis=1, keepdims=True)
        total = (d_norm - mean - normed * along) * inverse
        if beyond is not None:
            total = total + talls[2][...]
        total_ref[...] = total
        sums = [
            (shift_ref, pick(hot_t_ref[...], d_out)),
            (scale_ref, pick(hot_t_ref[...], d_out * normed)),
        ]
        if gated:
            sums.append((outs[4], pick(hot_t_ref[...], total * talls[-1][...])))
            low = (pick(hot_ref[...], flats[1][...]) * total).astype(BF16)
            column = jnp.sum(low.astype(F32), axis=0, keepdims=True)
        else:
            low = total.astype(BF16)
            column = jnp.sum(total, axis=0, keepdims=True)
        sums.append((column_ref, column))
        lows = outs[5:] if gated else outs[4:]
        if perms:
            for perm_ref, low_ref in zip(flats[2:], lows):
                low_ref[...] = matmul(low, perm_ref[...]).astype(BF16)
        else:
            lows[0][...] = low

        @pl.when(pl.program_id(0) == 0)
        def _():
            for ref, term in sums:
                ref[...] = term

        @pl.when(pl.program_id(0) > 0)
        def _():
            for ref, term in sums:
                ref[...] += term

    given = [hot, hot_t] + tall + flat
    specs = [by_tokens(hot), pl.BlockSpec((hot_t.shape[0], TOKENS), lambda j: (0, j))]
    specs += [by_tokens(part) for part in tall] + [whole(part) for part in flat]
    shape = jax.ShapeDtypeStruct
    image = shape(scale.shape, F32)
    outs = [shape((tokens, width), F32), image, image, shape((1, width), F32)]
    outs += [image] if gated else []
    outs += [shape((tokens, width), BF16) for _ in range(max(len(perms), 1))]
    out_specs = [by_tokens(part) if part.shape[0] == tokens else whole(part) for part in outs]
    return run(body, (tokens // TOKENS,), given, specs, outs, out_specs)


def slim_back(d_resid, token_hot, arrays, plan, perm, n_embed):
    width, wide = perm.shape[0], token_hot.shape[1]
    rows = sum(arrays[which].shape[1] // width for which, _ in plan)
    room = rows + (-rows % 16)

    def body(d_ref, hot_ref, perm_ref, *refs):
        out_ref, gains = refs[-2], refs[-1]
        gains[...] = jnp.zeros_like(gains)
        at = 0
        for which, row in plan:
            for column in range(0, arrays[which].shape[1], width):
                gains[at : at + 1, :] = refs[which][row : row + 1, column : column + width]
                at += 1
        place = lax.broadcasted_iota(jnp.int32, (room, wide), 1)
        own = lax.broadcasted_iota(jnp.int32, (room, wide), 0) + n_embed
        own = jnp.where(own < n_embed + rows, own, -1)
        total = matmul_tn(d_ref[...], hot_ref[...])
        chosen = jnp.where(place == own, 1.0, 0.0).astype(BF16)
        total = total + matmul_tn(gains[...].astype(BF16), chosen)
        out_ref[...] = matmul(perm_ref[...], total.astype(BF16)).astype(BF16)

    given = [d_resid, token_hot, perm] + list(arrays)
    outs = jax.ShapeDtypeStruct((width, wide), BF16)
    specs = [whole(value) for value in given]
    scratch = [pltpu.VMEM((room, width), F32)]
    return run(body, (1,), given, specs, outs, whole(outs), scratch)


def layout(scale_row):
    position = jnp.arange(scale_row.shape[0], dtype=jnp.int32)
    opening = scale_row == 0
    image_id = jnp.cumsum(opening.astype(jnp.int32)) - 1
    starts_at = lax.cummax(jnp.where(opening, position, 0), axis=0)
    return (image_id, position - starts_at, scale_row < LEVELS)


def adam_step(weight, moment, square, gradient, clip_factor, step_rate):
    gradient = gradient * clip_factor
    moment = BETA_ONE * moment + (1.0 - BETA_ONE) * gradient
    square = BETA_TWO * square + (1.0 - BETA_TWO) * gradient * gradient
    first_hat = moment / (1.0 - BETA_ONE**STEPS)
    second_hat = square / (1.0 - BETA_TWO**STEPS)
    weight = weight - step_rate * (first_hat / (jnp.sqrt(second_hat) + ADAM_EPS) + DECAY * weight)
    return (weight, moment, square, weight.astype(BF16))


def per_device(
    ways,
    features,
    scale_ids,
    class_ids,
    code_targets,
    token_weights,
    attn_weight,
    attn_moment,
    attn_square,
    mlp_weight,
    mlp_moment,
    mlp_square,
    ada_weight,
    ada_moment,
    ada_square,
    embed_weight,
    embed_moment,
    embed_square,
    gains_weight,
    gains_moment,
    gains_square,
    head_weight,
    head_moment,
    head_square,
):
    devices, n_vocab = ways["devices"], ways["n_vocab"]
    bits_y, bits_x, bits_z = ways["y"], ways["x"], ways["z"]
    path_one = bits_z + bits_y + bits_x
    path_two = bits_z + bits_x + bits_y
    me = lax.axis_index("dp") * n_vocab + lax.axis_index("vocab")
    rows = attn_weight.shape[0]
    width = rows * devices
    top, quarter = width // 2, width // 4
    ff_rows = FF // width
    ada_at = 7 + ff_rows
    head_at = ada_at + 8
    off_level = CLASSES + POSITIONS
    off_word = off_level + LEVELS
    length = scale_ids.shape[1]
    used = min(POSITIONS, length)
    n_gains = gains_weight.shape[0]
    n_embed = used + LEVELS + CHANNELS
    half_ff, half_qkv = FF // 2, 3 * width // 2

    def swap(value, mask):
        return swapped(value, mask, devices)

    def grown(masks, *values):
        for mask in masks:
            values = [grow(value, mask, devices) for value in values]
        return values if len(values) > 1 else values[0]

    scale_row = scale_ids[0]
    image_id, inside, counted = layout(scale_row)
    counted = counted.astype(F32)
    facts = jnp.concatenate(
        [class_ids[0], jnp.sum(counted).astype(jnp.int32)[None], jnp.zeros((119,), jnp.int32)]
    )[None]
    weighted = token_weights[0] * counted
    row_info = jnp.stack([code_targets[0].astype(F32), weighted])[None]

    embed16 = embed_weight.astype(BF16)
    slim = jnp.concatenate(
        [
            embed16[CLASSES : CLASSES + used],
            embed16[off_level : off_word + CHANNELS],
            gains_weight.astype(BF16),
        ],
        axis=0,
    )
    fill = -slim.shape[0] % 128
    slim = jnp.pad(slim, ((0, fill), (0, 0))).T
    wide = slim.shape[1]
    half_slim = wide // 2
    qkv_one = jnp.concatenate(
        [attn_weight[:, :half_qkv].astype(BF16), slim[:, :half_slim]], axis=1
    )
    qkv_two = jnp.concatenate(
        [attn_weight[:, half_qkv : 3 * width].astype(BF16), slim[:, half_slim:]], axis=1
    )
    up = jnp.concatenate(
        [
            mlp_weight[0, :, :half_ff],
            attn_weight[:, 3 * width : 3 * width + top],
            mlp_weight[0, :, half_ff:],
            attn_weight[:, 3 * width + top :],
        ],
        axis=1,
    ).astype(BF16)
    down = mlp_weight[1].astype(BF16)
    head16 = head_weight.astype(BF16)
    ada16 = ada_weight.astype(BF16)

    one_y, one_x, two_x, two_y = bits_y, bits_x, bits_x, bits_y
    slots = devices * MAXIMG
    n_x, n_y, n_z = 1 << len(bits_x), 1 << len(bits_y), 1 << len(bits_z)

    def to_two(value):
        shaped = value.reshape((2, n_x, n_y, n_z * MAXIMG) + value.shape[1:])
        return jnp.swapaxes(shaped, 1, 2).reshape(value.shape)

    def to_one(value):
        shaped = value.reshape((2, n_y, n_x, n_z * MAXIMG) + value.shape[1:])
        return jnp.swapaxes(shaped, 1, 2).reshape(value.shape)

    order = path_one + [1]
    groups = [order[at : at + 2] for at in range(0, len(order), 2)]
    parts = spread(facts, groups[0], devices)
    qkv_one, qkv_two = widen(qkv_one, bits_z[:1], devices), widen(qkv_two, bits_z[:1], devices)
    parts, qkv_one, qkv_two = tie(parts, qkv_one, qkv_two)
    parts = spread(stack(parts), groups[1], devices)
    qkv_one = widen(stack(qkv_one), bits_z[1:], devices)
    qkv_two = widen(stack(qkv_two), bits_z[1:], devices)
    perm_one, perm_one_t = hot_rows(source_rows(path_one + [1], me, rows))
    perm_two, perm_two_t = hot_rows(source_rows(path_two + [1], me, rows))
    parts, qkv_one, qkv_two, up = tie(parts, qkv_one, qkv_two, up)
    for group in groups[2:]:
        parts = spread(stack(parts), group, devices)
    qkv_one, qkv_two = widen(stack(qkv_one), one_y, devices), widen(stack(qkv_two), two_x, devices)
    parts, perm_one, perm_two, up = tie(parts, perm_one, perm_two, up)

    facts = stack(parts)
    total_count = jnp.sum(facts[:, MAXIMG]).astype(F32)
    class_hot = (
        facts[:, :MAXIMG].reshape(slots)[:, None] == jnp.arange(CLASSES, dtype=jnp.int32)[None, :]
    ).astype(BF16)
    class_vec = matmul(class_hot, embed16[:CLASSES])
    class_act = jax.nn.silu(class_vec).astype(BF16)
    cuts = (2 * width, 5 * width)
    act_two = to_two(class_act)
    act_first = class_act.reshape(2, n_x, n_y, n_z, MAXIMG, rows)
    act_first = jnp.transpose(act_first, (0, 3, 1, 2, 4, 5)).reshape(slots, rows)
    path_first = bits_y + bits_x + bits_z
    first = matmul(act_first, ada16[:, : cuts[0]]).astype(BF16)
    first = lend(first, [1], devices)
    row_info = widen(row_info, bits_x, devices)
    first, row_info = tie(first, row_info)
    for mask in reversed(bits_z):
        first = lend(added(*first), [mask], devices)
        (first,) = tie(first)
    first, qkv_one, qkv_two, up, row_info = tie(first, qkv_one, qkv_two, up, row_info)

    first = lend(added(*first), bits_x, devices)
    up = widen(up, bits_z[:1], devices)
    qkv_one, qkv_two = stack(qkv_one), stack(qkv_two)
    for mask in bits_x[:-1]:
        qkv_one = grow(qkv_one, mask, devices)
    for mask in bits_y[:-1]:
        qkv_two = grow(qkv_two, mask, devices)
    one_far, two_far = swap(qkv_one, bits_x[-1]), swap(qkv_two, bits_y[-1])
    row_info = widen(stack(row_info), [1], devices)
    first, row_info, qkv_one, qkv_two = tie(first, row_info, qkv_one, qkv_two)
    first = lend(added(*first), bits_y, devices)
    first, qkv_one, qkv_two, up = tie(first, qkv_one, qkv_two, up)
    first = added(*first, F32)
    up = widen(stack(up), bits_z[1:], devices)
    one_near_c, two_near_c = swap(qkv_one, 1), swap(qkv_two, 1)
    pos_hot = (inside[:, None] == jnp.arange(used, dtype=jnp.int32)[None, :]).astype(BF16)
    level_hot = (scale_row[:, None] == jnp.arange(LEVELS, dtype=jnp.int32)[None, :]).astype(BF16)
    token_hot = jnp.concatenate(
        [pos_hot, level_hot, features[0], jnp.zeros((length, wide - n_embed), BF16)], axis=1
    )
    image = jnp.arange(MAXIMG, dtype=jnp.int32)
    hot = (image_id[:, None] == image[None, :]).astype(BF16)
    hot_t = (image[:, None] == image_id[None, :]).astype(BF16)
    allowed = (image_id[:, None] == image_id[None, :]) & (scale_row[None, :] <= scale_row[:, None])
    mask_rows = jnp.where(allowed, 0.0, NEG_FILL).astype(F32)
    mods_rest = jnp.concatenate(
        [
            matmul(class_act, ada16[:, cuts[0] : cuts[1]]).astype(BF16),
            matmul(act_two, ada16[:, cuts[1] :]).astype(BF16),
        ],
        axis=1,
    )
    first, one_far, two_far, one_near_c, two_near_c, mods_rest, token_hot, mask_rows = tie(
        first, one_far, two_far, one_near_c, two_near_c, mods_rest, token_hot, mask_rows
    )
    row_info = jnp.swapaxes(stack(row_info), 0, 1).reshape(2, -1)

    one_far_c, two_far_c = swap(one_far, 1), swap(two_far, 1)
    mods_rest = lend(mods_rest, [1], devices)
    one_far_c, two_far_c, mods_rest, first, down, up = tie(
        one_far_c, two_far_c, mods_rest, first, down, up
    )

    half_up = half_ff + top
    up = stack(up)
    up_one, up_two = widen(up[:, :half_up], one_y, devices), widen(up[:, half_up:], two_x, devices)
    mods_rest = added(*mods_rest)
    cut = cuts[1] - cuts[0]
    mod_one = lend(mods_rest[:, :cut], bits_x, devices)
    mod_two = lend(mods_rest[:, cut:], bits_y, devices)
    down = widen(down, bits_z[:1], devices)
    blocks_one = [qkv_one, one_far, one_near_c, one_far_c]
    blocks_two = [qkv_two, two_far, two_near_c, two_far_c]
    slim = jnp.concatenate(
        [
            matmul_tn(stack([block[:, half_qkv:] for block in blocks_one]), perm_one),
            matmul_tn(stack([block[:, half_qkv:] for block in blocks_two]), perm_two),
        ],
        axis=0,
    )
    gain_rows = slim[n_embed : n_embed + n_gains]
    ada_bias = gain_rows[ada_at:head_at].reshape(1, -1)
    resid_in = matmul(token_hot, slim.astype(BF16)) + gain_rows[0]
    first = first + ada_bias[:, : cuts[0]]
    mods = [first[:, :width], first[:, width:]]
    u_one, u_two = norm_ahead(resid_in, hot, mods[0], mods[1], [perm_one_t, perm_two_t])
    w_qkv = ((blocks_one, half_qkv), (blocks_two, half_qkv))
    qkv_bias = jnp.concatenate(
        [gain_rows[1:2], jnp.zeros((1, width), F32), gain_rows[2:3]], axis=1
    )
    q_gain, k_gain = gain_rows[5:6], gain_rows[6:7]
    qkv = times_sets([u_one, u_two], w_qkv, qkv_bias)
    qkv, up_one, up_two, mod_one, mod_two, down, head16 = tie(
        qkv, up_one, up_two, mod_one, mod_two, down, head16
    )

    up_one, up_two = stack(up_one), stack(up_two)
    for mask in bits_x[:-1]:
        up_one = grow(up_one, mask, devices)
    for mask in bits_y[:-1]:
        up_two = grow(up_two, mask, devices)
    proj_one, proj_two = up_one[:, half_ff:], up_two[:, half_ff:]
    up_one, up_two = up_one[:, :half_ff], up_two[:, :half_ff]
    proj_one_far, proj_two_far = swap(proj_one, bits_x[-1]), swap(proj_two, bits_y[-1])
    mod_one = lend(added(*mod_one), bits_y, devices)
    mod_two = lend(added(*mod_two), bits_x, devices)
    head16 = widen(head16, bits_y, devices)
    mixture = attend(qkv, q_gain, k_gain, mask_rows)
    mixture, proj_one_far, proj_two_far, up_one, up_two, mod_one, mod_two, head16, down = tie(
        mixture, proj_one_far, proj_two_far, up_one, up_two, mod_one, mod_two, head16, down
    )

    up_one_far, up_two_far = swap(up_one, bits_x[-1]), swap(up_two, bits_y[-1])
    mods_rest = jnp.concatenate([added(*mod_one), added(*mod_two)], axis=1)
    mods_rest = lend(mods_rest, bits_z[-1:], devices)
    proj_one_c, proj_two_c = swap(proj_one, 1), swap(proj_two, 1)
    proj_one_fc, proj_two_fc = swap(proj_one_far, 1), swap(proj_two_far, 1)
    mix_one = matmul(mixture, perm_one_t).astype(BF16)
    mix_two = matmul(mixture, perm_two_t).astype(BF16)
    mix_one, mix_two, proj_one_c, proj_two_c, proj_one_fc, proj_two_fc, mods_rest = tie(
        mix_one, mix_two, proj_one_c, proj_two_c, proj_one_fc, proj_two_fc, mods_rest
    )
    w_proj = (
        ([proj_one, proj_one_far, proj_one_c, proj_one_fc], None),
        ([proj_two, proj_two_far, proj_two_c, proj_two_fc], None),
    )
    mods_rest = lend(added(*mods_rest), bits_z[:-1], devices)
    attn_out = times_sets([mix_one, mix_two], w_proj, gain_rows[3:4])
    attn_out, mods_rest, down = tie(attn_out, mods_rest, down)
    mods_rest = added(*mods_rest, F32) + ada_bias[:, cuts[0] :]
    mods += [mods_rest[:, at : at + width] for at in range(0, 6 * width, width)]
    up_one_c, up_two_c = swap(up_one, 1), swap(up_two, 1)
    down = widen(stack(down), bits_z[1:], devices)
    u_mid_one, u_mid_two, resid_mid = norm_ahead(
        resid_in, hot, mods[3], mods[4], [perm_one_t, perm_two_t], mods[2], attn_out
    )
    u_mid_one, u_mid_two, up_one_far, up_two_far, up_one_c, up_two_c, down = tie(
        u_mid_one, u_mid_two, up_one_far, up_two_far, up_one_c, up_two_c, down
    )

    up_one_fc, up_two_fc = swap(up_one_far, 1), swap(up_two_far, 1)
    u_mid_one, u_mid_two, up_one_fc, up_two_fc, down = tie(
        u_mid_one, u_mid_two, up_one_fc, up_two_fc, down
    )
    down = stack(down)
    down_one = widen(down[:, :half_ff], one_y, devices)
    down_two = widen(down[:, half_ff:], two_x, devices)
    head16 = widen(stack(head16), bits_z[:1], devices)
    w_up = (
        ([up_one, up_one_far, up_one_c, up_one_fc], None),
        ([up_two, up_two_far, up_two_c, up_two_fc], None),
    )
    up_bias = gain_rows[7:ada_at].reshape(1, -1)
    hidden, active = times_sets([u_mid_one, u_mid_two], w_up, up_bias, bend=True)
    active, down_one, down_two = tie(active, down_one, down_two)

    down_one, down_two = stack(down_one), stack(down_two)
    for mask in bits_x[:-1]:
        down_one = grow(down_one, mask, devices)
    for mask in bits_y[:-1]:
        down_two = grow(down_two, mask, devices)
    down_one_far, down_two_far = swap(down_one, bits_x[-1]), swap(down_two, bits_y[-1])
    down_one_c, down_two_c = swap(down_one, 1), swap(down_two, 1)
    active, down_one_far, down_two_far, down_one_c, down_two_c, head16 = tie(
        active, down_one_far, down_two_far, down_one_c, down_two_c, head16
    )

    down_one_fc, down_two_fc = swap(down_one_far, 1), swap(down_two_far, 1)
    head16 = widen(stack(head16), bits_z[1:], devices)
    active, down_one_fc, down_two_fc = tie(active, down_one_fc, down_two_fc)
    w_down = (
        ([down_one, down_one_far, down_one_c, down_one_fc], None),
        ([down_two, down_two_far, down_two_c, down_two_fc], None),
    )
    perms = [perm_one, perm_two]
    mlp_out = back_sets(active[None], w_down, perms, gain_rows[4:5], exact=True)
    head_masks = bits_y + bits_z
    perm_head, perm_head_t = hot_rows(
        source_rows(
            [mask // n_vocab for mask in head_masks], lax.axis_index("dp"), head_weight.shape[0]
        )
    )
    head_rel, resid_out = norm_ahead(
        resid_mid, hot, mods[6], mods[7], [perm_head_t], mods[5], mlp_out
    )
    head_rel, head16 = tie(head_rel, head16)
    head16 = stack(head16)

    vocab_masks = bits_x + [1]
    rows_all = grown(bits_x[:-1], head_rel)
    far = swap(rows_all, bits_x[-1])
    near_c = swap(rows_all, 1)
    code_span = head_weight.shape[1]
    code_start = lax.axis_index("vocab") * code_span
    head_bias = lax.dynamic_slice_in_dim(gain_rows[head_at:].reshape(-1), code_start, code_span)
    code = jnp.arange(code_span, dtype=jnp.int32)[None, :] + code_start

    def part_stats(part, info):
        logits = matmul(part, head16) + head_bias
        local_max = jnp.max(logits, axis=1)
        exp_sums = jnp.sum(jnp.exp(logits - local_max[:, None]), axis=1)
        is_target = (code == info[0].astype(jnp.int32)[:, None]).astype(F32)
        picked = jnp.sum(is_target * logits, axis=1)
        return logits, is_target, jnp.stack([local_max, exp_sums, picked])

    each = rows_all.shape[0]
    info_of = [row_info[:, at * each : (at + 1) * each] for at in range(4)]
    near_rows = jnp.concatenate([rows_all, near_c], axis=0)
    near_info = jnp.concatenate([info_of[0], info_of[2]], axis=1)
    far_info = jnp.concatenate([info_of[1], info_of[3]], axis=1)
    near_logits, near_target, near_stats = part_stats(near_rows, near_info)
    near_stats, far = tie(near_stats, far)
    far_rows = jnp.concatenate([far, swap(far, 1)], axis=0)
    far_logits, far_target, far_stats = part_stats(far_rows, far_info)
    places = [x ^ c for x in (0, bits_x[-1]) for c in (0, 1)]
    places = [place ^ other for place in places for other in place_masks(bits_x[:-1])]
    stats = jnp.concatenate([near_stats, far_stats], axis=1)
    group = [stats]
    for other in place_masks(vocab_masks)[1:]:
        their = jnp.split(swap(stats, other), n_vocab, axis=1)
        group.append(
            jnp.concatenate([their[places.index(place ^ other)] for place in places], axis=1)
        )
    row_max = group[0][0]
    for other in group[1:]:
        row_max = jnp.maximum(row_max, other[0])
    totals = sum(other[1] * jnp.exp(other[0] - row_max) for other in group)
    target_logit = sum(other[2] for other in group)
    log_total = row_max + jnp.log(totals)
    loss_part = jnp.sum((near_info[1] * (log_total - target_logit)[: 2 * each])[:length])
    mid = 2 * each

    def part_back(logits, is_target, info, log_total):
        coef = info[1] / total_count
        grad = coef[:, None] * (jnp.exp(logits - log_total[:, None]) - is_target)
        return grad.astype(BF16)

    d_far_logits = part_back(far_logits, far_target, far_info, log_total[mid:])
    d_near_logits = part_back(near_logits, near_target, near_info, log_total[:mid])
    d_far = matmul_nt(d_far_logits, head16).astype(BF16)
    d_near = matmul_nt(d_near_logits, head16).astype(BF16)
    to_core = jnp.concatenate([d_near[each:], d_far[each:]], axis=0)
    back = swap(to_core, 1)
    d_far, d_near = added(d_far[:each], back[each:]), added(d_near[:each], back[:each])
    rows_all = jnp.concatenate([near_rows, far_rows], axis=0)
    d_logits = jnp.concatenate([d_near_logits, d_far_logits], axis=0)
    d_far, head16 = tie(d_far, head16)
    d_head_in = added(d_near, swap(d_far, bits_x[-1]), F32)
    for mask in reversed(bits_x[:-1]):
        d_head_in = keep_half(d_head_in.astype(BF16), mask, devices, F32)
    head_far = matmul_tn(rows_all[:, top:], d_logits).astype(BF16)
    head_near = matmul_tn(rows_all[:, :top], d_logits).astype(BF16)
    bias_grad = lax.dynamic_update_slice(
        jnp.zeros((V,), F32), jnp.sum(d_logits.astype(F32), axis=0), (code_start,)
    )
    d_head_in, head_far, head_near = tie(d_head_in, head_far, head_near)

    def cross(one, two):
        return swap(one, bits_x[-1]), swap(two, bits_y[-1])

    def join(one, two, one_back, two_back):
        one, two = added(one, one_back), added(two, two_back)
        for mask in reversed(bits_y[:-1]):
            two = keep_half(two, mask, devices)
        for mask in reversed(bits_x[:-1]):
            one = keep_half(one, mask, devices)
        half = one.shape[0] // 2
        return tuple(
            jnp.concatenate([one[at : at + half], two[at : at + half]], axis=1) for at in (0, half)
        )

    def turn(one, two, one_back, two_back):
        one, one_far = halves_of(one, one_back)
        two, two_far = halves_of(two, two_back)
        for mask in reversed(bits_x[:-1]):
            whole_one = jnp.concatenate([one, one_far], axis=0)
            one, one_far = halves_of(
                whole_one[: whole_one.shape[0] // 2],
                swap(whole_one[whole_one.shape[0] // 2 :], mask),
            )
        for mask in reversed(bits_y[:-1]):
            whole_two = jnp.concatenate([two, two_far], axis=0)
            two, two_far = halves_of(
                whole_two[: whole_two.shape[0] // 2],
                swap(whole_two[whole_two.shape[0] // 2 :], mask),
            )
        return one, one_far, two, two_far

    def cross_back(one_far, two_far):
        return swap(one_far, bits_y[-1]), swap(two_far, bits_x[-1])

    perms = [perm_one, perm_two]
    ones, twos = (0, half_ff), (half_ff, FF)
    q_ones, q_twos = (0, half_qkv), (half_qkv, 3 * width)
    downs, ups = [None, None], [u_mid_one, u_mid_two]
    mixes, ins = [mix_one, mix_two], [u_one, u_two]
    ffs, projs, qkvs = [ones, twos], [(0, top), (top, width)], [q_ones, q_twos]

    active = active[None]
    head_back = swap(head_far, head_masks[-1])
    d_head_in = in_halves_outside(lambda part: matmul(part, perm_head), d_head_in)
    d_resid_out, d_shift_head, d_scale_head, down_bias, d_gate_two, *downs = norm_back(
        resid_out,
        d_head_in,
        hot,
        hot_t,
        mods[7],
        gate=mods[5],
        branch=mlp_out,
        perms=[perm_one_t, perm_two_t],
    )
    down_f = grad_sets(downs, active, ffs)
    downs, down_f = tie(downs, down_f)
    down_b = swap(down_f, 1)
    d_hid, up_bias_sum = times_sets(downs, w_down, hidden=hidden)
    d_hid, down_b = tie(d_hid, down_b)
    d_hid = d_hid[None]
    down_n1, down_f1, down_n2, down_f2 = grad_sets(downs, active, ffs, down_b)
    up_f = grad_sets(ups, d_hid, ffs)
    d_hid, down_f1, down_f2, down_n1, down_n2, up_f = tie(
        d_hid, down_f1, down_f2, down_n1, down_n2, up_f
    )
    down_x1, down_x2 = cross(down_f1, down_f2)
    up_b = swap(up_f, 1)
    d_u = back_sets(d_hid, w_up, perms)
    d_u, up_b = tie(d_u, up_b)
    up_n1, up_f1, up_n2, up_f2 = grad_sets(ups, d_hid, ffs, up_b)
    d_resid_mid, d_shift_two, d_scale_two, proj_bias, d_gate_one, d_low = norm_back(
        resid_mid, d_u, hot, hot_t, mods[4], beyond=d_resid_out, gate=mods[2], branch=attn_out
    )
    d_low, down_x1, down_x2, up_f1, up_f2, up_n1, up_n2, head_back, head_near = tie(
        d_low, down_x1, down_x2, up_f1, up_f2, up_n1, up_n2, head_back, head_near
    )
    down_n1, down_f1, down_n2, down_f2 = turn(down_n1, down_n2, down_x1, down_x2)
    head_near, head_far = halves_of(head_near, head_back)
    d_low, down_f1, down_f2, up_f1, up_f2, head_far = tie(
        d_low, down_f1, down_f2, up_f1, up_f2, head_far
    )
    down_x1, down_x2 = cross_back(down_f1, down_f2)
    up_x1, up_x2 = cross(up_f1, up_f2)
    head_back = swap(head_far, head_masks[-2])
    d_low = d_low[None]
    proj_f = grad_sets(mixes, d_low, projs)
    d_mix = back_sets(d_low, w_proj, perms, out=BF16)
    d_qkv, attn_sums = attend_back(qkv, q_gain, k_gain, mask_rows, d_mix)
    d_qkv, proj_f, down_x1, down_x2, down_n1, down_n2, up_x1, up_x2, head_back, head_near = tie(
        d_qkv, proj_f, down_x1, down_x2, down_n1, down_n2, up_x1, up_x2, head_back, head_near
    )
    up_n1, up_f1, up_n2, up_f2 = turn(up_n1, up_n2, up_x1, up_x2)
    down_near, down_far = join(down_n1, down_n2, down_x1, down_x2)
    d_qkv, up_f1, up_f2, down_far, proj_f = tie(d_qkv, up_f1, up_f2, down_far, proj_f)
    up_x1, up_x2 = cross_back(up_f1, up_f2)
    down_back = swap(down_far, bits_z[-1])
    proj_b = swap(proj_f, 1)
    qkv_f = grad_sets(ins, d_qkv, qkvs)
    d_qkv, qkv_f, proj_b = tie(d_qkv, qkv_f, proj_b)
    qkv_b = swap(qkv_f, 1)
    head_near = added(head_near, head_back)
    head_grad = lend(head_near, head_masks[:-2], devices)
    d_u = back_sets(d_qkv, w_qkv, perms)
    d_u, qkv_b, up_x1, up_x2, down_back, down_near, head_grad = tie(
        d_u, qkv_b, up_x1, up_x2, down_back, down_near, head_grad
    )
    head_grad = added(*head_grad, F32)
    down_near, down_far = halves_of(down_near, down_back)
    d_u, down_far, qkv_b, up_x1, up_x2 = tie(d_u, down_far, qkv_b, up_x1, up_x2)
    down_back = swap(down_far, bits_z[-2])

    def beside(one, two):
        return jnp.concatenate([one, two], axis=1)

    qkv_n1, qkv_f1, qkv_n2, qkv_f2 = grad_sets(ins, d_qkv, qkvs, qkv_b)
    proj_n1, proj_f1, proj_n2, proj_f2 = grad_sets(mixes, d_low, projs, proj_b)
    up_near, up_far = join(up_n1, up_n2, up_x1, up_x2)
    d_resid_in, d_shift_one, d_scale_one, word_bias, d_res16 = norm_back(
        resid_in, d_u, hot, hot_t, mods[1], beyond=d_resid_mid
    )
    d_mod = jnp.concatenate(
        [
            d_shift_one,
            d_scale_one,
            d_gate_one,
            d_shift_two,
            d_scale_two,
            d_gate_two,
            d_shift_head,
            d_scale_head,
        ],
        axis=1,
    ).astype(BF16)
    qkv_f1, qkv_f2 = beside(qkv_f1, proj_f1), beside(qkv_f2, proj_f2)
    d_mod, d_res16, up_far, qkv_f1, qkv_f2, qkv_n1, qkv_n2, proj_n1, proj_n2 = tie(
        d_mod, d_res16, up_far, qkv_f1, qkv_f2, qkv_n1, qkv_n2, proj_n1, proj_n2
    )
    qkv_x1, qkv_x2 = cross(qkv_f1, qkv_f2)
    up_back = swap(up_far, bits_z[-1])
    all_mod = widen(d_mod, bits_z, devices)
    ada_sums = jnp.sum(d_mod.astype(F32), axis=0, keepdims=True)
    arrays = [word_bias, attn_sums, proj_bias, down_bias, up_bias_sum, ada_sums, bias_grad[None]]
    plan = [(0, 0), (1, 2), (1, 3), (2, 0), (3, 0), (1, 0), (1, 1), (4, 0), (5, 0), (6, 0)]
    d_slim = slim_back(d_res16, token_hot, arrays, plan, perm_one, n_embed)
    d_slim = lend(d_slim, bits_x + [1], devices)
    qkv_n1, qkv_n2 = beside(qkv_n1, proj_n1), beside(qkv_n2, proj_n2)
    qkv_x1, qkv_x2, qkv_n1, qkv_n2, all_mod, d_slim, up_back, up_near, down_back = tie(
        qkv_x1, qkv_x2, qkv_n1, qkv_n2, all_mod, d_slim, up_back, up_near, down_back
    )
    qkv_n1, qkv_f1, qkv_n2, qkv_f2 = turn(qkv_n1, qkv_n2, qkv_x1, qkv_x2)
    up_near, up_far = halves_of(up_near, up_back)
    qkv_x1, qkv_x2 = cross_back(qkv_f1, qkv_f2)
    up_back = swap(up_far, bits_z[-2])
    all_mod = stack(all_mod)
    all_first = widen(all_mod[:, : cuts[1]], bits_y, devices)
    all_two = widen(all_mod[:, cuts[1] :], bits_x, devices)
    qkv_x1, qkv_x2, qkv_n1, qkv_n2, up_back, all_first, all_two, d_slim = tie(
        qkv_x1, qkv_x2, qkv_n1, qkv_n2, up_back, all_first, all_two, d_slim
    )
    near, far = join(qkv_n1, qkv_n2, qkv_x1, qkv_x2)
    attn_back = swap(far, bits_z[-1])
    all_two = widen(stack(all_two), bits_y, devices)
    all_first = widen(stack(all_first), bits_x, devices)
    d_slim = lend(added(*d_slim), bits_z + bits_y, devices)
    attn_back, near, all_two, all_first, d_slim = tie(attn_back, near, all_two, all_first, d_slim)
    near, far = halves_of(near, attn_back)
    attn_back = swap(far, bits_z[-2])
    all_two = grown([1], stack(all_two))
    all_first = grown([1], stack(all_first))

    def close(near, back):
        masks = bits_z[:-2]
        near = added(near, back, BF16 if masks else F32)
        return keep_all(near, masks, devices)

    attn_rows, up_rows, down_rows = (
        close(near, attn_back),
        close(up_near, up_back),
        close(down_near, down_back),
    )
    slim_grad = added(*d_slim, F32).T
    half_attn = half_qkv + top
    attn_grad = jnp.concatenate(
        [
            attn_rows[:, :half_qkv],
            attn_rows[:, half_attn : half_attn + half_qkv],
            attn_rows[:, half_qkv:half_attn],
            attn_rows[:, half_attn + half_qkv :],
        ],
        axis=1,
    )
    mlp_grad = jnp.stack([up_rows, down_rows])
    ada_grad = jnp.concatenate([matmul_tn(class_act, all_first), matmul_tn(act_two, all_two)], axis=1)
    d_class_act = matmul_nt(all_first, ada16[:, : cuts[1]]) + to_one(
        matmul_nt(all_two, ada16[:, cuts[1] :])
    )
    _, silu_back = jax.vjp(jax.nn.silu, class_vec)
    d_class = precise_tn(class_hot.astype(F32), silu_back(d_class_act)[0])
    embed_grad = jnp.concatenate(
        [
            d_class,
            slim_grad[:used],
            jnp.zeros((POSITIONS - used, rows), F32),
            slim_grad[used:n_embed],
        ],
        axis=0,
    )
    gains_grad = slim_grad[n_embed : n_embed + n_gains]

    gradients = (attn_grad, mlp_grad, ada_grad, embed_grad, gains_grad, head_grad)
    squares_local = jnp.zeros((), F32)
    for gradient in gradients:
        squares_local = squares_local + jnp.sum(gradient * gradient)
    sums = sum_all(
        jnp.stack([squares_local, loss_part])[None], [1] + bits_x + bits_y + bits_z, devices
    )
    total_sq, loss_sum = sums[0, 0], sums[0, 1]
    grad_norm = jnp.sqrt(total_sq)
    clip_factor = jnp.minimum(1.0, CLIP_NORM / (grad_norm + 1e-06))
    masters = (attn_weight, mlp_weight, ada_weight, embed_weight, gains_weight, head_weight)
    moments = (attn_moment, mlp_moment, ada_moment, embed_moment, gains_moment, head_moment)
    squares = (attn_square, mlp_square, ada_square, embed_square, gains_square, head_square)
    updates = []
    for number in range(6):
        updates.extend(
            adam_step(
                masters[number],
                moments[number],
                squares[number],
                gradients[number],
                clip_factor,
                RATES[number],
            )
        )
    return tuple(updates) + (grad_norm, loss_sum, total_count)


def solution(mesh):
    n_dp, n_vocab = mesh.shape["dp"], mesh.shape["vocab"]
    n_z = 1 << (n_dp.bit_length() // 2)
    devices = n_dp * n_vocab

    def bits(least, top):
        found = []
        while least < top:
            found, least = [least] + found, least * 2
        return found

    ways = {"devices": devices, "n_vocab": n_vocab}
    ways["x"] = bits(2, n_vocab)
    ways["y"] = bits(n_vocab, devices // n_z)
    ways["z"] = bits(devices // n_z, devices)
    every = ("dp", "vocab")
    by_row = P(every, None)
    by_mid = P(None, every, None)
    by_column = P(None, every)
    head = P("dp", "vocab")
    placed = (P(every, None, None), by_row, by_row, by_row, by_row)
    for spec in (by_row, by_mid, by_row, by_column, by_column, head):
        placed = placed + (spec,) * 3
    given = ()
    for spec in (by_row, by_mid, by_row, by_column, by_column, head):
        given = given + (spec,) * 4

    def step(*arrays):
        return per_device(ways, *arrays)

    return jax.shard_map(
        step, mesh=mesh, in_specs=placed, out_specs=given + (P(), P(), P()), check_vma=False
    )
```

```python
import jax
import jax.numpy as jnp
from jax import lax
from jax.experimental import pallas as pl
from jax.experimental.pallas import tpu as pltpu
from jax.sharding import PartitionSpec as P

HEADS = 16
HEAD_DIM = 64
FF = 4096
V = 4096
CHANNELS = 32
CLASSES = 1001
POSITIONS = 680
LEVELS = 10
MAXIMG = 8
STEPS = 10


EPS_NORM = 1e-06
BETA_ONE = 0.9
BETA_TWO = 0.95
ADAM_EPS = 1e-08
DECAY = 0.05
CLIP_NORM = 0.001
RATES = (0.03, 0.03, 0.03, 0.15, 0.4, 0.03)
NEG_FILL = -1e30
BF16 = jnp.bfloat16
F32 = jnp.float32
SPANS = (1024, 512)
TOKENS = 128
PAIR = 2 * HEAD_DIM


def matmul(left, right):
    return jnp.dot(left, right, preferred_element_type=F32)


def matmul_tn(left, right):
    return lax.dot_general(left, right, (((0,), (0,)), ((), ())), preferred_element_type=F32)


def matmul_nt(left, right):
    return lax.dot_general(left, right, (((1,), (1,)), ((), ())), preferred_element_type=F32)


def precise_tn(left, right):
    return lax.dot_general(left, right, (((0,), (0,)), ((), ())), precision=lax.Precision.HIGHEST)


def pick(hot, values):
    return in_halves(lambda part: matmul(hot, part), values)


def in_halves(times, values):
    upper = values.astype(BF16)
    return times(upper) + times((values - upper.astype(F32)).astype(BF16))


def in_halves_outside(times, values):
    upper = lax.reduce_precision(values, 8, 7)
    return times(upper.astype(BF16)) + times((values - upper).astype(BF16))


def swapped(value, mask, devices):
    return lax.ppermute(value, ("dp", "vocab"), [(i, i ^ mask) for i in range(devices)])


def tie(*values):
    return lax.optimization_barrier(values)


def grow(value, mask, devices):
    return jnp.concatenate([value, swapped(value, mask, devices)], axis=0)


def spread(value, masks, devices):
    if len(masks) == 2:
        masks = masks + [masks[0] ^ masks[1]]
    return [value] + [swapped(value, mask, devices) for mask in masks]


def stack(parts):
    return jnp.concatenate(parts, axis=0)


def widen(value, masks, devices):
    for mask in masks[:-1]:
        value = grow(value, mask, devices)
    return [value, swapped(value, masks[-1], devices)]


def added(mine, theirs, out=BF16):
    return (mine.astype(F32) + theirs.astype(F32)).astype(out)


def keep_half(value, mask, devices, out=BF16):
    half = value.shape[0] // 2
    return added(value[:half], swapped(value[half:].astype(BF16), mask, devices), out)


def lend(value, masks, devices):
    for mask in reversed(masks[1:]):
        value = keep_half(value, mask, devices)
    half = value.shape[0] // 2
    return [value[:half], swapped(value[half:].astype(BF16), masks[0], devices)]


def keep_all(value, masks, devices):
    for mask in reversed(masks):
        value = keep_half(value, mask, devices, F32 if mask == masks[0] else BF16)
    return value


def halves_of(mine, back, out=BF16):
    half = mine.shape[0] // 2
    return (added(mine[:half], back[:half], out), added(mine[half:], back[half:], out))


def sum_all(value, bits, devices):
    for at in range(0, len(bits), 3):
        masks = place_masks(bits[at : at + 3])[1:]
        value = value + sum(swapped(value, mask, devices) for mask in masks)
    return value


def place_masks(masks):
    places = [0]
    for mask in masks:
        places = places + [place ^ mask for place in places]
    return places


def source_rows(masks, me, rows):
    differ = jnp.repeat(jnp.array(place_masks(masks), jnp.int32), rows)
    row = jnp.tile(jnp.arange(rows, dtype=jnp.int32), 1 << len(masks))
    return (differ ^ me) * rows + row


def hot_rows(source):
    place = jnp.arange(source.shape[0], dtype=jnp.int32)
    return (
        (source[:, None] == place[None, :]).astype(BF16),
        (place[:, None] == source[None, :]).astype(BF16),
    )


def run(body, grid, given, specs, outs, out_specs, scratch=()):
    return pl.pallas_call(
        body,
        grid=grid,
        in_specs=specs,
        out_shape=outs,
        out_specs=out_specs,
        scratch_shapes=scratch,
        compiler_params=pltpu.CompilerParams(vmem_limit_bytes=48 << 20),
        cost_estimate=pl.CostEstimate(flops=1000, bytes_accessed=1000, transcendentals=0),
    )(*given)


def whole(value):
    return pl.BlockSpec(value.shape, lambda j: (0,) * value.ndim)


def span_of(*sizes):
    return [span for span in SPANS if all(size % span == 0 for size in sizes)][0]


def columns_of(sets):
    return [blocks[0].shape[1] if used is None else used[1] - used[0] for blocks, used in sets]


def starts_of(sets):
    return [0 if used is None else used[0] for _, used in sets]


def two_sets(sets, first, span):
    one, two = [start // span for start in starts_of(sets)]
    specs = [
        pl.BlockSpec((block.shape[0], span), lambda j: (0, one + jnp.minimum(j, first - 1)))
        for block in sets[0][0]
    ]
    specs += [
        pl.BlockSpec((block.shape[0], span), lambda j: (0, two + jnp.maximum(j - first, 0)))
        for block in sets[1][0]
    ]
    return specs


def gelu_parts(value):
    inner = 0.7978845608028654 * (value + 0.044715 * (value * value * value))
    bend = jnp.tanh(inner)
    return bend


def gelu(value):
    return 0.5 * value * (1.0 + gelu_parts(value))


def gelu_slope(value):
    bend = gelu_parts(value)
    rise = 0.7978845608028654 * (1.0 + 3.0 * 0.044715 * value * value)
    return 0.5 * (1.0 + bend) + 0.5 * value * (1.0 - bend * bend) * rise


def times_sets(left, sets, bias=None, hidden=None, bend=False):
    tokens = left[0].shape[0]
    columns = columns_of(sets)
    span = span_of(*columns, *starts_of(sets))
    first, steps = columns[0] // span, sum(columns) // span
    specs = two_sets(sets, first, span)
    count = len(sets[0][0])
    extra = [value for value in (bias, hidden) if value is not None]
    column = lambda j: (0, j)
    extra_specs = [pl.BlockSpec((value.shape[0], span), column) for value in extra]

    def body(one_ref, two_ref, *refs):
        extras, blocks = refs[: len(extra)], refs[len(extra) : len(extra) + 2 * count]
        outs = refs[len(extra) + 2 * count :]

        def part(u_ref, blocks):
            total, at = None, 0
            for block in blocks:
                rows = block.shape[0]
                term = matmul(u_ref[:, at : at + rows], block[...])
                total = term if total is None else total + term
                at += rows
            if bias is not None:
                total = total + extras[0][...]
            if hidden is not None:
                slope = gelu_slope(extras[-1][...])
                low = (total * slope).astype(BF16)
                outs[0][...] = low
                outs[1][...] = jnp.sum(low.astype(F32), axis=0, keepdims=True)
            else:
                outs[0][...] = total
                if bend:
                    outs[1][...] = gelu(total).astype(BF16)

        pl.when(pl.program_id(0) < first)(lambda: part(one_ref, blocks[:count]))
        pl.when(pl.program_id(0) >= first)(lambda: part(two_ref, blocks[count:]))

    wide = steps * span
    shape = jax.ShapeDtypeStruct
    outs, out_specs = [shape((tokens, wide), F32)], [pl.BlockSpec((tokens, span), column)]
    if hidden is not None:
        outs = [shape((tokens, wide), BF16), shape((1, wide), F32)]
        out_specs.append(pl.BlockSpec((1, span), column))
    elif bend:
        outs.append(shape((tokens, wide), BF16))
        out_specs.append(pl.BlockSpec((tokens, span), column))
    given = list(left) + extra + list(sets[0][0]) + list(sets[1][0])
    specs = [whole(value) for value in left] + extra_specs + specs
    found = run(body, (steps,), given, specs, outs, out_specs)
    return found if len(outs) > 1 else found[0]


def span_spec(value, span):
    each = value.shape[2] // span
    return pl.BlockSpec((1, value.shape[1], span), lambda j: (j // each, 0, j % each))


def back_sets(right, sets, perms, bias=None, exact=False, out=F32):
    tokens = right.shape[1]
    columns = columns_of(sets)
    span = span_of(right.shape[2], *columns, *starts_of(sets))
    first, steps = columns[0] // span, sum(columns) // span
    specs = two_sets(sets, first, span)
    count = len(sets[0][0])
    width = perms[0].shape[0]
    extra = [] if bias is None else [bias]

    def body(right_ref, one_ref, two_ref, *refs):
        extras, blocks = refs[: len(extra)], refs[len(extra) : len(extra) + 2 * count]
        out_ref, one_sum, two_sum = refs[len(extra) + 2 * count :]
        step = pl.program_id(0)

        def part(sums, blocks, start):
            terms = [matmul_nt(right_ref[0], block[...]) for block in blocks]
            term = jnp.concatenate(terms, axis=1)

            @pl.when(step == start)
            def _():
                sums[...] = term

            @pl.when(step > start)
            def _():
                sums[...] += term

        pl.when(step < first)(lambda: part(one_sum, blocks[:count], 0))
        pl.when(step >= first)(lambda: part(two_sum, blocks[count:], first))

        @pl.when(step == steps - 1)
        def _():
            total = None
            for sums, perm in ((one_sum, one_ref), (two_sum, two_ref)):
                if exact:
                    term = in_halves(lambda part: matmul(part, perm[...]), sums[...])
                else:
                    term = matmul(sums[...].astype(BF16), perm[...])
                total = term if total is None else total + term
            if bias is not None:
                total = total + extras[0][...]
            out_ref[...] = total.astype(out)

    given = [right] + list(perms) + extra + list(sets[0][0]) + list(sets[1][0])
    specs = [span_spec(right, span)] + [whole(value) for value in list(perms) + extra] + specs
    outs = jax.ShapeDtypeStruct((tokens, width), out)
    scratch = [pltpu.VMEM((tokens, width), F32)] * 2
    return run(body, (steps,), given, specs, outs, whole(outs), scratch)


def grad_sets(left, right, columns, back=None):
    tokens, width = left[0].shape
    parts = 2 if back is not None else 1
    half = width // 2
    count = half // parts
    wide = [stop - start for start, stop in columns]
    span = span_of(right.shape[2], *wide, *[start for start, _ in columns])
    each = right.shape[2] // span
    first, steps = wide[0] // span, sum(wide) // span
    at = [start // span for start, _ in columns]

    def place(j):
        block = jnp.where(j < first, j + at[0], j - first + at[1])
        return (block // each, 0, block % each)

    def body(one_ref, two_ref, right_ref, *refs):
        def part(left_ref, outs):
            total = matmul_tn(left_ref[...], right_ref[0])
            if back is not None:
                total = total + refs[0][...].astype(F32)
            for which, out in enumerate(outs):
                out[...] = total[which * count : (which + 1) * count].astype(BF16)

        step = pl.program_id(0)
        if back is None:
            pl.when(step < first)(lambda: part(one_ref, refs))
            pl.when(step >= first)(lambda: part(two_ref, refs))
        else:
            pl.when(step < first)(lambda: part(one_ref, refs[1:3]))
            pl.when(step >= first)(lambda: part(two_ref, refs[3:]))

    side = 0 if back is not None else 1
    given = list(left) + [right]
    specs = [pl.BlockSpec((tokens, half), lambda j: (0, side)) for _ in left]
    specs.append(pl.BlockSpec((1, tokens, span), place))
    own = pl.BlockSpec((half, span), lambda j: (0, j))
    if back is None:
        outs = jax.ShapeDtypeStruct((half, sum(wide)), BF16)
        return run(body, (steps,), given, specs, outs, own)
    outs, out_specs = [], []
    indices = (lambda j: (0, jnp.minimum(j, first - 1)), lambda j: (0, jnp.maximum(j - first, 0)))
    for size, index in zip(wide, indices):
        outs += [jax.ShapeDtypeStruct((count, size), BF16)] * 2
        out_specs += [pl.BlockSpec((count, span), index)] * 2
    return run(body, (steps,), given + [back], specs + [own], outs, out_specs)


def head_scale(value, left_half):
    square = value * value
    one = jnp.sum(jnp.where(left_half, square, 0.0), axis=1, keepdims=True)
    two = jnp.sum(jnp.where(left_half, 0.0, square), axis=1, keepdims=True)
    return jnp.where(
        left_half,
        lax.rsqrt(one * (1.0 / HEAD_DIM) + EPS_NORM),
        lax.rsqrt(two * (1.0 / HEAD_DIM) + EPS_NORM),
    )


def soft_rows(q_norm, k_norm, mask):
    scores = matmul_nt(q_norm, k_norm) * HEAD_DIM ** (-0.5) + mask
    terms = jnp.exp(scores - jnp.max(scores, axis=1, keepdims=True))
    return terms * (1.0 / jnp.sum(terms, axis=1, keepdims=True))


def pair_specs(tokens):
    pairs = HEADS // 2
    return [
        pl.BlockSpec((tokens, PAIR), lambda j: (0, j)),
        pl.BlockSpec((tokens, PAIR), lambda j: (0, pairs + j)),
        pl.BlockSpec((tokens, PAIR), lambda j: (0, 2 * pairs + j)),
        pl.BlockSpec((1, PAIR), lambda j: (0, j)),
        pl.BlockSpec((1, PAIR), lambda j: (0, j)),
        pl.BlockSpec((tokens, tokens), lambda j: (0, 0)),
    ]


def attend(qkv, q_gain, k_gain, mask):
    tokens, width = qkv.shape[0], qkv.shape[1] // 3

    def body(q_ref, k_ref, v_ref, qg_ref, kg_ref, mask_ref, out_ref):
        left_half = lax.broadcasted_iota(jnp.int32, (1, PAIR), 1) < HEAD_DIM
        query, key = q_ref[...], k_ref[...]
        q_norm = (query * head_scale(query, left_half) * qg_ref[...]).astype(BF16)
        k_norm = (key * head_scale(key, left_half) * kg_ref[...]).astype(BF16)
        v_low = v_ref[...].astype(BF16)
        zero = jnp.zeros_like(q_norm)
        mixed = []
        for one in (jnp.where(left_half, q_norm, zero), jnp.where(left_half, zero, q_norm)):
            probs = soft_rows(one, k_norm, mask_ref[...])
            mixed.append(matmul(probs.astype(BF16), v_low))
        out_ref[...] = jnp.where(left_half, mixed[0], mixed[1]).astype(BF16)

    outs = jax.ShapeDtypeStruct((tokens, width), BF16)
    spec = pl.BlockSpec((tokens, PAIR), lambda j: (0, j))
    given = [qkv, qkv, qkv, q_gain, k_gain, mask]
    return run(body, (HEADS // 2,), given, pair_specs(tokens), outs, spec)


def attend_back(qkv, q_gain, k_gain, mask, d_mix):
    tokens, width = qkv.shape[0], qkv.shape[1] // 3

    def body(q_ref, k_ref, v_ref, qg_ref, kg_ref, mask_ref, dm_ref, out_ref, sums_ref):
        left_half = lax.broadcasted_iota(jnp.int32, (1, PAIR), 1) < HEAD_DIM
        query, key = q_ref[...], k_ref[...]
        q_scale, k_scale = head_scale(query, left_half), head_scale(key, left_half)
        q_norm = (query * q_scale * qg_ref[...]).astype(BF16)
        k_norm = (key * k_scale * kg_ref[...]).astype(BF16)
        v_low, d_mix = v_ref[...].astype(BF16), dm_ref[...]
        zero = jnp.zeros_like(q_norm)
        found = []
        for side in range(2):
            own = (lambda v: jnp.where(left_half, v, zero)) if side == 0 else (
                lambda v: jnp.where(left_half, zero, v)
            )
            probs = soft_rows(own(q_norm), k_norm, mask_ref[...])
            d_values = matmul_tn(probs.astype(BF16), d_mix)
            d_probs = matmul_nt(own(d_mix), v_low)
            inner = jnp.sum(d_probs * probs, axis=1, keepdims=True)
            d_scores = (probs * (d_probs - inner)).astype(BF16)
            found.append((matmul(d_scores, k_norm), matmul_tn(d_scores, q_norm), d_values))
        d_qn, d_kn, d_values = (jnp.where(left_half, one, two) for one, two in zip(*found))
        sums = []
        for at, value, scale, gain, d_norm in (
            (0, query, q_scale, qg_ref[...], d_qn * HEAD_DIM ** (-0.5)),
            (1, key, k_scale, kg_ref[...], d_kn * HEAD_DIM ** (-0.5)),
        ):
            product = d_norm * value
            sums.append(jnp.sum(product * scale, axis=0, keepdims=True))
            product = product * gain
            one = jnp.sum(jnp.where(left_half, product, 0.0), axis=1, keepdims=True)
            two = jnp.sum(jnp.where(left_half, 0.0, product), axis=1, keepdims=True)
            mean = jnp.where(left_half, one, two) * (1.0 / HEAD_DIM)
            d_value = scale * (gain * d_norm - value * (scale * scale) * mean)
            out_ref[at] = d_value.astype(BF16)
        out_ref[2] = d_values.astype(BF16)
        sums.append(jnp.sum(out_ref[0].astype(F32), axis=0, keepdims=True))
        sums.append(jnp.sum(out_ref[2].astype(F32), axis=0, keepdims=True))
        sums_ref[...] = jnp.concatenate(sums + [jnp.zeros((4, PAIR), F32)], axis=0)

    outs = [
        jax.ShapeDtypeStruct((3, tokens, width), BF16),
        jax.ShapeDtypeStruct((8, width), F32),
    ]
    out_specs = [
        pl.BlockSpec((3, tokens, PAIR), lambda j: (0, 0, j)),
        pl.BlockSpec((8, PAIR), lambda j: (0, j)),
    ]
    given = [qkv, qkv, qkv, q_gain, k_gain, mask, d_mix]
    specs = pair_specs(tokens) + [pl.BlockSpec((tokens, PAIR), lambda j: (0, j))]
    return run(body, (HEADS // 2,), given, specs, outs, out_specs)


def row_stats(value):
    center = value - jnp.mean(value, axis=1, keepdims=True)
    return center, lax.rsqrt(jnp.mean(center * center, axis=1, keepdims=True) + EPS_NORM)


def by_tokens(value):
    return pl.BlockSpec((TOKENS, value.shape[1]), lambda j: (j, 0))


def norm_ahead(value, hot, shift, scale, perms, gate=None, branch=None):
    tokens, width = value.shape
    extra = [] if gate is None else [gate, branch]

    def body(value_ref, hot_ref, shift_ref, scale_ref, *refs):
        total = value_ref[...]
        outs = refs[len(extra) + len(perms) :]
        if gate is not None:
            total = total + pick(hot_ref[...], refs[0][...]) * refs[1][...]
            outs[-1][...] = total
        center, inverse = row_stats(total)
        scales = 1.0 + pick(hot_ref[...], scale_ref[...])
        normed = center * inverse * scales + pick(hot_ref[...], shift_ref[...])
        normed = normed.astype(BF16)
        for perm_ref, out_ref in zip(refs[len(extra) : len(extra) + len(perms)], outs):
            out_ref[...] = matmul(normed, perm_ref[...]).astype(BF16)

    given = [value, hot, shift, scale] + extra + list(perms)
    specs = [by_tokens(value), by_tokens(hot), whole(shift), whole(scale)]
    specs += [whole(gate), by_tokens(branch)] if extra else []
    specs += [whole(perm) for perm in perms]
    outs = [jax.ShapeDtypeStruct((tokens, width), BF16) for _ in perms]
    outs += [jax.ShapeDtypeStruct((tokens, width), F32)] if extra else []
    out_specs = [by_tokens(value) for _ in outs]
    return run(body, (tokens // TOKENS,), given, specs, outs, out_specs)


def norm_back(value, d_out, hot, hot_t, scale, beyond=None, gate=None, branch=None, perms=()):
    tokens, width = value.shape
    gated = gate is not None
    tall = [value, d_out] + ([] if beyond is None else [beyond]) + ([branch] if gated else [])
    flat = [scale] + ([gate] if gated else []) + list(perms)

    def body(hot_ref, hot_t_ref, *refs):
        talls, flats = refs[: len(tall)], refs[len(tall) : len(tall) + len(flat)]
        outs = refs[len(tall) + len(flat) :]
        total_ref, shift_ref, scale_ref, column_ref = outs[:4]
        d_out = talls[1][...]
        center, inverse = row_stats(talls[0][...])
        normed = center * inverse
        d_norm = d_out * (1.0 + pick(hot_ref[...], flats[0][...]))
        mean = jnp.mean(d_norm, axis=1, keepdims=True)
        along = jnp.mean(d_norm * normed, axis=1, keepdims=True)
        total = (d_norm - mean - normed * along) * inverse
        if beyond is not None:
            total = total + talls[2][...]
        total_ref[...] = total
        sums = [
            (shift_ref, pick(hot_t_ref[...], d_out)),
            (scale_ref, pick(hot_t_ref[...], d_out * normed)),
        ]
        if gated:
            sums.append((outs[4], pick(hot_t_ref[...], total * talls[-1][...])))
            low = (pick(hot_ref[...], flats[1][...]) * total).astype(BF16)
            column = jnp.sum(low.astype(F32), axis=0, keepdims=True)
        else:
            low = total.astype(BF16)
            column = jnp.sum(total, axis=0, keepdims=True)
        sums.append((column_ref, column))
        lows = outs[5:] if gated else outs[4:]
        if perms:
            for perm_ref, low_ref in zip(flats[2:], lows):
                low_ref[...] = matmul(low, perm_ref[...]).astype(BF16)
        else:
            lows[0][...] = low

        @pl.when(pl.program_id(0) == 0)
        def _():
            for ref, term in sums:
                ref[...] = term

        @pl.when(pl.program_id(0) > 0)
        def _():
            for ref, term in sums:
                ref[...] += term

    given = [hot, hot_t] + tall + flat
    specs = [by_tokens(hot), pl.BlockSpec((hot_t.shape[0], TOKENS), lambda j: (0, j))]
    specs += [by_tokens(part) for part in tall] + [whole(part) for part in flat]
    shape = jax.ShapeDtypeStruct
    image = shape(scale.shape, F32)
    outs = [shape((tokens, width), F32), image, image, shape((1, width), F32)]
    outs += [image] if gated else []
    outs += [shape((tokens, width), BF16) for _ in range(max(len(perms), 1))]
    out_specs = [by_tokens(part) if part.shape[0] == tokens else whole(part) for part in outs]
    return run(body, (tokens // TOKENS,), given, specs, outs, out_specs)


def slim_back(d_resid, token_hot, arrays, plan, perms, n_embed):
    width, wide = perms[0].shape[0], token_hot.shape[1]
    half = wide // 2
    rows = sum(arrays[which].shape[1] // width for which, _ in plan)
    room = rows + (-rows % 16)

    def body(d_ref, hot_ref, one_ref, two_ref, *refs):
        out_ref, gains = refs[-2], refs[-1]
        gains[...] = jnp.zeros_like(gains)
        at = 0
        for which, row in plan:
            for column in range(0, arrays[which].shape[1], width):
                gains[at : at + 1, :] = refs[which][row : row + 1, column : column + width]
                at += 1
        place = lax.broadcasted_iota(jnp.int32, (room, wide), 1)
        own = lax.broadcasted_iota(jnp.int32, (room, wide), 0) + n_embed
        own = jnp.where(own < n_embed + rows, own, -1)
        total = matmul_tn(d_ref[...], hot_ref[...])
        chosen = jnp.where(place == own, 1.0, 0.0).astype(BF16)
        total = total + matmul_tn(gains[...].astype(BF16), chosen)
        low = total.astype(BF16)
        out_ref[:, :half] = matmul(one_ref[...], low[:, :half]).astype(BF16)
        out_ref[:, half:] = matmul(two_ref[...], low[:, half:]).astype(BF16)

    given = [d_resid, token_hot] + list(perms) + list(arrays)
    outs = jax.ShapeDtypeStruct((width, wide), BF16)
    specs = [whole(value) for value in given]
    scratch = [pltpu.VMEM((room, width), F32)]
    return run(body, (1,), given, specs, outs, whole(outs), scratch)


def layout(scale_row):
    position = jnp.arange(scale_row.shape[0], dtype=jnp.int32)
    opening = scale_row == 0
    image_id = jnp.cumsum(opening.astype(jnp.int32)) - 1
    starts_at = lax.cummax(jnp.where(opening, position, 0), axis=0)
    return (image_id, position - starts_at, scale_row < LEVELS)


def adam_step(weight, moment, square, gradient, clip_factor, step_rate):
    gradient = gradient * clip_factor
    moment = BETA_ONE * moment + (1.0 - BETA_ONE) * gradient
    square = BETA_TWO * square + (1.0 - BETA_TWO) * gradient * gradient
    first_hat = moment / (1.0 - BETA_ONE**STEPS)
    second_hat = square / (1.0 - BETA_TWO**STEPS)
    weight = weight - step_rate * (first_hat / (jnp.sqrt(second_hat) + ADAM_EPS) + DECAY * weight)
    return (weight, moment, square, weight.astype(BF16))


def per_device(
    ways,
    features,
    scale_ids,
    class_ids,
    code_targets,
    token_weights,
    attn_weight,
    attn_moment,
    attn_square,
    mlp_weight,
    mlp_moment,
    mlp_square,
    ada_weight,
    ada_moment,
    ada_square,
    embed_weight,
    embed_moment,
    embed_square,
    gains_weight,
    gains_moment,
    gains_square,
    head_weight,
    head_moment,
    head_square,
):
    devices, n_vocab = ways["devices"], ways["n_vocab"]
    bits_y, bits_x, bits_z = ways["y"], ways["x"], ways["z"]
    path_one = bits_z + bits_y + bits_x
    path_two = bits_z + bits_x + bits_y
    me = lax.axis_index("dp") * n_vocab + lax.axis_index("vocab")
    rows = attn_weight.shape[0]
    width = rows * devices
    top, quarter = width // 2, width // 4
    ff_rows = FF // width
    ada_at = 7 + ff_rows
    head_at = ada_at + 8
    off_level = CLASSES + POSITIONS
    off_word = off_level + LEVELS
    length = scale_ids.shape[1]
    used = min(POSITIONS, length)
    n_gains = gains_weight.shape[0]
    n_embed = used + LEVELS + CHANNELS
    half_ff, half_qkv = FF // 2, 3 * width // 2

    def swap(value, mask):
        return swapped(value, mask, devices)

    def grown(masks, *values):
        for mask in masks:
            values = [grow(value, mask, devices) for value in values]
        return values if len(values) > 1 else values[0]

    scale_row = scale_ids[0]
    image_id, inside, counted = layout(scale_row)
    counted = counted.astype(F32)
    facts = jnp.concatenate(
        [class_ids[0], jnp.sum(counted).astype(jnp.int32)[None], jnp.zeros((119,), jnp.int32)]
    )[None]
    weighted = token_weights[0] * counted
    row_info = jnp.stack([code_targets[0].astype(F32), weighted])[None]

    embed16 = embed_weight.astype(BF16)
    slim = jnp.concatenate(
        [
            embed16[CLASSES : CLASSES + used],
            embed16[off_level : off_word + CHANNELS],
            gains_weight.astype(BF16),
        ],
        axis=0,
    )
    fill = -slim.shape[0] % 128
    slim = jnp.pad(slim, ((0, fill), (0, 0))).T
    wide = slim.shape[1]
    half_slim = wide // 2
    qkv_one = jnp.concatenate(
        [attn_weight[:, :half_qkv].astype(BF16), slim[:, :half_slim]], axis=1
    )
    qkv_two = jnp.concatenate(
        [attn_weight[:, half_qkv : 3 * width].astype(BF16), slim[:, half_slim:]], axis=1
    )
    up = jnp.concatenate(
        [
            mlp_weight[0, :, :half_ff],
            attn_weight[:, 3 * width : 3 * width + top],
            mlp_weight[0, :, half_ff:],
            attn_weight[:, 3 * width + top :],
        ],
        axis=1,
    ).astype(BF16)
    down = mlp_weight[1].astype(BF16)
    head16 = head_weight.astype(BF16)
    ada16 = ada_weight.astype(BF16)

    one_y, one_x, two_x, two_y = bits_y, bits_x, bits_x, bits_y
    slots = devices * MAXIMG
    n_x, n_y, n_z = 1 << len(bits_x), 1 << len(bits_y), 1 << len(bits_z)

    def to_two(value):
        shaped = value.reshape((2, n_x, n_y, n_z * MAXIMG) + value.shape[1:])
        return jnp.swapaxes(shaped, 1, 2).reshape(value.shape)

    def to_one(value):
        shaped = value.reshape((2, n_y, n_x, n_z * MAXIMG) + value.shape[1:])
        return jnp.swapaxes(shaped, 1, 2).reshape(value.shape)

    order = path_one + [1]
    groups = [order[at : at + 2] for at in range(0, len(order), 2)]
    parts = spread(facts, groups[0], devices)
    qkv_one, qkv_two = widen(qkv_one, bits_z[:1], devices), widen(qkv_two, bits_z[:1], devices)
    parts, qkv_one, qkv_two = tie(parts, qkv_one, qkv_two)
    parts = spread(stack(parts), groups[1], devices)
    qkv_one = widen(stack(qkv_one), bits_z[1:], devices)
    qkv_two = widen(stack(qkv_two), bits_z[1:], devices)
    parts, qkv_one, qkv_two, up, head16 = tie(parts, qkv_one, qkv_two, up, head16)
    for group in groups[2:]:
        parts = spread(stack(parts), group, devices)
    qkv_one, qkv_two = widen(stack(qkv_one), one_y, devices), widen(stack(qkv_two), two_x, devices)
    head16 = widen(head16, bits_y, devices)
    parts, up, me = tie(parts, up, me)

    facts = stack(parts)
    total_count = jnp.sum(facts[:, MAXIMG]).astype(F32)
    class_hot = (
        facts[:, :MAXIMG].reshape(slots)[:, None] == jnp.arange(CLASSES, dtype=jnp.int32)[None, :]
    ).astype(BF16)
    class_vec = matmul(class_hot, embed16[:CLASSES])
    class_act = jax.nn.silu(class_vec).astype(BF16)
    cuts = (2 * width, 5 * width)
    act_two = to_two(class_act)
    act_first = class_act.reshape(2, n_x, n_y, n_z, MAXIMG, rows)
    act_first = jnp.transpose(act_first, (0, 3, 1, 2, 4, 5)).reshape(slots, rows)
    path_first = bits_y + bits_x + bits_z
    first = matmul(act_first, ada16[:, : cuts[0]]).astype(BF16)
    first = lend(first, [1], devices)
    row_info = widen(row_info, bits_x, devices)
    first, row_info, me, head16 = tie(first, row_info, me, head16)
    perm_one, perm_one_t = hot_rows(source_rows(path_one + [1], me, rows))
    perm_two, perm_two_t = hot_rows(source_rows(path_two + [1], me, rows))
    for mask in reversed(bits_z):
        first = lend(added(*first), [mask], devices)
        (first,) = tie(first)
    first, qkv_one, qkv_two, up, row_info = tie(first, qkv_one, qkv_two, up, row_info)

    first = lend(added(*first), bits_x, devices)
    up = widen(up, bits_z[:1], devices)
    qkv_one, qkv_two = stack(qkv_one), stack(qkv_two)
    for mask in bits_x[:-1]:
        qkv_one = grow(qkv_one, mask, devices)
    for mask in bits_y[:-1]:
        qkv_two = grow(qkv_two, mask, devices)
    one_far, two_far = swap(qkv_one, bits_x[-1]), swap(qkv_two, bits_y[-1])
    row_info = widen(stack(row_info), [1], devices)
    first, row_info, qkv_one, qkv_two = tie(first, row_info, qkv_one, qkv_two)
    first = lend(added(*first), bits_y, devices)
    first, qkv_one, qkv_two, up = tie(first, qkv_one, qkv_two, up)
    first = added(*first, F32)
    up = widen(stack(up), bits_z[1:], devices)
    one_near_c, two_near_c = swap(qkv_one, 1), swap(qkv_two, 1)
    pos_hot = (inside[:, None] == jnp.arange(used, dtype=jnp.int32)[None, :]).astype(BF16)
    level_hot = (scale_row[:, None] == jnp.arange(LEVELS, dtype=jnp.int32)[None, :]).astype(BF16)
    token_hot = jnp.concatenate(
        [pos_hot, level_hot, features[0], jnp.zeros((length, wide - n_embed), BF16)], axis=1
    )
    image = jnp.arange(MAXIMG, dtype=jnp.int32)
    hot = (image_id[:, None] == image[None, :]).astype(BF16)
    hot_t = (image[:, None] == image_id[None, :]).astype(BF16)
    allowed = (image_id[:, None] == image_id[None, :]) & (scale_row[None, :] <= scale_row[:, None])
    mask_rows = jnp.where(allowed, 0.0, NEG_FILL).astype(F32)
    mods_rest = jnp.concatenate(
        [
            matmul(class_act, ada16[:, cuts[0] : cuts[1]]).astype(BF16),
            matmul(act_two, ada16[:, cuts[1] :]).astype(BF16),
        ],
        axis=1,
    )
    first, one_far, two_far, one_near_c, two_near_c, mods_rest, up, token_hot, mask_rows = tie(
        first, one_far, two_far, one_near_c, two_near_c, mods_rest, up, token_hot, mask_rows
    )
    row_info = jnp.swapaxes(stack(row_info), 0, 1).reshape(2, -1)

    one_far_c, two_far_c = swap(one_far, 1), swap(two_far, 1)
    mods_rest = lend(mods_rest, [1], devices)
    half_up = half_ff + top
    up = stack(up)
    up_one, up_two = widen(up[:, :half_up], one_y, devices), widen(up[:, half_up:], two_x, devices)
    one_far_c, two_far_c, mods_rest, first, down = tie(
        one_far_c, two_far_c, mods_rest, first, down
    )

    mods_rest = added(*mods_rest)
    cut = cuts[1] - cuts[0]
    mod_one = lend(mods_rest[:, :cut], bits_x, devices)
    mod_two = lend(mods_rest[:, cut:], bits_y, devices)
    down = widen(down, bits_z[:1], devices)
    blocks_one = [qkv_one, one_far, one_near_c, one_far_c]
    blocks_two = [qkv_two, two_far, two_near_c, two_far_c]
    slim = jnp.concatenate(
        [
            matmul_tn(stack([block[:, half_qkv:] for block in blocks_one]), perm_one),
            matmul_tn(stack([block[:, half_qkv:] for block in blocks_two]), perm_two),
        ],
        axis=0,
    )
    gain_rows = slim[n_embed : n_embed + n_gains]
    ada_bias = gain_rows[ada_at:head_at].reshape(1, -1)
    resid_in = matmul(token_hot, slim.astype(BF16)) + gain_rows[0]
    first = first + ada_bias[:, : cuts[0]]
    mods = [first[:, :width], first[:, width:]]
    u_one, u_two = norm_ahead(resid_in, hot, mods[0], mods[1], [perm_one_t, perm_two_t])
    w_qkv = ((blocks_one, (0, half_qkv)), (blocks_two, (0, half_qkv)))
    qkv_bias = jnp.concatenate(
        [gain_rows[1:2], jnp.zeros((1, width), F32), gain_rows[2:3]], axis=1
    )
    q_gain, k_gain = gain_rows[5:6], gain_rows[6:7]
    qkv = times_sets([u_one, u_two], w_qkv, qkv_bias)
    qkv, up_one, up_two, mod_one, mod_two, down, head16 = tie(
        qkv, up_one, up_two, mod_one, mod_two, down, head16
    )

    up_one, up_two = stack(up_one), stack(up_two)
    for mask in bits_x[:-1]:
        up_one = grow(up_one, mask, devices)
    for mask in bits_y[:-1]:
        up_two = grow(up_two, mask, devices)
    mod_one = lend(added(*mod_one), bits_y, devices)
    mod_two = lend(added(*mod_two), bits_x, devices)
    up_one_far, up_two_far = swap(up_one, bits_x[-1]), swap(up_two, bits_y[-1])
    down = widen(stack(down), bits_z[1:], devices)
    mixture = attend(qkv, q_gain, k_gain, mask_rows)
    mixture, mod_one, mod_two, down, up_one, up_two = tie(
        mixture, mod_one, mod_two, down, up_one, up_two
    )

    mods_rest = jnp.concatenate([added(*mod_one), added(*mod_two)], axis=1)
    mods_rest = lend(mods_rest, bits_z[-1:], devices)
    up_one_c, up_two_c = swap(up_one, 1), swap(up_two, 1)
    mix_one = matmul(mixture, perm_one_t).astype(BF16)
    mix_two = matmul(mixture, perm_two_t).astype(BF16)
    mix_one, mix_two, mods_rest, up_one_c, up_two_c, down = tie(
        mix_one, mix_two, mods_rest, up_one_c, up_two_c, down
    )
    mods_rest = lend(added(*mods_rest), bits_z[:-1], devices)
    down = stack(down)
    down_one = widen(down[:, :half_ff], one_y, devices)
    down_two = widen(down[:, half_ff:], two_x, devices)
    mix_one, mix_two, mods_rest, up_one_far, up_two_far, head16 = tie(
        mix_one, mix_two, mods_rest, up_one_far, up_two_far, head16
    )
    up_one_fc, up_two_fc = swap(up_one_far, 1), swap(up_two_far, 1)
    head16 = widen(stack(head16), bits_z[:1], devices)
    mix_one, mix_two, up_one_fc, up_two_fc = tie(mix_one, mix_two, up_one_fc, up_two_fc)
    blocks_one = [up_one, up_one_far, up_one_c, up_one_fc]
    blocks_two = [up_two, up_two_far, up_two_c, up_two_fc]
    w_up = ((blocks_one, (0, half_ff)), (blocks_two, (0, half_ff)))
    w_proj = ((blocks_one, (half_ff, half_up)), (blocks_two, (half_ff, half_up)))
    mods_rest = added(*mods_rest, F32) + ada_bias[:, cuts[0] :]
    mods += [mods_rest[:, at : at + width] for at in range(0, 6 * width, width)]
    attn_out = times_sets([mix_one, mix_two], w_proj, gain_rows[3:4])
    u_mid_one, u_mid_two, resid_mid = norm_ahead(
        resid_in, hot, mods[3], mods[4], [perm_one_t, perm_two_t], mods[2], attn_out
    )
    u_mid_one, u_mid_two, resid_mid, down_one, down_two = tie(
        u_mid_one, u_mid_two, resid_mid, down_one, down_two
    )
    down_one, down_two = stack(down_one), stack(down_two)
    for mask in bits_x[:-1]:
        down_one = grow(down_one, mask, devices)
    for mask in bits_y[:-1]:
        down_two = grow(down_two, mask, devices)
    down_one_far, down_two_far = swap(down_one, bits_x[-1]), swap(down_two, bits_y[-1])
    down_one_c, down_two_c = swap(down_one, 1), swap(down_two, 1)
    up_bias = gain_rows[7:ada_at].reshape(1, -1)
    hidden, active = times_sets([u_mid_one, u_mid_two], w_up, up_bias, bend=True)
    active, down_one_far, down_two_far, down_one_c, down_two_c, head16 = tie(
        active, down_one_far, down_two_far, down_one_c, down_two_c, head16
    )

    down_one_fc, down_two_fc = swap(down_one_far, 1), swap(down_two_far, 1)
    head16 = widen(stack(head16), bits_z[1:], devices)
    active, down_one_fc, down_two_fc = tie(active, down_one_fc, down_two_fc)
    w_down = (
        ([down_one, down_one_far, down_one_c, down_one_fc], None),
        ([down_two, down_two_far, down_two_c, down_two_fc], None),
    )
    perms = [perm_one, perm_two]
    mlp_out = back_sets(active[None], w_down, perms, gain_rows[4:5], exact=True)
    head_masks = bits_y + bits_z
    perm_head, perm_head_t = hot_rows(
        source_rows(
            [mask // n_vocab for mask in head_masks], lax.axis_index("dp"), head_weight.shape[0]
        )
    )
    head_rel, resid_out = norm_ahead(
        resid_mid, hot, mods[6], mods[7], [perm_head_t], mods[5], mlp_out
    )
    head_rel, head16 = tie(head_rel, head16)
    head16 = stack(head16)

    vocab_masks = bits_x + [1]
    rows_all = grown(bits_x[:-1], head_rel)
    far = swap(rows_all, bits_x[-1])
    near_c = swap(rows_all, 1)
    code_span = head_weight.shape[1]
    code_start = lax.axis_index("vocab") * code_span
    head_bias = lax.dynamic_slice_in_dim(gain_rows[head_at:].reshape(-1), code_start, code_span)
    code = jnp.arange(code_span, dtype=jnp.int32)[None, :] + code_start

    def part_stats(part, info):
        logits = matmul(part, head16) + head_bias
        local_max = jnp.max(logits, axis=1)
        exp_sums = jnp.sum(jnp.exp(logits - local_max[:, None]), axis=1)
        is_target = (code == info[0].astype(jnp.int32)[:, None]).astype(F32)
        picked = jnp.sum(is_target * logits, axis=1)
        return logits, is_target, jnp.stack([local_max, exp_sums, picked])

    each = rows_all.shape[0]
    info_of = [row_info[:, at * each : (at + 1) * each] for at in range(4)]
    near_rows = jnp.concatenate([rows_all, near_c], axis=0)
    near_info = jnp.concatenate([info_of[0], info_of[2]], axis=1)
    far_info = jnp.concatenate([info_of[1], info_of[3]], axis=1)
    near_logits, near_target, near_stats = part_stats(near_rows, near_info)
    near_stats, far = tie(near_stats, far)
    far_rows = jnp.concatenate([far, swap(far, 1)], axis=0)
    far_logits, far_target, far_stats = part_stats(far_rows, far_info)
    places = [x ^ c for x in (0, bits_x[-1]) for c in (0, 1)]
    places = [place ^ other for place in places for other in place_masks(bits_x[:-1])]
    stats = jnp.concatenate([near_stats, far_stats], axis=1)
    group = [stats]
    for other in place_masks(vocab_masks)[1:]:
        their = jnp.split(swap(stats, other), n_vocab, axis=1)
        group.append(
            jnp.concatenate([their[places.index(place ^ other)] for place in places], axis=1)
        )
    row_max = group[0][0]
    for other in group[1:]:
        row_max = jnp.maximum(row_max, other[0])
    totals = sum(other[1] * jnp.exp(other[0] - row_max) for other in group)
    target_logit = sum(other[2] for other in group)
    log_total = row_max + jnp.log(totals)
    loss_part = jnp.sum((near_info[1] * (log_total - target_logit)[: 2 * each])[:length])
    mid = 2 * each

    def part_back(logits, is_target, info, log_total):
        coef = info[1] / total_count
        grad = coef[:, None] * (jnp.exp(logits - log_total[:, None]) - is_target)
        return grad.astype(BF16)

    d_far_logits = part_back(far_logits, far_target, far_info, log_total[mid:])
    d_near_logits = part_back(near_logits, near_target, near_info, log_total[:mid])
    d_far = matmul_nt(d_far_logits, head16).astype(BF16)
    d_near = matmul_nt(d_near_logits, head16).astype(BF16)
    to_core = jnp.concatenate([d_near[each:], d_far[each:]], axis=0)
    back = swap(to_core, 1)
    d_far, d_near = added(d_far[:each], back[each:]), added(d_near[:each], back[:each])
    rows_all = jnp.concatenate([near_rows, far_rows], axis=0)
    d_logits = jnp.concatenate([d_near_logits, d_far_logits], axis=0)
    d_far, head16 = tie(d_far, head16)
    d_head_in = added(d_near, swap(d_far, bits_x[-1]), F32)
    for mask in reversed(bits_x[:-1]):
        d_head_in = keep_half(d_head_in.astype(BF16), mask, devices, F32)
    head_far = matmul_tn(rows_all[:, top:], d_logits).astype(BF16)
    head_near = matmul_tn(rows_all[:, :top], d_logits).astype(BF16)
    bias_grad = lax.dynamic_update_slice(
        jnp.zeros((V,), F32), jnp.sum(d_logits.astype(F32), axis=0), (code_start,)
    )
    d_head_in, head_far, head_near = tie(d_head_in, head_far, head_near)

    def cross(one, two):
        return swap(one, bits_x[-1]), swap(two, bits_y[-1])

    def join(one, two, one_back, two_back):
        one, two = added(one, one_back), added(two, two_back)
        for mask in reversed(bits_y[:-1]):
            two = keep_half(two, mask, devices)
        for mask in reversed(bits_x[:-1]):
            one = keep_half(one, mask, devices)
        half = one.shape[0] // 2
        return tuple(
            jnp.concatenate([one[at : at + half], two[at : at + half]], axis=1) for at in (0, half)
        )

    def turn(one, two, one_back, two_back):
        one, one_far = halves_of(one, one_back)
        two, two_far = halves_of(two, two_back)
        for mask in reversed(bits_x[:-1]):
            whole_one = jnp.concatenate([one, one_far], axis=0)
            one, one_far = halves_of(
                whole_one[: whole_one.shape[0] // 2],
                swap(whole_one[whole_one.shape[0] // 2 :], mask),
            )
        for mask in reversed(bits_y[:-1]):
            whole_two = jnp.concatenate([two, two_far], axis=0)
            two, two_far = halves_of(
                whole_two[: whole_two.shape[0] // 2],
                swap(whole_two[whole_two.shape[0] // 2 :], mask),
            )
        return one, one_far, two, two_far

    def cross_back(one_far, two_far):
        return swap(one_far, bits_y[-1]), swap(two_far, bits_x[-1])

    perms = [perm_one, perm_two]
    ones, twos = (0, half_ff), (half_ff, FF)
    q_ones, q_twos = (0, half_qkv), (half_qkv, 3 * width)
    downs, ups = [None, None], [u_mid_one, u_mid_two]
    mixes, ins = [mix_one, mix_two], [u_one, u_two]
    ffs, projs, qkvs = [ones, twos], [(0, top), (top, width)], [q_ones, q_twos]

    active = active[None]
    head_back = swap(head_far, head_masks[-1])
    d_head_in = in_halves_outside(lambda part: matmul(part, perm_head), d_head_in)
    d_resid_out, d_shift_head, d_scale_head, down_bias, d_gate_two, *downs = norm_back(
        resid_out,
        d_head_in,
        hot,
        hot_t,
        mods[7],
        gate=mods[5],
        branch=mlp_out,
        perms=[perm_one_t, perm_two_t],
    )
    down_f = grad_sets(downs, active, ffs)
    downs, down_f = tie(downs, down_f)
    down_b = swap(down_f, 1)
    d_hid, up_bias_sum = times_sets(downs, w_down, hidden=hidden)
    d_hid, down_b = tie(d_hid, down_b)
    d_hid = d_hid[None]
    down_n1, down_f1, down_n2, down_f2 = grad_sets(downs, active, ffs, down_b)
    up_f = grad_sets(ups, d_hid, ffs)
    d_hid, down_f1, down_f2, down_n1, down_n2, up_f = tie(
        d_hid, down_f1, down_f2, down_n1, down_n2, up_f
    )
    down_x1, down_x2 = cross(down_f1, down_f2)
    up_b = swap(up_f, 1)
    d_u = back_sets(d_hid, w_up, perms)
    d_u, up_b = tie(d_u, up_b)
    up_n1, up_f1, up_n2, up_f2 = grad_sets(ups, d_hid, ffs, up_b)
    d_resid_mid, d_shift_two, d_scale_two, proj_bias, d_gate_one, d_low = norm_back(
        resid_mid, d_u, hot, hot_t, mods[4], beyond=d_resid_out, gate=mods[2], branch=attn_out
    )
    d_low, down_x1, down_x2, up_f1, up_f2, up_n1, up_n2, head_back, head_near = tie(
        d_low, down_x1, down_x2, up_f1, up_f2, up_n1, up_n2, head_back, head_near
    )
    down_n1, down_f1, down_n2, down_f2 = turn(down_n1, down_n2, down_x1, down_x2)
    d_low, down_f1, down_f2, up_f1, up_f2, head_back = tie(
        d_low, down_f1, down_f2, up_f1, up_f2, head_back
    )
    head_near, head_far = halves_of(head_near, head_back)
    down_x1, down_x2 = cross_back(down_f1, down_f2)
    up_x1, up_x2 = cross(up_f1, up_f2)
    head_back = swap(head_far, head_masks[-2])
    d_low = d_low[None]
    proj_f = grad_sets(mixes, d_low, projs)
    d_mix = back_sets(d_low, w_proj, perms, out=BF16)
    d_qkv, attn_sums = attend_back(qkv, q_gain, k_gain, mask_rows, d_mix)
    d_qkv, proj_f, down_x1, down_x2, down_n1, down_n2, up_x1, up_x2, head_back, head_near = tie(
        d_qkv, proj_f, down_x1, down_x2, down_n1, down_n2, up_x1, up_x2, head_back, head_near
    )
    up_n1, up_f1, up_n2, up_f2 = turn(up_n1, up_n2, up_x1, up_x2)
    down_near, down_far = join(down_n1, down_n2, down_x1, down_x2)
    d_qkv, up_f1, up_f2, down_far, proj_f = tie(d_qkv, up_f1, up_f2, down_far, proj_f)
    up_x1, up_x2 = cross_back(up_f1, up_f2)
    down_back = swap(down_far, bits_z[-1])
    proj_b = swap(proj_f, 1)
    qkv_f = grad_sets(ins, d_qkv, qkvs)
    d_qkv, qkv_f, proj_b = tie(d_qkv, qkv_f, proj_b)
    qkv_b = swap(qkv_f, 1)
    head_near = added(head_near, head_back)
    head_grad = lend(head_near, head_masks[:-2], devices)
    d_u = back_sets(d_qkv, w_qkv, perms)
    d_u, qkv_b, up_x1, up_x2, down_back, down_near, head_grad = tie(
        d_u, qkv_b, up_x1, up_x2, down_back, down_near, head_grad
    )
    head_grad = added(*head_grad, F32)
    down_near, down_far = halves_of(down_near, down_back)
    d_u, down_far, qkv_b, up_x1, up_x2 = tie(d_u, down_far, qkv_b, up_x1, up_x2)
    down_back = swap(down_far, bits_z[-2])
    d_resid_in, d_shift_one, d_scale_one, word_bias, d_res16 = norm_back(
        resid_in, d_u, hot, hot_t, mods[1], beyond=d_resid_mid
    )
    d_mod = jnp.concatenate(
        [
            d_shift_one,
            d_scale_one,
            d_gate_one,
            d_shift_two,
            d_scale_two,
            d_gate_two,
            d_shift_head,
            d_scale_head,
        ],
        axis=1,
    ).astype(BF16)
    ada_sums = jnp.sum(d_mod.astype(F32), axis=0, keepdims=True)
    arrays = [word_bias, attn_sums, proj_bias, down_bias, up_bias_sum, ada_sums, bias_grad[None]]
    plan = [(0, 0), (1, 2), (1, 3), (2, 0), (3, 0), (1, 0), (1, 1), (4, 0), (5, 0), (6, 0)]
    d_slim = slim_back(d_res16, token_hot, arrays, plan, perms, n_embed)
    d_slim, d_mod, qkv_b = tie(d_slim, d_mod, qkv_b)
    slim_b = swap(d_slim[top:], 1)
    qkv_n1, qkv_f1, qkv_n2, qkv_f2 = grad_sets(ins, d_qkv, qkvs, qkv_b)
    proj_n1, proj_f1, proj_n2, proj_f2 = grad_sets(mixes, d_low, projs, proj_b)
    (
        qkv_n1,
        qkv_f1,
        qkv_n2,
        qkv_f2,
        proj_n1,
        proj_f1,
        proj_n2,
        proj_f2,
        slim_b,
        down_back,
        up_x1,
        up_x2,
    ) = tie(
        qkv_n1,
        qkv_f1,
        qkv_n2,
        qkv_f2,
        proj_n1,
        proj_f1,
        proj_n2,
        proj_f2,
        slim_b,
        down_back,
        up_x1,
        up_x2,
    )

    def beside(*parts):
        return jnp.concatenate(parts, axis=1)

    far_slim = added(d_slim[quarter:top], slim_b[quarter:])
    qkv_f1 = beside(qkv_f1, proj_f1, far_slim[:, :half_slim])
    qkv_f2 = beside(qkv_f2, proj_f2, far_slim[:, half_slim:])
    up_near, up_far = join(up_n1, up_n2, up_x1, up_x2)
    d_mod, up_far, qkv_f1, qkv_f2 = tie(d_mod, up_far, qkv_f1, qkv_f2)
    qkv_x1, qkv_x2 = cross(qkv_f1, qkv_f2)
    up_back = swap(up_far, bits_z[-1])
    all_mod = widen(d_mod, bits_z, devices)
    near_slim = added(d_slim[:quarter], slim_b[:quarter])
    qkv_n1 = beside(qkv_n1, proj_n1, near_slim[:, :half_slim])
    qkv_n2 = beside(qkv_n2, proj_n2, near_slim[:, half_slim:])
    qkv_x1, qkv_x2, qkv_n1, qkv_n2, all_mod, up_back, up_near = tie(
        qkv_x1, qkv_x2, qkv_n1, qkv_n2, all_mod, up_back, up_near
    )
    qkv_n1, qkv_f1, qkv_n2, qkv_f2 = turn(qkv_n1, qkv_n2, qkv_x1, qkv_x2)
    up_near, up_far = halves_of(up_near, up_back)
    qkv_x1, qkv_x2 = cross_back(qkv_f1, qkv_f2)
    up_back = swap(up_far, bits_z[-2])
    all_mod = stack(all_mod)
    all_first = widen(all_mod[:, : cuts[1]], bits_y, devices)
    all_two = widen(all_mod[:, cuts[1] :], bits_x, devices)
    qkv_x1, qkv_x2, qkv_n1, qkv_n2, up_back, all_first, all_two = tie(
        qkv_x1, qkv_x2, qkv_n1, qkv_n2, up_back, all_first, all_two
    )
    near, far = join(qkv_n1, qkv_n2, qkv_x1, qkv_x2)
    attn_back = swap(far, bits_z[-1])
    all_two = widen(stack(all_two), bits_y, devices)
    all_first = widen(stack(all_first), bits_x, devices)
    attn_back, near, all_two, all_first = tie(attn_back, near, all_two, all_first)
    near, far = halves_of(near, attn_back)
    attn_back = swap(far, bits_z[-2])
    all_two = grown([1], stack(all_two))
    all_first = grown([1], stack(all_first))

    def close(near, back):
        masks = bits_z[:-2]
        near = added(near, back, BF16 if masks else F32)
        return keep_all(near, masks, devices)

    up_rows, down_rows = close(up_near, up_back), close(down_near, down_back)
    mlp_grad = jnp.stack([up_rows, down_rows])
    ada_grad = jnp.concatenate([matmul_tn(class_act, all_first), matmul_tn(act_two, all_two)], axis=1)
    d_class_act = matmul_nt(all_first, ada16[:, : cuts[1]]) + to_one(
        matmul_nt(all_two, ada16[:, cuts[1] :])
    )
    _, silu_back = jax.vjp(jax.nn.silu, class_vec)
    d_class = precise_tn(class_hot.astype(F32), silu_back(d_class_act)[0])
    squares_local = jnp.zeros((), F32)
    for gradient in (mlp_grad, ada_grad, d_class, head_grad):
        squares_local = squares_local + jnp.sum(gradient * gradient)
    squares_local, mlp_grad, ada_grad, d_class, near, attn_back = tie(
        squares_local, mlp_grad, ada_grad, d_class, near, attn_back
    )
    attn_rows = close(near, attn_back)
    squares_local = squares_local + jnp.sum(attn_rows * attn_rows)
    half_attn = half_qkv + top
    half_all = half_attn + half_slim
    attn_grad = jnp.concatenate(
        [
            attn_rows[:, :half_qkv],
            attn_rows[:, half_all : half_all + half_qkv],
            attn_rows[:, half_qkv:half_attn],
            attn_rows[:, half_all + half_qkv : half_all + half_attn],
        ],
        axis=1,
    )
    slim_grad = jnp.concatenate(
        [attn_rows[:, half_attn:half_all], attn_rows[:, half_all + half_attn :]], axis=1
    ).T
    embed_grad = jnp.concatenate(
        [
            d_class,
            slim_grad[:used],
            jnp.zeros((POSITIONS - used, rows), F32),
            slim_grad[used:n_embed],
        ],
        axis=0,
    )
    gains_grad = slim_grad[n_embed : n_embed + n_gains]
    gradients = (attn_grad, mlp_grad, ada_grad, embed_grad, gains_grad, head_grad)
    sums = sum_all(
        jnp.stack([squares_local, loss_part])[None], [1] + bits_x + bits_y + bits_z, devices
    )
    total_sq, loss_sum = sums[0, 0], sums[0, 1]
    grad_norm = jnp.sqrt(total_sq)
    clip_factor = jnp.minimum(1.0, CLIP_NORM / (grad_norm + 1e-06))
    masters = (attn_weight, mlp_weight, ada_weight, embed_weight, gains_weight, head_weight)
    moments = (attn_moment, mlp_moment, ada_moment, embed_moment, gains_moment, head_moment)
    squares = (attn_square, mlp_square, ada_square, embed_square, gains_square, head_square)
    updates = []
    for number in range(6):
        updates.extend(
            adam_step(
                masters[number],
                moments[number],
                squares[number],
                gradients[number],
                clip_factor,
                RATES[number],
            )
        )
    return tuple(updates) + (grad_norm, loss_sum, total_count)


def solution(mesh):
    n_dp, n_vocab = mesh.shape["dp"], mesh.shape["vocab"]
    n_z = 1 << (n_dp.bit_length() // 2)
    devices = n_dp * n_vocab

    def bits(least, top):
        found = []
        while least < top:
            found, least = [least] + found, least * 2
        return found

    ways = {"devices": devices, "n_vocab": n_vocab}
    ways["x"] = bits(2, n_vocab)
    ways["y"] = bits(n_vocab, devices // n_z)
    ways["z"] = bits(devices // n_z, devices)
    every = ("dp", "vocab")
    by_row = P(every, None)
    by_mid = P(None, every, None)
    by_column = P(None, every)
    head = P("dp", "vocab")
    placed = (P(every, None, None), by_row, by_row, by_row, by_row)
    for spec in (by_row, by_mid, by_row, by_column, by_column, head):
        placed = placed + (spec,) * 3
    given = ()
    for spec in (by_row, by_mid, by_row, by_column, by_column, head):
        given = given + (spec,) * 4

    def step(*arrays):
        return per_device(ways, *arrays)

    return jax.shard_map(
        step, mesh=mesh, in_specs=placed, out_specs=given + (P(), P(), P()), check_vma=False
    )
```

```python
import jax
import jax.numpy as jnp
from jax import lax
from jax.experimental import pallas as pl
from jax.experimental.pallas import tpu as pltpu
from jax.sharding import PartitionSpec as P

HEADS = 16
HEAD_DIM = 64
FF = 4096
V = 4096
CHANNELS = 32
CLASSES = 1001
POSITIONS = 680
LEVELS = 10
MAXIMG = 8
STEPS = 10


EPS_NORM = 1e-06
BETA_ONE = 0.9
BETA_TWO = 0.95
ADAM_EPS = 1e-08
DECAY = 0.05
CLIP_NORM = 0.001
RATES = (0.03, 0.03, 0.03, 0.15, 0.4, 0.03)
NEG_FILL = -1e30
BF16 = jnp.bfloat16
F32 = jnp.float32
SPANS = (1024, 512)
TOKENS = 128
PAIR = 2 * HEAD_DIM


def matmul(left, right):
    return jnp.dot(left, right, preferred_element_type=F32)


def matmul_tn(left, right):
    return lax.dot_general(left, right, (((0,), (0,)), ((), ())), preferred_element_type=F32)


def matmul_nt(left, right):
    return lax.dot_general(left, right, (((1,), (1,)), ((), ())), preferred_element_type=F32)


def precise_tn(left, right):
    return lax.dot_general(left, right, (((0,), (0,)), ((), ())), precision=lax.Precision.HIGHEST)


def pick(hot, values):
    return in_halves(lambda part: matmul(hot, part), values)


def in_halves(times, values):
    upper = values.astype(BF16)
    return times(upper) + times((values - upper.astype(F32)).astype(BF16))


def in_halves_outside(times, values):
    upper = lax.reduce_precision(values, 8, 7)
    return times(upper.astype(BF16)) + times((values - upper).astype(BF16))


def swapped(value, mask, devices):
    return lax.ppermute(value, ("dp", "vocab"), [(i, i ^ mask) for i in range(devices)])


def tie(*values):
    return lax.optimization_barrier(values)


def grow(value, mask, devices):
    return jnp.concatenate([value, swapped(value, mask, devices)], axis=0)


def spread(value, masks, devices):
    if len(masks) == 2:
        masks = masks + [masks[0] ^ masks[1]]
    return [value] + [swapped(value, mask, devices) for mask in masks]


def stack(parts):
    return jnp.concatenate(parts, axis=0)


def widen(value, masks, devices):
    for mask in masks[:-1]:
        value = grow(value, mask, devices)
    return [value, swapped(value, masks[-1], devices)]


def added(mine, theirs, out=BF16):
    return (mine.astype(F32) + theirs.astype(F32)).astype(out)


def keep_half(value, mask, devices, out=BF16):
    half = value.shape[0] // 2
    return added(value[:half], swapped(value[half:].astype(BF16), mask, devices), out)


def lend(value, masks, devices):
    for mask in reversed(masks[1:]):
        value = keep_half(value, mask, devices)
    half = value.shape[0] // 2
    return [value[:half], swapped(value[half:].astype(BF16), masks[0], devices)]


def keep_all(value, masks, devices):
    for mask in reversed(masks):
        value = keep_half(value, mask, devices, F32 if mask == masks[0] else BF16)
    return value


def halves_of(mine, back, out=BF16):
    half = mine.shape[0] // 2
    return (added(mine[:half], back[:half], out), added(mine[half:], back[half:], out))


def sum_all(value, bits, devices):
    for at in range(0, len(bits), 2):
        masks = place_masks(bits[at : at + 2])[1:]
        value = value + sum(swapped(value, mask, devices) for mask in masks)
    return value


def place_masks(masks):
    places = [0]
    for mask in masks:
        places = places + [place ^ mask for place in places]
    return places


def source_rows(masks, me, rows):
    differ = jnp.repeat(jnp.array(place_masks(masks), jnp.int32), rows)
    row = jnp.tile(jnp.arange(rows, dtype=jnp.int32), 1 << len(masks))
    return (differ ^ me) * rows + row


def hot_rows(source):
    place = jnp.arange(source.shape[0], dtype=jnp.int32)
    return (
        (source[:, None] == place[None, :]).astype(BF16),
        (place[:, None] == source[None, :]).astype(BF16),
    )


def run(body, grid, given, specs, outs, out_specs, scratch=()):
    return pl.pallas_call(
        body,
        grid=grid,
        in_specs=specs,
        out_shape=outs,
        out_specs=out_specs,
        scratch_shapes=scratch,
        compiler_params=pltpu.CompilerParams(vmem_limit_bytes=24 << 20),
        cost_estimate=pl.CostEstimate(flops=1000, bytes_accessed=1000, transcendentals=0),
    )(*given)


def whole(value):
    return pl.BlockSpec(value.shape, lambda j: (0,) * value.ndim)


def span_of(*sizes):
    return [span for span in SPANS if all(size % span == 0 for size in sizes)][0]


def columns_of(sets):
    return [blocks[0].shape[1] if used is None else used[1] - used[0] for blocks, used in sets]


def starts_of(sets):
    return [0 if used is None else used[0] for _, used in sets]


def two_sets(sets, first, span):
    one, two = [start // span for start in starts_of(sets)]
    specs = [
        pl.BlockSpec((block.shape[0], span), lambda j: (0, one + jnp.minimum(j, first - 1)))
        for block in sets[0][0]
    ]
    specs += [
        pl.BlockSpec((block.shape[0], span), lambda j: (0, two + jnp.maximum(j - first, 0)))
        for block in sets[1][0]
    ]
    return specs


def gelu_parts(value):
    inner = 0.7978845608028654 * (value + 0.044715 * (value * value * value))
    bend = jnp.tanh(inner)
    return bend


def gelu(value):
    return 0.5 * value * (1.0 + gelu_parts(value))


def gelu_slope(value):
    bend = gelu_parts(value)
    rise = 0.7978845608028654 * (1.0 + 3.0 * 0.044715 * value * value)
    return 0.5 * (1.0 + bend) + 0.5 * value * (1.0 - bend * bend) * rise


def times_sets(left, sets, bias=None, hidden=None, bend=False):
    tokens = left[0].shape[0]
    columns = columns_of(sets)
    span = span_of(*columns, *starts_of(sets))
    first, steps = columns[0] // span, sum(columns) // span
    specs = two_sets(sets, first, span)
    count = len(sets[0][0])
    extra = [value for value in (bias, hidden) if value is not None]
    column = lambda j: (0, j)
    extra_specs = [pl.BlockSpec((value.shape[0], span), column) for value in extra]

    def body(one_ref, two_ref, *refs):
        extras, blocks = refs[: len(extra)], refs[len(extra) : len(extra) + 2 * count]
        outs = refs[len(extra) + 2 * count :]

        def part(u_ref, blocks):
            total, at = None, 0
            for block in blocks:
                rows = block.shape[0]
                term = matmul(u_ref[:, at : at + rows], block[...])
                total = term if total is None else total + term
                at += rows
            if bias is not None:
                total = total + extras[0][...]
            if hidden is not None:
                slope = gelu_slope(extras[-1][...])
                low = (total * slope).astype(BF16)
                outs[0][...] = low
                outs[1][...] = jnp.sum(low.astype(F32), axis=0, keepdims=True)
            else:
                outs[0][...] = total
                if bend:
                    outs[1][...] = gelu(total).astype(BF16)

        pl.when(pl.program_id(0) < first)(lambda: part(one_ref, blocks[:count]))
        pl.when(pl.program_id(0) >= first)(lambda: part(two_ref, blocks[count:]))

    wide = steps * span
    shape = jax.ShapeDtypeStruct
    outs, out_specs = [shape((tokens, wide), F32)], [pl.BlockSpec((tokens, span), column)]
    if hidden is not None:
        outs = [shape((tokens, wide), BF16), shape((1, wide), F32)]
        out_specs.append(pl.BlockSpec((1, span), column))
    elif bend:
        outs.append(shape((tokens, wide), BF16))
        out_specs.append(pl.BlockSpec((tokens, span), column))
    given = list(left) + extra + list(sets[0][0]) + list(sets[1][0])
    specs = [whole(value) for value in left] + extra_specs + specs
    found = run(body, (steps,), given, specs, outs, out_specs)
    return found if len(outs) > 1 else found[0]


def span_spec(value, span):
    each = value.shape[2] // span
    return pl.BlockSpec((1, value.shape[1], span), lambda j: (j // each, 0, j % each))


def back_sets(right, sets, perms, bias=None, exact=False, out=F32):
    tokens = right.shape[1]
    columns = columns_of(sets)
    span = span_of(right.shape[2], *columns, *starts_of(sets))
    first, steps = columns[0] // span, sum(columns) // span
    specs = two_sets(sets, first, span)
    count = len(sets[0][0])
    width = perms[0].shape[0]
    extra = [] if bias is None else [bias]

    def body(right_ref, one_ref, two_ref, *refs):
        extras, blocks = refs[: len(extra)], refs[len(extra) : len(extra) + 2 * count]
        out_ref, one_sum, two_sum = refs[len(extra) + 2 * count :]
        step = pl.program_id(0)

        def part(sums, blocks, start):
            terms = [matmul_nt(right_ref[0], block[...]) for block in blocks]
            term = jnp.concatenate(terms, axis=1)

            @pl.when(step == start)
            def _():
                sums[...] = term

            @pl.when(step > start)
            def _():
                sums[...] += term

        pl.when(step < first)(lambda: part(one_sum, blocks[:count], 0))
        pl.when(step >= first)(lambda: part(two_sum, blocks[count:], first))

        @pl.when(step == steps - 1)
        def _():
            total = None
            for sums, perm in ((one_sum, one_ref), (two_sum, two_ref)):
                if exact:
                    term = in_halves(lambda part: matmul(part, perm[...]), sums[...])
                else:
                    term = matmul(sums[...].astype(BF16), perm[...])
                total = term if total is None else total + term
            if bias is not None:
                total = total + extras[0][...]
            out_ref[...] = total.astype(out)

    given = [right] + list(perms) + extra + list(sets[0][0]) + list(sets[1][0])
    specs = [span_spec(right, span)] + [whole(value) for value in list(perms) + extra] + specs
    outs = jax.ShapeDtypeStruct((tokens, width), out)
    scratch = [pltpu.VMEM((tokens, width), F32)] * 2
    return run(body, (steps,), given, specs, outs, whole(outs), scratch)


def grad_sets(left, right, columns, back=None):
    tokens, width = left[0].shape
    parts = 2 if back is not None else 1
    half = width // 2
    count = half // parts
    wide = [stop - start for start, stop in columns]
    span = span_of(right.shape[2], *wide, *[start for start, _ in columns])
    each = right.shape[2] // span
    first, steps = wide[0] // span, sum(wide) // span
    at = [start // span for start, _ in columns]

    def place(j):
        block = jnp.where(j < first, j + at[0], j - first + at[1])
        return (block // each, 0, block % each)

    def body(one_ref, two_ref, right_ref, *refs):
        def part(left_ref, outs):
            total = matmul_tn(left_ref[...], right_ref[0])
            if back is not None:
                total = total + refs[0][...].astype(F32)
            for which, out in enumerate(outs):
                out[...] = total[which * count : (which + 1) * count].astype(BF16)

        step = pl.program_id(0)
        if back is None:
            pl.when(step < first)(lambda: part(one_ref, refs))
            pl.when(step >= first)(lambda: part(two_ref, refs))
        else:
            pl.when(step < first)(lambda: part(one_ref, refs[1:3]))
            pl.when(step >= first)(lambda: part(two_ref, refs[3:]))

    side = 0 if back is not None else 1
    given = list(left) + [right]
    specs = [pl.BlockSpec((tokens, half), lambda j: (0, side)) for _ in left]
    specs.append(pl.BlockSpec((1, tokens, span), place))
    own = pl.BlockSpec((half, span), lambda j: (0, j))
    if back is None:
        outs = jax.ShapeDtypeStruct((half, sum(wide)), BF16)
        return run(body, (steps,), given, specs, outs, own)
    outs, out_specs = [], []
    indices = (lambda j: (0, jnp.minimum(j, first - 1)), lambda j: (0, jnp.maximum(j - first, 0)))
    for size, index in zip(wide, indices):
        outs += [jax.ShapeDtypeStruct((count, size), BF16)] * 2
        out_specs += [pl.BlockSpec((count, span), index)] * 2
    return run(body, (steps,), given + [back], specs + [own], outs, out_specs)


def head_scale(value, left_half):
    square = value * value
    one = jnp.sum(jnp.where(left_half, square, 0.0), axis=1, keepdims=True)
    two = jnp.sum(jnp.where(left_half, 0.0, square), axis=1, keepdims=True)
    return jnp.where(
        left_half,
        lax.rsqrt(one * (1.0 / HEAD_DIM) + EPS_NORM),
        lax.rsqrt(two * (1.0 / HEAD_DIM) + EPS_NORM),
    )


def soft_rows(q_norm, k_norm, mask):
    scores = matmul_nt(q_norm, k_norm) * HEAD_DIM ** (-0.5) + mask
    terms = jnp.exp(scores - jnp.max(scores, axis=1, keepdims=True))
    return terms * (1.0 / jnp.sum(terms, axis=1, keepdims=True))


def pair_specs(tokens):
    pairs = HEADS // 2
    return [
        pl.BlockSpec((tokens, PAIR), lambda j: (0, j)),
        pl.BlockSpec((tokens, PAIR), lambda j: (0, pairs + j)),
        pl.BlockSpec((tokens, PAIR), lambda j: (0, 2 * pairs + j)),
        pl.BlockSpec((1, PAIR), lambda j: (0, j)),
        pl.BlockSpec((1, PAIR), lambda j: (0, j)),
        pl.BlockSpec((tokens, tokens), lambda j: (0, 0)),
    ]


def attend(qkv, q_gain, k_gain, mask):
    tokens, width = qkv.shape[0], qkv.shape[1] // 3

    def body(q_ref, k_ref, v_ref, qg_ref, kg_ref, mask_ref, out_ref):
        left_half = lax.broadcasted_iota(jnp.int32, (1, PAIR), 1) < HEAD_DIM
        query, key = q_ref[...], k_ref[...]
        q_norm = (query * head_scale(query, left_half) * qg_ref[...]).astype(BF16)
        k_norm = (key * head_scale(key, left_half) * kg_ref[...]).astype(BF16)
        v_low = v_ref[...].astype(BF16)
        zero = jnp.zeros_like(q_norm)
        mixed = []
        for one in (jnp.where(left_half, q_norm, zero), jnp.where(left_half, zero, q_norm)):
            probs = soft_rows(one, k_norm, mask_ref[...])
            mixed.append(matmul(probs.astype(BF16), v_low))
        out_ref[...] = jnp.where(left_half, mixed[0], mixed[1]).astype(BF16)

    outs = jax.ShapeDtypeStruct((tokens, width), BF16)
    spec = pl.BlockSpec((tokens, PAIR), lambda j: (0, j))
    given = [qkv, qkv, qkv, q_gain, k_gain, mask]
    return run(body, (HEADS // 2,), given, pair_specs(tokens), outs, spec)


def attend_back(qkv, q_gain, k_gain, mask, d_mix):
    tokens, width = qkv.shape[0], qkv.shape[1] // 3

    def body(q_ref, k_ref, v_ref, qg_ref, kg_ref, mask_ref, dm_ref, out_ref, sums_ref):
        left_half = lax.broadcasted_iota(jnp.int32, (1, PAIR), 1) < HEAD_DIM
        query, key = q_ref[...], k_ref[...]
        q_scale, k_scale = head_scale(query, left_half), head_scale(key, left_half)
        q_norm = (query * q_scale * qg_ref[...]).astype(BF16)
        k_norm = (key * k_scale * kg_ref[...]).astype(BF16)
        v_low, d_mix = v_ref[...].astype(BF16), dm_ref[...]
        zero = jnp.zeros_like(q_norm)
        found = []
        for side in range(2):
            own = (lambda v: jnp.where(left_half, v, zero)) if side == 0 else (
                lambda v: jnp.where(left_half, zero, v)
            )
            probs = soft_rows(own(q_norm), k_norm, mask_ref[...])
            d_values = matmul_tn(probs.astype(BF16), d_mix)
            d_probs = matmul_nt(own(d_mix), v_low)
            inner = jnp.sum(d_probs * probs, axis=1, keepdims=True)
            d_scores = (probs * (d_probs - inner)).astype(BF16)
            found.append((matmul(d_scores, k_norm), matmul_tn(d_scores, q_norm), d_values))
        d_qn, d_kn, d_values = (jnp.where(left_half, one, two) for one, two in zip(*found))
        sums = []
        for at, value, scale, gain, d_norm in (
            (0, query, q_scale, qg_ref[...], d_qn * HEAD_DIM ** (-0.5)),
            (1, key, k_scale, kg_ref[...], d_kn * HEAD_DIM ** (-0.5)),
        ):
            product = d_norm * value
            sums.append(jnp.sum(product * scale, axis=0, keepdims=True))
            product = product * gain
            one = jnp.sum(jnp.where(left_half, product, 0.0), axis=1, keepdims=True)
            two = jnp.sum(jnp.where(left_half, 0.0, product), axis=1, keepdims=True)
            mean = jnp.where(left_half, one, two) * (1.0 / HEAD_DIM)
            d_value = scale * (gain * d_norm - value * (scale * scale) * mean)
            out_ref[at] = d_value.astype(BF16)
        out_ref[2] = d_values.astype(BF16)
        sums.append(jnp.sum(out_ref[0].astype(F32), axis=0, keepdims=True))
        sums.append(jnp.sum(out_ref[2].astype(F32), axis=0, keepdims=True))
        sums_ref[...] = jnp.concatenate(sums + [jnp.zeros((4, PAIR), F32)], axis=0)

    outs = [
        jax.ShapeDtypeStruct((3, tokens, width), BF16),
        jax.ShapeDtypeStruct((8, width), F32),
    ]
    out_specs = [
        pl.BlockSpec((3, tokens, PAIR), lambda j: (0, 0, j)),
        pl.BlockSpec((8, PAIR), lambda j: (0, j)),
    ]
    given = [qkv, qkv, qkv, q_gain, k_gain, mask, d_mix]
    specs = pair_specs(tokens) + [pl.BlockSpec((tokens, PAIR), lambda j: (0, j))]
    return run(body, (HEADS // 2,), given, specs, outs, out_specs)


def row_stats(value):
    center = value - jnp.mean(value, axis=1, keepdims=True)
    return center, lax.rsqrt(jnp.mean(center * center, axis=1, keepdims=True) + EPS_NORM)


def by_tokens(value):
    return pl.BlockSpec((TOKENS, value.shape[1]), lambda j: (j, 0))


def norm_ahead(value, hot, shift, scale, perms, gate=None, branch=None):
    tokens, width = value.shape
    extra = [] if gate is None else [gate, branch]

    def body(value_ref, hot_ref, shift_ref, scale_ref, *refs):
        total = value_ref[...]
        outs = refs[len(extra) + len(perms) :]
        if gate is not None:
            total = total + pick(hot_ref[...], refs[0][...]) * refs[1][...]
            outs[-1][...] = total
        center, inverse = row_stats(total)
        scales = 1.0 + pick(hot_ref[...], scale_ref[...])
        normed = center * inverse * scales + pick(hot_ref[...], shift_ref[...])
        normed = normed.astype(BF16)
        for perm_ref, out_ref in zip(refs[len(extra) : len(extra) + len(perms)], outs):
            out_ref[...] = matmul(normed, perm_ref[...]).astype(BF16)

    given = [value, hot, shift, scale] + extra + list(perms)
    specs = [by_tokens(value), by_tokens(hot), whole(shift), whole(scale)]
    specs += [whole(gate), by_tokens(branch)] if extra else []
    specs += [whole(perm) for perm in perms]
    outs = [jax.ShapeDtypeStruct((tokens, width), BF16) for _ in perms]
    outs += [jax.ShapeDtypeStruct((tokens, width), F32)] if extra else []
    out_specs = [by_tokens(value) for _ in outs]
    return run(body, (tokens // TOKENS,), given, specs, outs, out_specs)


def norm_back(value, d_out, hot, hot_t, scale, beyond=None, gate=None, branch=None, perms=()):
    tokens, width = value.shape
    gated = gate is not None
    tall = [value, d_out] + ([] if beyond is None else [beyond]) + ([branch] if gated else [])
    flat = [scale] + ([gate] if gated else []) + list(perms)

    def body(hot_ref, hot_t_ref, *refs):
        talls, flats = refs[: len(tall)], refs[len(tall) : len(tall) + len(flat)]
        outs = refs[len(tall) + len(flat) :]
        total_ref, shift_ref, scale_ref, column_ref = outs[:4]
        d_out = talls[1][...]
        center, inverse = row_stats(talls[0][...])
        normed = center * inverse
        d_norm = d_out * (1.0 + pick(hot_ref[...], flats[0][...]))
        mean = jnp.mean(d_norm, axis=1, keepdims=True)
        along = jnp.mean(d_norm * normed, axis=1, keepdims=True)
        total = (d_norm - mean - normed * along) * inverse
        if beyond is not None:
            total = total + talls[2][...]
        total_ref[...] = total
        sums = [
            (shift_ref, pick(hot_t_ref[...], d_out)),
            (scale_ref, pick(hot_t_ref[...], d_out * normed)),
        ]
        if gated:
            sums.append((outs[4], pick(hot_t_ref[...], total * talls[-1][...])))
            low = (pick(hot_ref[...], flats[1][...]) * total).astype(BF16)
            column = jnp.sum(low.astype(F32), axis=0, keepdims=True)
        else:
            low = total.astype(BF16)
            column = jnp.sum(total, axis=0, keepdims=True)
        sums.append((column_ref, column))
        lows = outs[5:] if gated else outs[4:]
        if perms:
            for perm_ref, low_ref in zip(flats[2:], lows):
                low_ref[...] = matmul(low, perm_ref[...]).astype(BF16)
        else:
            lows[0][...] = low

        @pl.when(pl.program_id(0) == 0)
        def _():
            for ref, term in sums:
                ref[...] = term

        @pl.when(pl.program_id(0) > 0)
        def _():
            for ref, term in sums:
                ref[...] += term

    given = [hot, hot_t] + tall + flat
    specs = [by_tokens(hot), pl.BlockSpec((hot_t.shape[0], TOKENS), lambda j: (0, j))]
    specs += [by_tokens(part) for part in tall] + [whole(part) for part in flat]
    shape = jax.ShapeDtypeStruct
    image = shape(scale.shape, F32)
    outs = [shape((tokens, width), F32), image, image, shape((1, width), F32)]
    outs += [image] if gated else []
    outs += [shape((tokens, width), BF16) for _ in range(max(len(perms), 1))]
    out_specs = [by_tokens(part) if part.shape[0] == tokens else whole(part) for part in outs]
    return run(body, (tokens // TOKENS,), given, specs, outs, out_specs)


def slim_back(d_resid, token_hot, arrays, plan, perms, n_embed):
    width, wide = perms[0].shape[0], token_hot.shape[1]
    half = wide // 2
    rows = sum(arrays[which].shape[1] // width for which, _ in plan)
    room = rows + (-rows % 16)

    def body(d_ref, hot_ref, one_ref, two_ref, *refs):
        out_ref, gains = refs[-2], refs[-1]
        gains[...] = jnp.zeros_like(gains)
        at = 0
        for which, row in plan:
            for column in range(0, arrays[which].shape[1], width):
                gains[at : at + 1, :] = refs[which][row : row + 1, column : column + width]
                at += 1
        place = lax.broadcasted_iota(jnp.int32, (room, wide), 1)
        own = lax.broadcasted_iota(jnp.int32, (room, wide), 0) + n_embed
        own = jnp.where(own < n_embed + rows, own, -1)
        total = matmul_tn(d_ref[...], hot_ref[...])
        chosen = jnp.where(place == own, 1.0, 0.0).astype(BF16)
        total = total + matmul_tn(gains[...].astype(BF16), chosen)
        low = total.astype(BF16)
        out_ref[:, :half] = matmul(one_ref[...], low[:, :half]).astype(BF16)
        out_ref[:, half:] = matmul(two_ref[...], low[:, half:]).astype(BF16)

    given = [d_resid, token_hot] + list(perms) + list(arrays)
    outs = jax.ShapeDtypeStruct((width, wide), BF16)
    specs = [whole(value) for value in given]
    scratch = [pltpu.VMEM((room, width), F32)]
    return run(body, (1,), given, specs, outs, whole(outs), scratch)


def layout(scale_row):
    position = jnp.arange(scale_row.shape[0], dtype=jnp.int32)
    opening = scale_row == 0
    image_id = jnp.cumsum(opening.astype(jnp.int32)) - 1
    starts_at = lax.cummax(jnp.where(opening, position, 0), axis=0)
    return (image_id, position - starts_at, scale_row < LEVELS)


def adam_step(weight, moment, square, gradient, clip_factor, step_rate):
    gradient = gradient * clip_factor
    moment = BETA_ONE * moment + (1.0 - BETA_ONE) * gradient
    square = BETA_TWO * square + (1.0 - BETA_TWO) * gradient * gradient
    first_hat = moment / (1.0 - BETA_ONE**STEPS)
    second_hat = square / (1.0 - BETA_TWO**STEPS)
    weight = weight - step_rate * (first_hat / (jnp.sqrt(second_hat) + ADAM_EPS) + DECAY * weight)
    return (weight, moment, square, weight.astype(BF16))


def per_device(
    ways,
    features,
    scale_ids,
    class_ids,
    code_targets,
    token_weights,
    attn_weight,
    attn_moment,
    attn_square,
    mlp_weight,
    mlp_moment,
    mlp_square,
    ada_weight,
    ada_moment,
    ada_square,
    embed_weight,
    embed_moment,
    embed_square,
    gains_weight,
    gains_moment,
    gains_square,
    head_weight,
    head_moment,
    head_square,
):
    devices, n_vocab = ways["devices"], ways["n_vocab"]
    bits_y, bits_x, bits_z = ways["y"], ways["x"], ways["z"]
    path_one = bits_z + bits_y + bits_x
    path_two = bits_z + bits_x + bits_y
    me = lax.axis_index("dp") * n_vocab + lax.axis_index("vocab")
    rows = attn_weight.shape[0]
    width = rows * devices
    top, quarter = width // 2, width // 4
    ff_rows = FF // width
    ada_at = 7 + ff_rows
    head_at = ada_at + 8
    off_level = CLASSES + POSITIONS
    off_word = off_level + LEVELS
    length = scale_ids.shape[1]
    used = min(POSITIONS, length)
    n_gains = gains_weight.shape[0]
    n_embed = used + LEVELS + CHANNELS
    half_ff, half_qkv = FF // 2, 3 * width // 2

    def swap(value, mask):
        return swapped(value, mask, devices)

    def grown(masks, *values):
        for mask in masks:
            values = [grow(value, mask, devices) for value in values]
        return values if len(values) > 1 else values[0]

    scale_row = scale_ids[0]
    image_id, inside, counted = layout(scale_row)
    counted = counted.astype(F32)
    facts = jnp.concatenate(
        [class_ids[0], jnp.sum(counted).astype(jnp.int32)[None], jnp.zeros((119,), jnp.int32)]
    )[None]
    weighted = token_weights[0] * counted
    row_info = jnp.stack([code_targets[0].astype(F32), weighted])[None]

    embed16 = embed_weight.astype(BF16)
    slim = jnp.concatenate(
        [
            embed16[CLASSES : CLASSES + used],
            embed16[off_level : off_word + CHANNELS],
            gains_weight.astype(BF16),
        ],
        axis=0,
    )
    fill = -slim.shape[0] % 128
    slim = jnp.pad(slim, ((0, fill), (0, 0))).T
    wide = slim.shape[1]
    half_slim = wide // 2
    qkv_one = jnp.concatenate(
        [attn_weight[:, :half_qkv].astype(BF16), slim[:, :half_slim]], axis=1
    )
    qkv_two = jnp.concatenate(
        [attn_weight[:, half_qkv : 3 * width].astype(BF16), slim[:, half_slim:]], axis=1
    )
    up = jnp.concatenate(
        [
            mlp_weight[0, :, :half_ff],
            attn_weight[:, 3 * width : 3 * width + top],
            mlp_weight[0, :, half_ff:],
            attn_weight[:, 3 * width + top :],
        ],
        axis=1,
    ).astype(BF16)
    down = mlp_weight[1].astype(BF16)
    head16 = head_weight.astype(BF16)
    ada16 = ada_weight.astype(BF16)

    one_y, one_x, two_x, two_y = bits_y, bits_x, bits_x, bits_y
    slots = devices * MAXIMG
    n_x, n_y, n_z = 1 << len(bits_x), 1 << len(bits_y), 1 << len(bits_z)

    def to_two(value):
        shaped = value.reshape((2, n_x, n_y, n_z * MAXIMG) + value.shape[1:])
        return jnp.swapaxes(shaped, 1, 2).reshape(value.shape)

    def to_one(value):
        shaped = value.reshape((2, n_y, n_x, n_z * MAXIMG) + value.shape[1:])
        return jnp.swapaxes(shaped, 1, 2).reshape(value.shape)

    order = path_one + [1]
    groups = [order[at : at + 2] for at in range(0, len(order), 2)]
    parts = spread(facts, groups[0], devices)
    qkv_one, qkv_two = widen(qkv_one, bits_z[:1], devices), widen(qkv_two, bits_z[:1], devices)
    parts, qkv_one, qkv_two = tie(parts, qkv_one, qkv_two)
    parts = spread(stack(parts), groups[1], devices)
    qkv_one = widen(stack(qkv_one), bits_z[1:], devices)
    qkv_two = widen(stack(qkv_two), bits_z[1:], devices)
    parts, qkv_one, qkv_two, up, head16 = tie(parts, qkv_one, qkv_two, up, head16)
    for group in groups[2:]:
        parts = spread(stack(parts), group, devices)
    qkv_one, qkv_two = widen(stack(qkv_one), one_y, devices), widen(stack(qkv_two), two_x, devices)
    head16 = widen(head16, bits_y, devices)
    parts, up, me = tie(parts, up, me)

    facts = stack(parts)
    total_count = jnp.sum(facts[:, MAXIMG]).astype(F32)
    class_hot = (
        facts[:, :MAXIMG].reshape(slots)[:, None] == jnp.arange(CLASSES, dtype=jnp.int32)[None, :]
    ).astype(BF16)
    class_vec = matmul(class_hot, embed16[:CLASSES])
    class_act = jax.nn.silu(class_vec).astype(BF16)
    cuts = (2 * width, 5 * width)
    act_two = to_two(class_act)
    act_first = class_act.reshape(2, n_x, n_y, n_z, MAXIMG, rows)
    act_first = jnp.transpose(act_first, (0, 3, 1, 2, 4, 5)).reshape(slots, rows)
    path_first = bits_y + bits_x + bits_z
    first = matmul(act_first, ada16[:, : cuts[0]]).astype(BF16)
    first = lend(first, [1], devices)
    row_info = widen(row_info, bits_x, devices)
    first, row_info, me, head16 = tie(first, row_info, me, head16)
    perm_one, perm_one_t = hot_rows(source_rows(path_one + [1], me, rows))
    perm_two, perm_two_t = hot_rows(source_rows(path_two + [1], me, rows))
    for mask in reversed(bits_z):
        first = lend(added(*first), [mask], devices)
        (first,) = tie(first)
    first, qkv_one, qkv_two, up, row_info = tie(first, qkv_one, qkv_two, up, row_info)

    first = lend(added(*first), bits_x, devices)
    up = widen(up, bits_z[:1], devices)
    qkv_one, qkv_two = stack(qkv_one), stack(qkv_two)
    for mask in bits_x[:-1]:
        qkv_one = grow(qkv_one, mask, devices)
    for mask in bits_y[:-1]:
        qkv_two = grow(qkv_two, mask, devices)
    one_far, two_far = swap(qkv_one, bits_x[-1]), swap(qkv_two, bits_y[-1])
    row_info = widen(stack(row_info), [1], devices)
    first, row_info, qkv_one, qkv_two = tie(first, row_info, qkv_one, qkv_two)
    first = lend(added(*first), bits_y, devices)
    first, qkv_one, qkv_two, up = tie(first, qkv_one, qkv_two, up)
    first = added(*first, F32)
    up = widen(stack(up), bits_z[1:], devices)
    one_near_c, two_near_c = swap(qkv_one, 1), swap(qkv_two, 1)
    pos_hot = (inside[:, None] == jnp.arange(used, dtype=jnp.int32)[None, :]).astype(BF16)
    level_hot = (scale_row[:, None] == jnp.arange(LEVELS, dtype=jnp.int32)[None, :]).astype(BF16)
    token_hot = jnp.concatenate(
        [pos_hot, level_hot, features[0], jnp.zeros((length, wide - n_embed), BF16)], axis=1
    )
    image = jnp.arange(MAXIMG, dtype=jnp.int32)
    hot = (image_id[:, None] == image[None, :]).astype(BF16)
    hot_t = (image[:, None] == image_id[None, :]).astype(BF16)
    allowed = (image_id[:, None] == image_id[None, :]) & (scale_row[None, :] <= scale_row[:, None])
    mask_rows = jnp.where(allowed, 0.0, NEG_FILL).astype(F32)
    mods_rest = jnp.concatenate(
        [
            matmul(class_act, ada16[:, cuts[0] : cuts[1]]).astype(BF16),
            matmul(act_two, ada16[:, cuts[1] :]).astype(BF16),
        ],
        axis=1,
    )
    first, one_far, two_far, one_near_c, two_near_c, mods_rest, up, token_hot, mask_rows = tie(
        first, one_far, two_far, one_near_c, two_near_c, mods_rest, up, token_hot, mask_rows
    )
    row_info = jnp.swapaxes(stack(row_info), 0, 1).reshape(2, -1)

    one_far_c, two_far_c = swap(one_far, 1), swap(two_far, 1)
    mods_rest = lend(mods_rest, [1], devices)
    half_up = half_ff + top
    up = stack(up)
    up_one, up_two = widen(up[:, :half_up], one_y, devices), widen(up[:, half_up:], two_x, devices)
    one_far_c, two_far_c, mods_rest, first, down = tie(
        one_far_c, two_far_c, mods_rest, first, down
    )

    mods_rest = added(*mods_rest)
    cut = cuts[1] - cuts[0]
    mod_one = lend(mods_rest[:, :cut], bits_x, devices)
    mod_two = lend(mods_rest[:, cut:], bits_y, devices)
    down = widen(down, bits_z[:1], devices)
    blocks_one = [qkv_one, one_far, one_near_c, one_far_c]
    blocks_two = [qkv_two, two_far, two_near_c, two_far_c]
    slim = jnp.concatenate(
        [
            matmul_tn(stack([block[:, half_qkv:] for block in blocks_one]), perm_one),
            matmul_tn(stack([block[:, half_qkv:] for block in blocks_two]), perm_two),
        ],
        axis=0,
    )
    gain_rows = slim[n_embed : n_embed + n_gains]
    ada_bias = gain_rows[ada_at:head_at].reshape(1, -1)
    resid_in = matmul(token_hot, slim.astype(BF16)) + gain_rows[0]
    first = first + ada_bias[:, : cuts[0]]
    mods = [first[:, :width], first[:, width:]]
    u_one, u_two = norm_ahead(resid_in, hot, mods[0], mods[1], [perm_one_t, perm_two_t])
    w_qkv = ((blocks_one, (0, half_qkv)), (blocks_two, (0, half_qkv)))
    qkv_bias = jnp.concatenate(
        [gain_rows[1:2], jnp.zeros((1, width), F32), gain_rows[2:3]], axis=1
    )
    q_gain, k_gain = gain_rows[5:6], gain_rows[6:7]
    qkv = times_sets([u_one, u_two], w_qkv, qkv_bias)
    qkv, up_one, up_two, mod_one, mod_two, down, head16 = tie(
        qkv, up_one, up_two, mod_one, mod_two, down, head16
    )

    up_one, up_two = stack(up_one), stack(up_two)
    for mask in bits_x[:-1]:
        up_one = grow(up_one, mask, devices)
    for mask in bits_y[:-1]:
        up_two = grow(up_two, mask, devices)
    mod_one = lend(added(*mod_one), bits_y, devices)
    mod_two = lend(added(*mod_two), bits_x, devices)
    up_one_far, up_two_far = swap(up_one, bits_x[-1]), swap(up_two, bits_y[-1])
    down = widen(stack(down), bits_z[1:], devices)
    mixture = attend(qkv, q_gain, k_gain, mask_rows)
    mixture, mod_one, mod_two, down, up_one, up_two = tie(
        mixture, mod_one, mod_two, down, up_one, up_two
    )

    mods_rest = jnp.concatenate([added(*mod_one), added(*mod_two)], axis=1)
    mods_rest = lend(mods_rest, bits_z[-1:], devices)
    up_one_c, up_two_c = swap(up_one, 1), swap(up_two, 1)
    mix_one = matmul(mixture, perm_one_t).astype(BF16)
    mix_two = matmul(mixture, perm_two_t).astype(BF16)
    mix_one, mix_two, mods_rest, up_one_c, up_two_c, down = tie(
        mix_one, mix_two, mods_rest, up_one_c, up_two_c, down
    )
    mods_rest = lend(added(*mods_rest), bits_z[:-1], devices)
    down = stack(down)
    down_one = widen(down[:, :half_ff], one_y, devices)
    down_two = widen(down[:, half_ff:], two_x, devices)
    mix_one, mix_two, mods_rest, up_one_far, up_two_far, head16 = tie(
        mix_one, mix_two, mods_rest, up_one_far, up_two_far, head16
    )
    up_one_fc, up_two_fc = swap(up_one_far, 1), swap(up_two_far, 1)
    head16 = widen(stack(head16), bits_z[:1], devices)
    mix_one, mix_two, up_one_fc, up_two_fc = tie(mix_one, mix_two, up_one_fc, up_two_fc)
    blocks_one = [up_one, up_one_far, up_one_c, up_one_fc]
    blocks_two = [up_two, up_two_far, up_two_c, up_two_fc]
    w_up = ((blocks_one, (0, half_ff)), (blocks_two, (0, half_ff)))
    w_proj = ((blocks_one, (half_ff, half_up)), (blocks_two, (half_ff, half_up)))
    mods_rest = added(*mods_rest, F32) + ada_bias[:, cuts[0] :]
    mods += [mods_rest[:, at : at + width] for at in range(0, 6 * width, width)]
    attn_out = times_sets([mix_one, mix_two], w_proj, gain_rows[3:4])
    u_mid_one, u_mid_two, resid_mid = norm_ahead(
        resid_in, hot, mods[3], mods[4], [perm_one_t, perm_two_t], mods[2], attn_out
    )
    u_mid_one, u_mid_two, resid_mid, down_one, down_two = tie(
        u_mid_one, u_mid_two, resid_mid, down_one, down_two
    )
    down_one, down_two = stack(down_one), stack(down_two)
    for mask in bits_x[:-1]:
        down_one = grow(down_one, mask, devices)
    for mask in bits_y[:-1]:
        down_two = grow(down_two, mask, devices)
    down_one_far, down_two_far = swap(down_one, bits_x[-1]), swap(down_two, bits_y[-1])
    down_one_c, down_two_c = swap(down_one, 1), swap(down_two, 1)
    up_bias = gain_rows[7:ada_at].reshape(1, -1)
    hidden, active = times_sets([u_mid_one, u_mid_two], w_up, up_bias, bend=True)
    active, down_one_far, down_two_far, down_one_c, down_two_c, head16 = tie(
        active, down_one_far, down_two_far, down_one_c, down_two_c, head16
    )

    down_one_fc, down_two_fc = swap(down_one_far, 1), swap(down_two_far, 1)
    head16 = widen(stack(head16), bits_z[1:], devices)
    active, down_one_fc, down_two_fc = tie(active, down_one_fc, down_two_fc)
    w_down = (
        ([down_one, down_one_far, down_one_c, down_one_fc], None),
        ([down_two, down_two_far, down_two_c, down_two_fc], None),
    )
    perms = [perm_one, perm_two]
    mlp_out = back_sets(active[None], w_down, perms, gain_rows[4:5], exact=True)
    head_masks = bits_y + bits_z
    perm_head, perm_head_t = hot_rows(
        source_rows(
            [mask // n_vocab for mask in head_masks], lax.axis_index("dp"), head_weight.shape[0]
        )
    )
    head_rel, resid_out = norm_ahead(
        resid_mid, hot, mods[6], mods[7], [perm_head_t], mods[5], mlp_out
    )
    head_rel, head16 = tie(head_rel, head16)
    head16 = stack(head16)

    vocab_masks = bits_x + [1]
    rows_all = grown(bits_x[:-1], head_rel)
    far = swap(rows_all, bits_x[-1])
    near_c = swap(rows_all, 1)
    code_span = head_weight.shape[1]
    code_start = lax.axis_index("vocab") * code_span
    head_bias = lax.dynamic_slice_in_dim(gain_rows[head_at:].reshape(-1), code_start, code_span)
    code = jnp.arange(code_span, dtype=jnp.int32)[None, :] + code_start

    def part_stats(part, info):
        logits = matmul(part, head16) + head_bias
        local_max = jnp.max(logits, axis=1)
        exp_sums = jnp.sum(jnp.exp(logits - local_max[:, None]), axis=1)
        is_target = (code == info[0].astype(jnp.int32)[:, None]).astype(F32)
        picked = jnp.sum(is_target * logits, axis=1)
        return logits, is_target, jnp.stack([local_max, exp_sums, picked])

    each = rows_all.shape[0]
    info_of = [row_info[:, at * each : (at + 1) * each] for at in range(4)]
    near_rows = jnp.concatenate([rows_all, near_c], axis=0)
    near_info = jnp.concatenate([info_of[0], info_of[2]], axis=1)
    far_info = jnp.concatenate([info_of[1], info_of[3]], axis=1)
    near_logits, near_target, near_stats = part_stats(near_rows, near_info)
    near_stats, far = tie(near_stats, far)
    far_rows = jnp.concatenate([far, swap(far, 1)], axis=0)
    far_logits, far_target, far_stats = part_stats(far_rows, far_info)
    places = [x ^ c for x in (0, bits_x[-1]) for c in (0, 1)]
    places = [place ^ other for place in places for other in place_masks(bits_x[:-1])]
    stats = jnp.concatenate([near_stats, far_stats], axis=1)
    group = [stats]
    for other in place_masks(vocab_masks)[1:]:
        their = jnp.split(swap(stats, other), n_vocab, axis=1)
        group.append(
            jnp.concatenate([their[places.index(place ^ other)] for place in places], axis=1)
        )
    row_max = group[0][0]
    for other in group[1:]:
        row_max = jnp.maximum(row_max, other[0])
    totals = sum(other[1] * jnp.exp(other[0] - row_max) for other in group)
    target_logit = sum(other[2] for other in group)
    log_total = row_max + jnp.log(totals)
    loss_part = jnp.sum((near_info[1] * (log_total - target_logit)[: 2 * each])[:length])
    mid = 2 * each

    def part_back(logits, is_target, info, log_total):
        coef = info[1] / total_count
        grad = coef[:, None] * (jnp.exp(logits - log_total[:, None]) - is_target)
        return grad.astype(BF16)

    d_far_logits = part_back(far_logits, far_target, far_info, log_total[mid:])
    d_near_logits = part_back(near_logits, near_target, near_info, log_total[:mid])
    d_far = matmul_nt(d_far_logits, head16).astype(BF16)
    d_near = matmul_nt(d_near_logits, head16).astype(BF16)
    to_core = jnp.concatenate([d_near[each:], d_far[each:]], axis=0)
    back = swap(to_core, 1)
    d_far, d_near = added(d_far[:each], back[each:]), added(d_near[:each], back[:each])
    rows_all = jnp.concatenate([near_rows, far_rows], axis=0)
    d_logits = jnp.concatenate([d_near_logits, d_far_logits], axis=0)
    d_far, head16 = tie(d_far, head16)
    d_head_in = added(d_near, swap(d_far, bits_x[-1]), F32)
    for mask in reversed(bits_x[:-1]):
        d_head_in = keep_half(d_head_in.astype(BF16), mask, devices, F32)
    head_far = matmul_tn(rows_all[:, top:], d_logits).astype(BF16)
    head_near = matmul_tn(rows_all[:, :top], d_logits).astype(BF16)
    bias_grad = lax.dynamic_update_slice(
        jnp.zeros((V,), F32), jnp.sum(d_logits.astype(F32), axis=0), (code_start,)
    )
    d_head_in, head_far, head_near = tie(d_head_in, head_far, head_near)

    def cross(one, two):
        return swap(one, bits_x[-1]), swap(two, bits_y[-1])

    def join(one, two, one_back, two_back):
        one, two = added(one, one_back), added(two, two_back)
        for mask in reversed(bits_y[:-1]):
            two = keep_half(two, mask, devices)
        for mask in reversed(bits_x[:-1]):
            one = keep_half(one, mask, devices)
        half = one.shape[0] // 2
        return tuple(
            jnp.concatenate([one[at : at + half], two[at : at + half]], axis=1) for at in (0, half)
        )

    def turn(one, two, one_back, two_back):
        one, one_far = halves_of(one, one_back)
        two, two_far = halves_of(two, two_back)
        for mask in reversed(bits_x[:-1]):
            whole_one = jnp.concatenate([one, one_far], axis=0)
            one, one_far = halves_of(
                whole_one[: whole_one.shape[0] // 2],
                swap(whole_one[whole_one.shape[0] // 2 :], mask),
            )
        for mask in reversed(bits_y[:-1]):
            whole_two = jnp.concatenate([two, two_far], axis=0)
            two, two_far = halves_of(
                whole_two[: whole_two.shape[0] // 2],
                swap(whole_two[whole_two.shape[0] // 2 :], mask),
            )
        return one, one_far, two, two_far

    def cross_back(one_far, two_far):
        return swap(one_far, bits_y[-1]), swap(two_far, bits_x[-1])

    perms = [perm_one, perm_two]
    ones, twos = (0, half_ff), (half_ff, FF)
    q_ones, q_twos = (0, half_qkv), (half_qkv, 3 * width)
    downs, ups = [None, None], [u_mid_one, u_mid_two]
    mixes, ins = [mix_one, mix_two], [u_one, u_two]
    ffs, projs, qkvs = [ones, twos], [(0, top), (top, width)], [q_ones, q_twos]

    active = active[None]
    head_back = swap(head_far, head_masks[-1])
    d_head_in = in_halves_outside(lambda part: matmul(part, perm_head), d_head_in)
    d_resid_out, d_shift_head, d_scale_head, down_bias, d_gate_two, *downs = norm_back(
        resid_out,
        d_head_in,
        hot,
        hot_t,
        mods[7],
        gate=mods[5],
        branch=mlp_out,
        perms=[perm_one_t, perm_two_t],
    )
    down_f = grad_sets(downs, active, ffs)
    downs, down_f = tie(downs, down_f)
    down_b = swap(down_f, 1)
    d_hid, up_bias_sum = times_sets(downs, w_down, hidden=hidden)
    d_hid, down_b = tie(d_hid, down_b)
    d_hid = d_hid[None]
    down_n1, down_f1, down_n2, down_f2 = grad_sets(downs, active, ffs, down_b)
    up_f = grad_sets(ups, d_hid, ffs)
    d_hid, down_f1, down_f2, down_n1, down_n2, up_f = tie(
        d_hid, down_f1, down_f2, down_n1, down_n2, up_f
    )
    down_x1, down_x2 = cross(down_f1, down_f2)
    up_b = swap(up_f, 1)
    d_u = back_sets(d_hid, w_up, perms)
    d_u, up_b = tie(d_u, up_b)
    up_n1, up_f1, up_n2, up_f2 = grad_sets(ups, d_hid, ffs, up_b)
    d_resid_mid, d_shift_two, d_scale_two, proj_bias, d_gate_one, d_low = norm_back(
        resid_mid, d_u, hot, hot_t, mods[4], beyond=d_resid_out, gate=mods[2], branch=attn_out
    )
    d_low, down_x1, down_x2, up_f1, up_f2, up_n1, up_n2, head_back, head_near = tie(
        d_low, down_x1, down_x2, up_f1, up_f2, up_n1, up_n2, head_back, head_near
    )
    down_n1, down_f1, down_n2, down_f2 = turn(down_n1, down_n2, down_x1, down_x2)
    d_low, down_f1, down_f2, up_f1, up_f2, head_back = tie(
        d_low, down_f1, down_f2, up_f1, up_f2, head_back
    )
    head_near, head_far = halves_of(head_near, head_back)
    down_x1, down_x2 = cross_back(down_f1, down_f2)
    up_x1, up_x2 = cross(up_f1, up_f2)
    head_back = swap(head_far, head_masks[-2])
    d_low = d_low[None]
    proj_f = grad_sets(mixes, d_low, projs)
    d_mix = back_sets(d_low, w_proj, perms, out=BF16)
    d_qkv, attn_sums = attend_back(qkv, q_gain, k_gain, mask_rows, d_mix)
    d_qkv, proj_f, down_x1, down_x2, down_n1, down_n2, up_x1, up_x2, head_back, head_near = tie(
        d_qkv, proj_f, down_x1, down_x2, down_n1, down_n2, up_x1, up_x2, head_back, head_near
    )
    up_n1, up_f1, up_n2, up_f2 = turn(up_n1, up_n2, up_x1, up_x2)
    down_near, down_far = join(down_n1, down_n2, down_x1, down_x2)
    d_qkv, up_f1, up_f2, down_far, proj_f = tie(d_qkv, up_f1, up_f2, down_far, proj_f)
    up_x1, up_x2 = cross_back(up_f1, up_f2)
    down_back = swap(down_far, bits_z[-1])
    proj_b = swap(proj_f, 1)
    qkv_f = grad_sets(ins, d_qkv, qkvs)
    d_qkv, qkv_f, proj_b = tie(d_qkv, qkv_f, proj_b)
    qkv_b = swap(qkv_f, 1)
    head_near = added(head_near, head_back)
    head_grad = lend(head_near, head_masks[:-2], devices)
    d_u = back_sets(d_qkv, w_qkv, perms)
    d_u, qkv_b, up_x1, up_x2, down_back, down_near, head_grad = tie(
        d_u, qkv_b, up_x1, up_x2, down_back, down_near, head_grad
    )
    head_grad = added(*head_grad, F32)
    down_near, down_far = halves_of(down_near, down_back)
    d_u, down_far, qkv_b, up_x1, up_x2 = tie(d_u, down_far, qkv_b, up_x1, up_x2)
    down_back = swap(down_far, bits_z[-2])
    d_resid_in, d_shift_one, d_scale_one, word_bias, d_res16 = norm_back(
        resid_in, d_u, hot, hot_t, mods[1], beyond=d_resid_mid
    )
    d_mod = jnp.concatenate(
        [
            d_shift_one,
            d_scale_one,
            d_gate_one,
            d_shift_two,
            d_scale_two,
            d_gate_two,
            d_shift_head,
            d_scale_head,
        ],
        axis=1,
    ).astype(BF16)
    ada_sums = jnp.sum(d_mod.astype(F32), axis=0, keepdims=True)
    arrays = [word_bias, attn_sums, proj_bias, down_bias, up_bias_sum, ada_sums, bias_grad[None]]
    plan = [(0, 0), (1, 2), (1, 3), (2, 0), (3, 0), (1, 0), (1, 1), (4, 0), (5, 0), (6, 0)]
    d_slim = slim_back(d_res16, token_hot, arrays, plan, perms, n_embed)
    d_slim, d_mod, qkv_b = tie(d_slim, d_mod, qkv_b)
    slim_b = swap(d_slim[top:], 1)
    qkv_n1, qkv_f1, qkv_n2, qkv_f2 = grad_sets(ins, d_qkv, qkvs, qkv_b)
    proj_n1, proj_f1, proj_n2, proj_f2 = grad_sets(mixes, d_low, projs, proj_b)
    (
        qkv_n1,
        qkv_f1,
        qkv_n2,
        qkv_f2,
        proj_n1,
        proj_f1,
        proj_n2,
        proj_f2,
        slim_b,
        down_back,
        up_x1,
        up_x2,
    ) = tie(
        qkv_n1,
        qkv_f1,
        qkv_n2,
        qkv_f2,
        proj_n1,
        proj_f1,
        proj_n2,
        proj_f2,
        slim_b,
        down_back,
        up_x1,
        up_x2,
    )

    def beside(*parts):
        return jnp.concatenate(parts, axis=1)

    far_slim = added(d_slim[quarter:top], slim_b[quarter:])
    qkv_f1 = beside(qkv_f1, proj_f1, far_slim[:, :half_slim])
    qkv_f2 = beside(qkv_f2, proj_f2, far_slim[:, half_slim:])
    up_near, up_far = join(up_n1, up_n2, up_x1, up_x2)
    d_mod, up_far, qkv_f1, qkv_f2 = tie(d_mod, up_far, qkv_f1, qkv_f2)
    qkv_x1, qkv_x2 = cross(qkv_f1, qkv_f2)
    up_back = swap(up_far, bits_z[-1])
    all_mod = widen(d_mod, bits_z, devices)
    near_slim = added(d_slim[:quarter], slim_b[:quarter])
    qkv_n1 = beside(qkv_n1, proj_n1, near_slim[:, :half_slim])
    qkv_n2 = beside(qkv_n2, proj_n2, near_slim[:, half_slim:])
    qkv_x1, qkv_x2, qkv_n1, qkv_n2, all_mod, up_back, up_near = tie(
        qkv_x1, qkv_x2, qkv_n1, qkv_n2, all_mod, up_back, up_near
    )
    qkv_n1, qkv_f1, qkv_n2, qkv_f2 = turn(qkv_n1, qkv_n2, qkv_x1, qkv_x2)
    up_near, up_far = halves_of(up_near, up_back)
    qkv_x1, qkv_x2 = cross_back(qkv_f1, qkv_f2)
    up_back = swap(up_far, bits_z[-2])
    all_mod = stack(all_mod)
    all_first = widen(all_mod[:, : cuts[1]], bits_y, devices)
    all_two = widen(all_mod[:, cuts[1] :], bits_x, devices)
    qkv_x1, qkv_x2, qkv_n1, qkv_n2, up_back, all_first, all_two = tie(
        qkv_x1, qkv_x2, qkv_n1, qkv_n2, up_back, all_first, all_two
    )
    near, far = join(qkv_n1, qkv_n2, qkv_x1, qkv_x2)
    attn_back = swap(far, bits_z[-1])
    all_two = widen(stack(all_two), bits_y, devices)
    all_first = widen(stack(all_first), bits_x, devices)
    attn_back, near, all_two, all_first = tie(attn_back, near, all_two, all_first)
    near, far = halves_of(near, attn_back)
    attn_back = swap(far, bits_z[-2])
    all_two = grown([1], stack(all_two))
    all_first = grown([1], stack(all_first))

    def close(near, back):
        masks = bits_z[:-2]
        near = added(near, back, BF16 if masks else F32)
        return keep_all(near, masks, devices)

    up_rows, down_rows = close(up_near, up_back), close(down_near, down_back)
    mlp_grad = jnp.stack([up_rows, down_rows])
    ada_grad = jnp.concatenate([matmul_tn(class_act, all_first), matmul_tn(act_two, all_two)], axis=1)
    d_class_act = matmul_nt(all_first, ada16[:, : cuts[1]]) + to_one(
        matmul_nt(all_two, ada16[:, cuts[1] :])
    )
    _, silu_back = jax.vjp(jax.nn.silu, class_vec)
    d_class = precise_tn(class_hot.astype(F32), silu_back(d_class_act)[0])
    squares_local = jnp.zeros((), F32)
    for gradient in (mlp_grad, ada_grad, d_class, head_grad):
        squares_local = squares_local + jnp.sum(gradient * gradient)
    squares_local, mlp_grad, ada_grad, d_class, near, attn_back = tie(
        squares_local, mlp_grad, ada_grad, d_class, near, attn_back
    )
    attn_rows = close(near, attn_back)
    squares_local = squares_local + jnp.sum(attn_rows * attn_rows)
    half_attn = half_qkv + top
    half_all = half_attn + half_slim
    attn_grad = jnp.concatenate(
        [
            attn_rows[:, :half_qkv],
            attn_rows[:, half_all : half_all + half_qkv],
            attn_rows[:, half_qkv:half_attn],
            attn_rows[:, half_all + half_qkv : half_all + half_attn],
        ],
        axis=1,
    )
    slim_grad = jnp.concatenate(
        [attn_rows[:, half_attn:half_all], attn_rows[:, half_all + half_attn :]], axis=1
    ).T
    embed_grad = jnp.concatenate(
        [
            d_class,
            slim_grad[:used],
            jnp.zeros((POSITIONS - used, rows), F32),
            slim_grad[used:n_embed],
        ],
        axis=0,
    )
    gains_grad = slim_grad[n_embed : n_embed + n_gains]
    gradients = (attn_grad, mlp_grad, ada_grad, embed_grad, gains_grad, head_grad)
    sums = sum_all(
        jnp.stack([squares_local, loss_part])[None], [1] + bits_x + bits_y + bits_z, devices
    )
    total_sq, loss_sum = sums[0, 0], sums[0, 1]
    grad_norm = jnp.sqrt(total_sq)
    clip_factor = jnp.minimum(1.0, CLIP_NORM / (grad_norm + 1e-06))
    masters = (attn_weight, mlp_weight, ada_weight, embed_weight, gains_weight, head_weight)
    moments = (attn_moment, mlp_moment, ada_moment, embed_moment, gains_moment, head_moment)
    squares = (attn_square, mlp_square, ada_square, embed_square, gains_square, head_square)
    updates = []
    for number in range(6):
        updates.extend(
            adam_step(
                masters[number],
                moments[number],
                squares[number],
                gradients[number],
                clip_factor,
                RATES[number],
            )
        )
    return tuple(updates) + (grad_norm, loss_sum, total_count)


def solution(mesh):
    n_dp, n_vocab = mesh.shape["dp"], mesh.shape["vocab"]
    n_z = 1 << (n_dp.bit_length() // 2)
    devices = n_dp * n_vocab

    def bits(least, top):
        found = []
        while least < top:
            found, least = [least] + found, least * 2
        return found

    ways = {"devices": devices, "n_vocab": n_vocab}
    ways["x"] = bits(2, n_vocab)
    ways["y"] = bits(n_vocab, devices // n_z)
    ways["z"] = bits(devices // n_z, devices)
    every = ("dp", "vocab")
    by_row = P(every, None)
    by_mid = P(None, every, None)
    by_column = P(None, every)
    head = P("dp", "vocab")
    placed = (P(every, None, None), by_row, by_row, by_row, by_row)
    for spec in (by_row, by_mid, by_row, by_column, by_column, head):
        placed = placed + (spec,) * 3
    given = ()
    for spec in (by_row, by_mid, by_row, by_column, by_column, head):
        given = given + (spec,) * 4

    def step(*arrays):
        return per_device(ways, *arrays)

    return jax.shard_map(
        step, mesh=mesh, in_specs=placed, out_specs=given + (P(), P(), P()), check_vma=False
    )
```

```python
import jax
import jax.numpy as jnp
from jax import lax
from jax.experimental import pallas as pl
from jax.experimental.pallas import tpu as pltpu
from jax.sharding import PartitionSpec as P

HEADS = 16
HEAD_DIM = 64
FF = 4096
V = 4096
CHANNELS = 32
CLASSES = 1001
POSITIONS = 680
LEVELS = 10
MAXIMG = 8
STEPS = 10


EPS_NORM = 1e-06
BETA_ONE = 0.9
BETA_TWO = 0.95
ADAM_EPS = 1e-08
DECAY = 0.05
CLIP_NORM = 0.001
RATES = (0.03, 0.03, 0.03, 0.15, 0.4, 0.03)
NEG_FILL = -1e30
BF16 = jnp.bfloat16
F32 = jnp.float32
SPANS = (1024, 512)
TOKENS = 128
PAIR = 2 * HEAD_DIM


def matmul(left, right):
    return jnp.dot(left, right, preferred_element_type=F32)


def matmul_tn(left, right):
    return lax.dot_general(left, right, (((0,), (0,)), ((), ())), preferred_element_type=F32)


def matmul_nt(left, right):
    return lax.dot_general(left, right, (((1,), (1,)), ((), ())), preferred_element_type=F32)


def precise_tn(left, right):
    return lax.dot_general(left, right, (((0,), (0,)), ((), ())), precision=lax.Precision.HIGHEST)


def pick(hot, values):
    return in_halves(lambda part: matmul(hot, part), values)


def in_halves(times, values):
    upper = values.astype(BF16)
    return times(upper) + times((values - upper.astype(F32)).astype(BF16))


def in_halves_outside(times, values):
    upper = lax.reduce_precision(values, 8, 7)
    return times(upper.astype(BF16)) + times((values - upper).astype(BF16))


def swapped(value, mask, devices):
    return lax.ppermute(value, ("dp", "vocab"), [(i, i ^ mask) for i in range(devices)])


def tie(*values):
    return lax.optimization_barrier(values)


def grow(value, mask, devices):
    return jnp.concatenate([value, swapped(value, mask, devices)], axis=0)


def spread(value, masks, devices):
    if len(masks) == 2:
        masks = masks + [masks[0] ^ masks[1]]
    return [value] + [swapped(value, mask, devices) for mask in masks]


def stack(parts):
    return jnp.concatenate(parts, axis=0)


def widen(value, masks, devices):
    for mask in masks[:-1]:
        value = grow(value, mask, devices)
    return [value, swapped(value, masks[-1], devices)]


def added(mine, theirs, out=BF16):
    return (mine.astype(F32) + theirs.astype(F32)).astype(out)


def keep_half(value, mask, devices, out=BF16):
    half = value.shape[0] // 2
    return added(value[:half], swapped(value[half:].astype(BF16), mask, devices), out)


def lend(value, masks, devices):
    for mask in reversed(masks[1:]):
        value = keep_half(value, mask, devices)
    half = value.shape[0] // 2
    return [value[:half], swapped(value[half:].astype(BF16), masks[0], devices)]


def keep_all(value, masks, devices):
    for mask in reversed(masks):
        value = keep_half(value, mask, devices, F32 if mask == masks[0] else BF16)
    return value


def halves_of(mine, back, out=BF16):
    half = mine.shape[0] // 2
    return (added(mine[:half], back[:half], out), added(mine[half:], back[half:], out))


def sum_all(value, bits, devices):
    for at in range(0, len(bits), 2):
        masks = place_masks(bits[at : at + 2])[1:]
        value = value + sum(swapped(value, mask, devices) for mask in masks)
    return value


def place_masks(masks):
    places = [0]
    for mask in masks:
        places = places + [place ^ mask for place in places]
    return places


def source_rows(masks, me, rows):
    differ = jnp.repeat(jnp.array(place_masks(masks), jnp.int32), rows)
    row = jnp.tile(jnp.arange(rows, dtype=jnp.int32), 1 << len(masks))
    return (differ ^ me) * rows + row


def hot_rows(source):
    place = jnp.arange(source.shape[0], dtype=jnp.int32)
    return (
        (source[:, None] == place[None, :]).astype(BF16),
        (place[:, None] == source[None, :]).astype(BF16),
    )


def run(body, grid, given, specs, outs, out_specs, scratch=()):
    return pl.pallas_call(
        body,
        grid=grid,
        in_specs=specs,
        out_shape=outs,
        out_specs=out_specs,
        scratch_shapes=scratch,
        compiler_params=pltpu.CompilerParams(vmem_limit_bytes=24 << 20),
        cost_estimate=pl.CostEstimate(flops=1000, bytes_accessed=1000, transcendentals=0),
    )(*given)


def whole(value):
    return pl.BlockSpec(value.shape, lambda j: (0,) * value.ndim)


def span_of(*sizes):
    return [span for span in SPANS if all(size % span == 0 for size in sizes)][0]


def columns_of(sets):
    return [blocks[0].shape[1] if used is None else used[1] - used[0] for blocks, used in sets]


def starts_of(sets):
    return [0 if used is None else used[0] for _, used in sets]


def two_sets(sets, first, span):
    one, two = [start // span for start in starts_of(sets)]
    specs = [
        pl.BlockSpec((block.shape[0], span), lambda j: (0, one + jnp.minimum(j, first - 1)))
        for block in sets[0][0]
    ]
    specs += [
        pl.BlockSpec((block.shape[0], span), lambda j: (0, two + jnp.maximum(j - first, 0)))
        for block in sets[1][0]
    ]
    return specs


def gelu_parts(value):
    inner = 0.7978845608028654 * (value + 0.044715 * (value * value * value))
    bend = jnp.tanh(inner)
    return bend


def gelu(value):
    return 0.5 * value * (1.0 + gelu_parts(value))


def gelu_slope(value):
    bend = gelu_parts(value)
    rise = 0.7978845608028654 * (1.0 + 3.0 * 0.044715 * value * value)
    return 0.5 * (1.0 + bend) + 0.5 * value * (1.0 - bend * bend) * rise


def times_sets(left, sets, bias=None, hidden=None, bend=False):
    tokens = left[0].shape[0]
    columns = columns_of(sets)
    span = span_of(*columns, *starts_of(sets))
    first, steps = columns[0] // span, sum(columns) // span
    specs = two_sets(sets, first, span)
    count = len(sets[0][0])
    extra = [value for value in (bias, hidden) if value is not None]
    column = lambda j: (0, j)
    extra_specs = [pl.BlockSpec((value.shape[0], span), column) for value in extra]

    def body(one_ref, two_ref, *refs):
        extras, blocks = refs[: len(extra)], refs[len(extra) : len(extra) + 2 * count]
        outs = refs[len(extra) + 2 * count :]

        def part(u_ref, blocks):
            total, at = None, 0
            for block in blocks:
                rows = block.shape[0]
                term = matmul(u_ref[:, at : at + rows], block[...])
                total = term if total is None else total + term
                at += rows
            if bias is not None:
                total = total + extras[0][...]
            if hidden is not None:
                slope = gelu_slope(extras[-1][...])
                low = (total * slope).astype(BF16)
                outs[0][...] = low
                outs[1][...] = jnp.sum(low.astype(F32), axis=0, keepdims=True)
            else:
                outs[0][...] = total
                if bend:
                    outs[1][...] = gelu(total).astype(BF16)

        pl.when(pl.program_id(0) < first)(lambda: part(one_ref, blocks[:count]))
        pl.when(pl.program_id(0) >= first)(lambda: part(two_ref, blocks[count:]))

    wide = steps * span
    shape = jax.ShapeDtypeStruct
    outs, out_specs = [shape((tokens, wide), F32)], [pl.BlockSpec((tokens, span), column)]
    if hidden is not None:
        outs = [shape((tokens, wide), BF16), shape((1, wide), F32)]
        out_specs.append(pl.BlockSpec((1, span), column))
    elif bend:
        outs.append(shape((tokens, wide), BF16))
        out_specs.append(pl.BlockSpec((tokens, span), column))
    given = list(left) + extra + list(sets[0][0]) + list(sets[1][0])
    specs = [whole(value) for value in left] + extra_specs + specs
    found = run(body, (steps,), given, specs, outs, out_specs)
    return found if len(outs) > 1 else found[0]


def span_spec(value, span):
    each = value.shape[2] // span
    return pl.BlockSpec((1, value.shape[1], span), lambda j: (j // each, 0, j % each))


def back_sets(right, sets, perms, bias=None, exact=False, out=F32):
    tokens = right.shape[1]
    columns = columns_of(sets)
    span = span_of(right.shape[2], *columns, *starts_of(sets))
    first, steps = columns[0] // span, sum(columns) // span
    specs = two_sets(sets, first, span)
    count = len(sets[0][0])
    width = perms[0].shape[0]
    extra = [] if bias is None else [bias]

    def body(right_ref, one_ref, two_ref, *refs):
        extras, blocks = refs[: len(extra)], refs[len(extra) : len(extra) + 2 * count]
        out_ref, one_sum, two_sum = refs[len(extra) + 2 * count :]
        step = pl.program_id(0)

        def part(sums, blocks, start):
            terms = [matmul_nt(right_ref[0], block[...]) for block in blocks]
            term = jnp.concatenate(terms, axis=1)

            @pl.when(step == start)
            def _():
                sums[...] = term

            @pl.when(step > start)
            def _():
                sums[...] += term

        pl.when(step < first)(lambda: part(one_sum, blocks[:count], 0))
        pl.when(step >= first)(lambda: part(two_sum, blocks[count:], first))

        @pl.when(step == steps - 1)
        def _():
            total = None
            for sums, perm in ((one_sum, one_ref), (two_sum, two_ref)):
                if exact:
                    term = in_halves(lambda part: matmul(part, perm[...]), sums[...])
                else:
                    term = matmul(sums[...].astype(BF16), perm[...])
                total = term if total is None else total + term
            if bias is not None:
                total = total + extras[0][...]
            out_ref[...] = total.astype(out)

    given = [right] + list(perms) + extra + list(sets[0][0]) + list(sets[1][0])
    specs = [span_spec(right, span)] + [whole(value) for value in list(perms) + extra] + specs
    outs = jax.ShapeDtypeStruct((tokens, width), out)
    scratch = [pltpu.VMEM((tokens, width), F32)] * 2
    return run(body, (steps,), given, specs, outs, whole(outs), scratch)


def grad_sets(left, right, columns, back=None):
    tokens, width = left[0].shape
    parts = 2 if back is not None else 1
    half = width // 2
    count = half // parts
    wide = [stop - start for start, stop in columns]
    span = span_of(right.shape[2], *wide, *[start for start, _ in columns])
    each = right.shape[2] // span
    first, steps = wide[0] // span, sum(wide) // span
    at = [start // span for start, _ in columns]

    def place(j):
        block = jnp.where(j < first, j + at[0], j - first + at[1])
        return (block // each, 0, block % each)

    def body(one_ref, two_ref, right_ref, *refs):
        def part(left_ref, outs):
            total = matmul_tn(left_ref[...], right_ref[0])
            if back is not None:
                total = total + refs[0][...].astype(F32)
            for which, out in enumerate(outs):
                out[...] = total[which * count : (which + 1) * count].astype(BF16)

        step = pl.program_id(0)
        if back is None:
            pl.when(step < first)(lambda: part(one_ref, refs))
            pl.when(step >= first)(lambda: part(two_ref, refs))
        else:
            pl.when(step < first)(lambda: part(one_ref, refs[1:3]))
            pl.when(step >= first)(lambda: part(two_ref, refs[3:]))

    side = 0 if back is not None else 1
    given = list(left) + [right]
    specs = [pl.BlockSpec((tokens, half), lambda j: (0, side)) for _ in left]
    specs.append(pl.BlockSpec((1, tokens, span), place))
    own = pl.BlockSpec((half, span), lambda j: (0, j))
    if back is None:
        outs = jax.ShapeDtypeStruct((half, sum(wide)), BF16)
        return run(body, (steps,), given, specs, outs, own)
    outs, out_specs = [], []
    indices = (lambda j: (0, jnp.minimum(j, first - 1)), lambda j: (0, jnp.maximum(j - first, 0)))
    for size, index in zip(wide, indices):
        outs += [jax.ShapeDtypeStruct((count, size), BF16)] * 2
        out_specs += [pl.BlockSpec((count, span), index)] * 2
    return run(body, (steps,), given + [back], specs + [own], outs, out_specs)


def head_scale(value, left_half):
    square = value * value
    one = jnp.sum(jnp.where(left_half, square, 0.0), axis=1, keepdims=True)
    two = jnp.sum(jnp.where(left_half, 0.0, square), axis=1, keepdims=True)
    return jnp.where(
        left_half,
        lax.rsqrt(one * (1.0 / HEAD_DIM) + EPS_NORM),
        lax.rsqrt(two * (1.0 / HEAD_DIM) + EPS_NORM),
    )


def soft_rows(q_norm, k_norm, mask):
    scores = matmul_nt(q_norm, k_norm) * HEAD_DIM ** (-0.5) + mask
    terms = jnp.exp(scores - jnp.max(scores, axis=1, keepdims=True))
    return terms * (1.0 / jnp.sum(terms, axis=1, keepdims=True))


def pair_specs(tokens):
    pairs = HEADS // 2
    return [
        pl.BlockSpec((tokens, PAIR), lambda j: (0, j)),
        pl.BlockSpec((tokens, PAIR), lambda j: (0, pairs + j)),
        pl.BlockSpec((tokens, PAIR), lambda j: (0, 2 * pairs + j)),
        pl.BlockSpec((1, PAIR), lambda j: (0, j)),
        pl.BlockSpec((1, PAIR), lambda j: (0, j)),
        pl.BlockSpec((tokens, tokens), lambda j: (0, 0)),
    ]


def attend(qkv, q_gain, k_gain, mask):
    tokens, width = qkv.shape[0], qkv.shape[1] // 3

    def body(q_ref, k_ref, v_ref, qg_ref, kg_ref, mask_ref, out_ref):
        left_half = lax.broadcasted_iota(jnp.int32, (1, PAIR), 1) < HEAD_DIM
        query, key = q_ref[...], k_ref[...]
        q_norm = (query * head_scale(query, left_half) * qg_ref[...]).astype(BF16)
        k_norm = (key * head_scale(key, left_half) * kg_ref[...]).astype(BF16)
        v_low = v_ref[...].astype(BF16)
        zero = jnp.zeros_like(q_norm)
        mixed = []
        for one in (jnp.where(left_half, q_norm, zero), jnp.where(left_half, zero, q_norm)):
            probs = soft_rows(one, k_norm, mask_ref[...])
            mixed.append(matmul(probs.astype(BF16), v_low))
        out_ref[...] = jnp.where(left_half, mixed[0], mixed[1]).astype(BF16)

    outs = jax.ShapeDtypeStruct((tokens, width), BF16)
    spec = pl.BlockSpec((tokens, PAIR), lambda j: (0, j))
    given = [qkv, qkv, qkv, q_gain, k_gain, mask]
    return run(body, (HEADS // 2,), given, pair_specs(tokens), outs, spec)


def attend_back(qkv, q_gain, k_gain, mask, d_mix):
    tokens, width = qkv.shape[0], qkv.shape[1] // 3

    def body(q_ref, k_ref, v_ref, qg_ref, kg_ref, mask_ref, dm_ref, out_ref, sums_ref):
        left_half = lax.broadcasted_iota(jnp.int32, (1, PAIR), 1) < HEAD_DIM
        query, key = q_ref[...], k_ref[...]
        q_scale, k_scale = head_scale(query, left_half), head_scale(key, left_half)
        q_norm = (query * q_scale * qg_ref[...]).astype(BF16)
        k_norm = (key * k_scale * kg_ref[...]).astype(BF16)
        v_low, d_mix = v_ref[...].astype(BF16), dm_ref[...]
        zero = jnp.zeros_like(q_norm)
        found = []
        for side in range(2):
            own = (lambda v: jnp.where(left_half, v, zero)) if side == 0 else (
                lambda v: jnp.where(left_half, zero, v)
            )
            probs = soft_rows(own(q_norm), k_norm, mask_ref[...])
            d_values = matmul_tn(probs.astype(BF16), d_mix)
            d_probs = matmul_nt(own(d_mix), v_low)
            inner = jnp.sum(d_probs * probs, axis=1, keepdims=True)
            d_scores = (probs * (d_probs - inner)).astype(BF16)
            found.append((matmul(d_scores, k_norm), matmul_tn(d_scores, q_norm), d_values))
        d_qn, d_kn, d_values = (jnp.where(left_half, one, two) for one, two in zip(*found))
        sums = []
        for at, value, scale, gain, d_norm in (
            (0, query, q_scale, qg_ref[...], d_qn * HEAD_DIM ** (-0.5)),
            (1, key, k_scale, kg_ref[...], d_kn * HEAD_DIM ** (-0.5)),
        ):
            product = d_norm * value
            sums.append(jnp.sum(product * scale, axis=0, keepdims=True))
            product = product * gain
            one = jnp.sum(jnp.where(left_half, product, 0.0), axis=1, keepdims=True)
            two = jnp.sum(jnp.where(left_half, 0.0, product), axis=1, keepdims=True)
            mean = jnp.where(left_half, one, two) * (1.0 / HEAD_DIM)
            d_value = scale * (gain * d_norm - value * (scale * scale) * mean)
            out_ref[at] = d_value.astype(BF16)
        out_ref[2] = d_values.astype(BF16)
        sums.append(jnp.sum(out_ref[0].astype(F32), axis=0, keepdims=True))
        sums.append(jnp.sum(out_ref[2].astype(F32), axis=0, keepdims=True))
        sums_ref[...] = jnp.concatenate(sums + [jnp.zeros((4, PAIR), F32)], axis=0)

    outs = [
        jax.ShapeDtypeStruct((3, tokens, width), BF16),
        jax.ShapeDtypeStruct((8, width), F32),
    ]
    out_specs = [
        pl.BlockSpec((3, tokens, PAIR), lambda j: (0, 0, j)),
        pl.BlockSpec((8, PAIR), lambda j: (0, j)),
    ]
    given = [qkv, qkv, qkv, q_gain, k_gain, mask, d_mix]
    specs = pair_specs(tokens) + [pl.BlockSpec((tokens, PAIR), lambda j: (0, j))]
    return run(body, (HEADS // 2,), given, specs, outs, out_specs)


def row_stats(value):
    center = value - jnp.mean(value, axis=1, keepdims=True)
    return center, lax.rsqrt(jnp.mean(center * center, axis=1, keepdims=True) + EPS_NORM)


def by_tokens(value):
    return pl.BlockSpec((TOKENS, value.shape[1]), lambda j: (j, 0))


def norm_ahead(value, hot, shift, scale, perms, gate=None, branch=None):
    tokens, width = value.shape
    extra = [] if gate is None else [gate, branch]

    def body(value_ref, hot_ref, shift_ref, scale_ref, *refs):
        total = value_ref[...]
        outs = refs[len(extra) + len(perms) :]
        if gate is not None:
            total = total + pick(hot_ref[...], refs[0][...]) * refs[1][...]
            outs[-1][...] = total
        center, inverse = row_stats(total)
        scales = 1.0 + pick(hot_ref[...], scale_ref[...])
        normed = center * inverse * scales + pick(hot_ref[...], shift_ref[...])
        normed = normed.astype(BF16)
        for perm_ref, out_ref in zip(refs[len(extra) : len(extra) + len(perms)], outs):
            out_ref[...] = matmul(normed, perm_ref[...]).astype(BF16)

    given = [value, hot, shift, scale] + extra + list(perms)
    specs = [by_tokens(value), by_tokens(hot), whole(shift), whole(scale)]
    specs += [whole(gate), by_tokens(branch)] if extra else []
    specs += [whole(perm) for perm in perms]
    outs = [jax.ShapeDtypeStruct((tokens, width), BF16) for _ in perms]
    outs += [jax.ShapeDtypeStruct((tokens, width), F32)] if extra else []
    out_specs = [by_tokens(value) for _ in outs]
    return run(body, (tokens // TOKENS,), given, specs, outs, out_specs)


def norm_back(value, d_out, hot, hot_t, scale, beyond=None, gate=None, branch=None, perms=()):
    tokens, width = value.shape
    gated = gate is not None
    tall = [value, d_out] + ([] if beyond is None else [beyond]) + ([branch] if gated else [])
    flat = [scale] + ([gate] if gated else []) + list(perms)

    def body(hot_ref, hot_t_ref, *refs):
        talls, flats = refs[: len(tall)], refs[len(tall) : len(tall) + len(flat)]
        outs = refs[len(tall) + len(flat) :]
        total_ref, shift_ref, scale_ref, column_ref = outs[:4]
        d_out = talls[1][...]
        center, inverse = row_stats(talls[0][...])
        normed = center * inverse
        d_norm = d_out * (1.0 + pick(hot_ref[...], flats[0][...]))
        mean = jnp.mean(d_norm, axis=1, keepdims=True)
        along = jnp.mean(d_norm * normed, axis=1, keepdims=True)
        total = (d_norm - mean - normed * along) * inverse
        if beyond is not None:
            total = total + talls[2][...]
        total_ref[...] = total
        sums = [
            (shift_ref, pick(hot_t_ref[...], d_out)),
            (scale_ref, pick(hot_t_ref[...], d_out * normed)),
        ]
        if gated:
            sums.append((outs[4], pick(hot_t_ref[...], total * talls[-1][...])))
            low = (pick(hot_ref[...], flats[1][...]) * total).astype(BF16)
            column = jnp.sum(low.astype(F32), axis=0, keepdims=True)
        else:
            low = total.astype(BF16)
            column = jnp.sum(total, axis=0, keepdims=True)
        sums.append((column_ref, column))
        lows = outs[5:] if gated else outs[4:]
        if perms:
            for perm_ref, low_ref in zip(flats[2:], lows):
                low_ref[...] = matmul(low, perm_ref[...]).astype(BF16)
        else:
            lows[0][...] = low

        @pl.when(pl.program_id(0) == 0)
        def _():
            for ref, term in sums:
                ref[...] = term

        @pl.when(pl.program_id(0) > 0)
        def _():
            for ref, term in sums:
                ref[...] += term

    given = [hot, hot_t] + tall + flat
    specs = [by_tokens(hot), pl.BlockSpec((hot_t.shape[0], TOKENS), lambda j: (0, j))]
    specs += [by_tokens(part) for part in tall] + [whole(part) for part in flat]
    shape = jax.ShapeDtypeStruct
    image = shape(scale.shape, F32)
    outs = [shape((tokens, width), F32), image, image, shape((1, width), F32)]
    outs += [image] if gated else []
    outs += [shape((tokens, width), BF16) for _ in range(max(len(perms), 1))]
    out_specs = [by_tokens(part) if part.shape[0] == tokens else whole(part) for part in outs]
    return run(body, (tokens // TOKENS,), given, specs, outs, out_specs)


def slim_back(d_resid, token_hot, arrays, plan, perms, n_embed):
    width, wide = perms[0].shape[0], token_hot.shape[1]
    half = wide // 2
    rows = sum(arrays[which].shape[1] // width for which, _ in plan)
    room = rows + (-rows % 16)

    def body(d_ref, hot_ref, one_ref, two_ref, *refs):
        out_ref, gains = refs[-2], refs[-1]
        gains[...] = jnp.zeros_like(gains)
        at = 0
        for which, row in plan:
            for column in range(0, arrays[which].shape[1], width):
                gains[at : at + 1, :] = refs[which][row : row + 1, column : column + width]
                at += 1
        place = lax.broadcasted_iota(jnp.int32, (room, wide), 1)
        own = lax.broadcasted_iota(jnp.int32, (room, wide), 0) + n_embed
        own = jnp.where(own < n_embed + rows, own, -1)
        total = matmul_tn(d_ref[...], hot_ref[...])
        chosen = jnp.where(place == own, 1.0, 0.0).astype(BF16)
        total = total + matmul_tn(gains[...].astype(BF16), chosen)
        low = total.astype(BF16)
        out_ref[:, :half] = matmul(one_ref[...], low[:, :half]).astype(BF16)
        out_ref[:, half:] = matmul(two_ref[...], low[:, half:]).astype(BF16)

    given = [d_resid, token_hot] + list(perms) + list(arrays)
    outs = jax.ShapeDtypeStruct((width, wide), BF16)
    specs = [whole(value) for value in given]
    scratch = [pltpu.VMEM((room, width), F32)]
    return run(body, (1,), given, specs, outs, whole(outs), scratch)


def layout(scale_row):
    position = jnp.arange(scale_row.shape[0], dtype=jnp.int32)
    opening = scale_row == 0
    image_id = jnp.cumsum(opening.astype(jnp.int32)) - 1
    starts_at = lax.cummax(jnp.where(opening, position, 0), axis=0)
    return (image_id, position - starts_at, scale_row < LEVELS)


def adam_step(weight, moment, square, gradient, clip_factor, step_rate):
    gradient = gradient * clip_factor
    moment = BETA_ONE * moment + (1.0 - BETA_ONE) * gradient
    square = BETA_TWO * square + (1.0 - BETA_TWO) * gradient * gradient
    first_hat = moment / (1.0 - BETA_ONE**STEPS)
    second_hat = square / (1.0 - BETA_TWO**STEPS)
    weight = weight - step_rate * (first_hat / (jnp.sqrt(second_hat) + ADAM_EPS) + DECAY * weight)
    return (weight, moment, square, weight.astype(BF16))


def per_device(
    ways,
    features,
    scale_ids,
    class_ids,
    code_targets,
    token_weights,
    attn_weight,
    attn_moment,
    attn_square,
    mlp_weight,
    mlp_moment,
    mlp_square,
    ada_weight,
    ada_moment,
    ada_square,
    embed_weight,
    embed_moment,
    embed_square,
    gains_weight,
    gains_moment,
    gains_square,
    head_weight,
    head_moment,
    head_square,
):
    devices, n_vocab = ways["devices"], ways["n_vocab"]
    bits_y, bits_x, bits_z = ways["y"], ways["x"], ways["z"]
    path_one = bits_z + bits_y + bits_x
    path_two = bits_z + bits_x + bits_y
    me = lax.axis_index("dp") * n_vocab + lax.axis_index("vocab")
    rows = attn_weight.shape[0]
    width = rows * devices
    top, quarter = width // 2, width // 4
    ff_rows = FF // width
    ada_at = 7 + ff_rows
    head_at = ada_at + 8
    off_level = CLASSES + POSITIONS
    off_word = off_level + LEVELS
    length = scale_ids.shape[1]
    used = min(POSITIONS, length)
    n_gains = gains_weight.shape[0]
    n_embed = used + LEVELS + CHANNELS
    half_ff, half_qkv = FF // 2, 3 * width // 2

    def swap(value, mask):
        return swapped(value, mask, devices)

    def grown(masks, *values):
        for mask in masks:
            values = [grow(value, mask, devices) for value in values]
        return values if len(values) > 1 else values[0]

    scale_row = scale_ids[0]
    image_id, inside, counted = layout(scale_row)
    counted = counted.astype(F32)
    facts = jnp.concatenate(
        [class_ids[0], jnp.sum(counted).astype(jnp.int32)[None], jnp.zeros((119,), jnp.int32)]
    )[None]
    weighted = token_weights[0] * counted
    row_info = jnp.stack([code_targets[0].astype(F32), weighted])[None]

    embed16 = embed_weight.astype(BF16)
    slim = jnp.concatenate(
        [
            embed16[CLASSES : CLASSES + used],
            embed16[off_level : off_word + CHANNELS],
            gains_weight.astype(BF16),
        ],
        axis=0,
    )
    fill = -slim.shape[0] % 128
    slim = jnp.pad(slim, ((0, fill), (0, 0))).T
    wide = slim.shape[1]
    half_slim = wide // 2
    qkv_one = jnp.concatenate(
        [attn_weight[:, :half_qkv].astype(BF16), slim[:, :half_slim]], axis=1
    )
    qkv_two = jnp.concatenate(
        [attn_weight[:, half_qkv : 3 * width].astype(BF16), slim[:, half_slim:]], axis=1
    )
    up = jnp.concatenate(
        [
            mlp_weight[0, :, :half_ff],
            attn_weight[:, 3 * width : 3 * width + top],
            mlp_weight[0, :, half_ff:],
            attn_weight[:, 3 * width + top :],
        ],
        axis=1,
    ).astype(BF16)
    down = mlp_weight[1].astype(BF16)
    head16 = head_weight.astype(BF16)
    ada16 = ada_weight.astype(BF16)

    one_y, one_x, two_x, two_y = bits_y, bits_x, bits_x, bits_y
    slots = devices * MAXIMG
    n_x, n_y, n_z = 1 << len(bits_x), 1 << len(bits_y), 1 << len(bits_z)

    def to_two(value):
        shaped = value.reshape((2, n_x, n_y, n_z * MAXIMG) + value.shape[1:])
        return jnp.swapaxes(shaped, 1, 2).reshape(value.shape)

    def to_one(value):
        shaped = value.reshape((2, n_y, n_x, n_z * MAXIMG) + value.shape[1:])
        return jnp.swapaxes(shaped, 1, 2).reshape(value.shape)

    order = path_one + [1]
    groups = [order[at : at + 2] for at in range(0, len(order), 2)]
    parts = spread(facts, groups[0], devices)
    qkv_one, qkv_two = widen(qkv_one, bits_z[:1], devices), widen(qkv_two, bits_z[:1], devices)
    parts, qkv_one, qkv_two = tie(parts, qkv_one, qkv_two)
    parts = spread(stack(parts), groups[1], devices)
    qkv_one = widen(stack(qkv_one), bits_z[1:], devices)
    qkv_two = widen(stack(qkv_two), bits_z[1:], devices)
    parts, qkv_one, qkv_two, up, head16 = tie(parts, qkv_one, qkv_two, up, head16)
    for group in groups[2:]:
        parts = spread(stack(parts), group, devices)
    qkv_one, qkv_two = widen(stack(qkv_one), one_y, devices), widen(stack(qkv_two), two_x, devices)
    head16 = widen(head16, bits_y, devices)
    parts, up, me = tie(parts, up, me)

    facts = stack(parts)
    total_count = jnp.sum(facts[:, MAXIMG]).astype(F32)
    class_hot = (
        facts[:, :MAXIMG].reshape(slots)[:, None] == jnp.arange(CLASSES, dtype=jnp.int32)[None, :]
    ).astype(BF16)
    class_vec = matmul(class_hot, embed16[:CLASSES])
    class_act = jax.nn.silu(class_vec).astype(BF16)
    cuts = (2 * width, 5 * width)
    act_two = to_two(class_act)
    act_first = class_act.reshape(2, n_x, n_y, n_z, MAXIMG, rows)
    act_first = jnp.transpose(act_first, (0, 3, 1, 2, 4, 5)).reshape(slots, rows)
    path_first = bits_y + bits_x + bits_z
    first = matmul(act_first, ada16[:, : cuts[0]]).astype(BF16)
    first = lend(first, [1], devices)
    row_info = widen(row_info, bits_x, devices)
    first, row_info, me, head16 = tie(first, row_info, me, head16)
    perm_one, perm_one_t = hot_rows(source_rows(path_one + [1], me, rows))
    perm_two, perm_two_t = hot_rows(source_rows(path_two + [1], me, rows))
    for mask in reversed(bits_z):
        first = lend(added(*first), [mask], devices)
        (first,) = tie(first)
    first, qkv_one, qkv_two, up, row_info = tie(first, qkv_one, qkv_two, up, row_info)

    first = lend(added(*first), bits_x, devices)
    up = widen(up, bits_z[:1], devices)
    qkv_one, qkv_two = stack(qkv_one), stack(qkv_two)
    for mask in bits_x[:-1]:
        qkv_one = grow(qkv_one, mask, devices)
    for mask in bits_y[:-1]:
        qkv_two = grow(qkv_two, mask, devices)
    one_far, two_far = swap(qkv_one, bits_x[-1]), swap(qkv_two, bits_y[-1])
    row_info = widen(stack(row_info), [1], devices)
    first, row_info, qkv_one, qkv_two = tie(first, row_info, qkv_one, qkv_two)
    first = lend(added(*first), bits_y, devices)
    first, qkv_one, qkv_two, up = tie(first, qkv_one, qkv_two, up)
    first = added(*first, F32)
    up = widen(stack(up), bits_z[1:], devices)
    one_near_c, two_near_c = swap(qkv_one, 1), swap(qkv_two, 1)
    pos_hot = (inside[:, None] == jnp.arange(used, dtype=jnp.int32)[None, :]).astype(BF16)
    level_hot = (scale_row[:, None] == jnp.arange(LEVELS, dtype=jnp.int32)[None, :]).astype(BF16)
    token_hot = jnp.concatenate(
        [pos_hot, level_hot, features[0], jnp.zeros((length, wide - n_embed), BF16)], axis=1
    )
    image = jnp.arange(MAXIMG, dtype=jnp.int32)
    hot = (image_id[:, None] == image[None, :]).astype(BF16)
    hot_t = (image[:, None] == image_id[None, :]).astype(BF16)
    allowed = (image_id[:, None] == image_id[None, :]) & (scale_row[None, :] <= scale_row[:, None])
    mask_rows = jnp.where(allowed, 0.0, NEG_FILL).astype(F32)
    mods_rest = jnp.concatenate(
        [
            matmul(class_act, ada16[:, cuts[0] : cuts[1]]).astype(BF16),
            matmul(act_two, ada16[:, cuts[1] :]).astype(BF16),
        ],
        axis=1,
    )
    first, one_far, two_far, one_near_c, two_near_c, mods_rest, up, token_hot, mask_rows = tie(
        first, one_far, two_far, one_near_c, two_near_c, mods_rest, up, token_hot, mask_rows
    )
    row_info = jnp.swapaxes(stack(row_info), 0, 1).reshape(2, -1)

    one_far_c, two_far_c = swap(one_far, 1), swap(two_far, 1)
    mods_rest = lend(mods_rest, [1], devices)
    half_up = half_ff + top
    up = stack(up)
    up_one, up_two = widen(up[:, :half_up], one_y, devices), widen(up[:, half_up:], two_x, devices)
    one_far_c, two_far_c, mods_rest, first, down = tie(
        one_far_c, two_far_c, mods_rest, first, down
    )

    mods_rest = added(*mods_rest)
    cut = cuts[1] - cuts[0]
    mod_one = lend(mods_rest[:, :cut], bits_x, devices)
    mod_two = lend(mods_rest[:, cut:], bits_y, devices)
    down = widen(down, bits_z[:1], devices)
    blocks_one = [qkv_one, one_far, one_near_c, one_far_c]
    blocks_two = [qkv_two, two_far, two_near_c, two_far_c]
    slim = jnp.concatenate(
        [
            matmul_tn(stack([block[:, half_qkv:] for block in blocks_one]), perm_one),
            matmul_tn(stack([block[:, half_qkv:] for block in blocks_two]), perm_two),
        ],
        axis=0,
    )
    gain_rows = slim[n_embed : n_embed + n_gains]
    ada_bias = gain_rows[ada_at:head_at].reshape(1, -1)
    resid_in = matmul(token_hot, slim.astype(BF16)) + gain_rows[0]
    first = first + ada_bias[:, : cuts[0]]
    mods = [first[:, :width], first[:, width:]]
    u_one, u_two = norm_ahead(resid_in, hot, mods[0], mods[1], [perm_one_t, perm_two_t])
    w_qkv = ((blocks_one, (0, half_qkv)), (blocks_two, (0, half_qkv)))
    qkv_bias = jnp.concatenate(
        [gain_rows[1:2], jnp.zeros((1, width), F32), gain_rows[2:3]], axis=1
    )
    q_gain, k_gain = gain_rows[5:6], gain_rows[6:7]
    qkv = times_sets([u_one, u_two], w_qkv, qkv_bias)
    qkv, up_one, up_two, mod_one, mod_two, down, head16 = tie(
        qkv, up_one, up_two, mod_one, mod_two, down, head16
    )

    up_one, up_two = stack(up_one), stack(up_two)
    for mask in bits_x[:-1]:
        up_one = grow(up_one, mask, devices)
    for mask in bits_y[:-1]:
        up_two = grow(up_two, mask, devices)
    mod_one = lend(added(*mod_one), bits_y, devices)
    mod_two = lend(added(*mod_two), bits_x, devices)
    up_one_far, up_two_far = swap(up_one, bits_x[-1]), swap(up_two, bits_y[-1])
    down = widen(stack(down), bits_z[1:], devices)
    mixture = attend(qkv, q_gain, k_gain, mask_rows)
    mixture, mod_one, mod_two, down, up_one, up_two = tie(
        mixture, mod_one, mod_two, down, up_one, up_two
    )

    mods_rest = jnp.concatenate([added(*mod_one), added(*mod_two)], axis=1)
    mods_rest = lend(mods_rest, bits_z[-1:], devices)
    up_one_c, up_two_c = swap(up_one, 1), swap(up_two, 1)
    mix_one = matmul(mixture, perm_one_t).astype(BF16)
    mix_two = matmul(mixture, perm_two_t).astype(BF16)
    mix_one, mix_two, mods_rest, up_one_c, up_two_c, down = tie(
        mix_one, mix_two, mods_rest, up_one_c, up_two_c, down
    )
    mods_rest = lend(added(*mods_rest), bits_z[:-1], devices)
    down = stack(down)
    down_one = widen(down[:, :half_ff], one_y, devices)
    down_two = widen(down[:, half_ff:], two_x, devices)
    mix_one, mix_two, mods_rest, up_one_far, up_two_far, head16 = tie(
        mix_one, mix_two, mods_rest, up_one_far, up_two_far, head16
    )
    up_one_fc, up_two_fc = swap(up_one_far, 1), swap(up_two_far, 1)
    head16 = widen(stack(head16), bits_z[:1], devices)
    mix_one, mix_two, up_one_fc, up_two_fc = tie(mix_one, mix_two, up_one_fc, up_two_fc)
    blocks_one = [up_one, up_one_far, up_one_c, up_one_fc]
    blocks_two = [up_two, up_two_far, up_two_c, up_two_fc]
    w_up = ((blocks_one, (0, half_ff)), (blocks_two, (0, half_ff)))
    w_proj = ((blocks_one, (half_ff, half_up)), (blocks_two, (half_ff, half_up)))
    mods_rest = added(*mods_rest, F32) + ada_bias[:, cuts[0] :]
    mods += [mods_rest[:, at : at + width] for at in range(0, 6 * width, width)]
    attn_out = times_sets([mix_one, mix_two], w_proj, gain_rows[3:4])
    u_mid_one, u_mid_two, resid_mid = norm_ahead(
        resid_in, hot, mods[3], mods[4], [perm_one_t, perm_two_t], mods[2], attn_out
    )
    u_mid_one, u_mid_two, resid_mid, down_one, down_two = tie(
        u_mid_one, u_mid_two, resid_mid, down_one, down_two
    )
    down_one, down_two = stack(down_one), stack(down_two)
    for mask in bits_x[:-1]:
        down_one = grow(down_one, mask, devices)
    for mask in bits_y[:-1]:
        down_two = grow(down_two, mask, devices)
    down_one_far, down_two_far = swap(down_one, bits_x[-1]), swap(down_two, bits_y[-1])
    down_one_c, down_two_c = swap(down_one, 1), swap(down_two, 1)
    up_bias = gain_rows[7:ada_at].reshape(1, -1)
    hidden, active = times_sets([u_mid_one, u_mid_two], w_up, up_bias, bend=True)
    active, down_one_far, down_two_far, down_one_c, down_two_c, head16 = tie(
        active, down_one_far, down_two_far, down_one_c, down_two_c, head16
    )

    down_one_fc, down_two_fc = swap(down_one_far, 1), swap(down_two_far, 1)
    head16 = widen(stack(head16), bits_z[1:], devices)
    active, down_one_fc, down_two_fc = tie(active, down_one_fc, down_two_fc)
    w_down = (
        ([down_one, down_one_far, down_one_c, down_one_fc], None),
        ([down_two, down_two_far, down_two_c, down_two_fc], None),
    )
    perms = [perm_one, perm_two]
    mlp_out = back_sets(active[None], w_down, perms, gain_rows[4:5], exact=True)
    head_masks = bits_y + bits_z
    perm_head, perm_head_t = hot_rows(
        source_rows(
            [mask // n_vocab for mask in head_masks], lax.axis_index("dp"), head_weight.shape[0]
        )
    )
    head_rel, resid_out = norm_ahead(
        resid_mid, hot, mods[6], mods[7], [perm_head_t], mods[5], mlp_out
    )
    head_rel, head16 = tie(head_rel, head16)
    head16 = stack(head16)

    vocab_masks = bits_x + [1]
    rows_all = grown(bits_x[:-1], head_rel)
    far = swap(rows_all, bits_x[-1])
    near_c = swap(rows_all, 1)
    code_span = head_weight.shape[1]
    code_start = lax.axis_index("vocab") * code_span
    head_bias = lax.dynamic_slice_in_dim(gain_rows[head_at:].reshape(-1), code_start, code_span)
    code = jnp.arange(code_span, dtype=jnp.int32)[None, :] + code_start

    def part_stats(part, info):
        logits = matmul(part, head16) + head_bias
        local_max = jnp.max(logits, axis=1)
        exp_sums = jnp.sum(jnp.exp(logits - local_max[:, None]), axis=1)
        is_target = (code == info[0].astype(jnp.int32)[:, None]).astype(F32)
        picked = jnp.sum(is_target * logits, axis=1)
        return logits, is_target, jnp.stack([local_max, exp_sums, picked])

    each = rows_all.shape[0]
    info_of = [row_info[:, at * each : (at + 1) * each] for at in range(4)]
    near_rows = jnp.concatenate([rows_all, near_c], axis=0)
    near_info = jnp.concatenate([info_of[0], info_of[2]], axis=1)
    far_info = jnp.concatenate([info_of[1], info_of[3]], axis=1)
    near_logits, near_target, near_stats = part_stats(near_rows, near_info)
    near_stats, far = tie(near_stats, far)
    far_rows = jnp.concatenate([far, swap(far, 1)], axis=0)
    far_logits, far_target, far_stats = part_stats(far_rows, far_info)
    places = [x ^ c for x in (0, bits_x[-1]) for c in (0, 1)]
    places = [place ^ other for place in places for other in place_masks(bits_x[:-1])]
    stats = jnp.concatenate([near_stats, far_stats], axis=1)
    group = [stats]
    for other in place_masks(vocab_masks)[1:]:
        their = jnp.split(swap(stats, other), n_vocab, axis=1)
        group.append(
            jnp.concatenate([their[places.index(place ^ other)] for place in places], axis=1)
        )
    row_max = group[0][0]
    for other in group[1:]:
        row_max = jnp.maximum(row_max, other[0])
    totals = sum(other[1] * jnp.exp(other[0] - row_max) for other in group)
    target_logit = sum(other[2] for other in group)
    log_total = row_max + jnp.log(totals)
    loss_part = jnp.sum((near_info[1] * (log_total - target_logit)[: 2 * each])[:length])
    mid = 2 * each

    def part_back(logits, is_target, info, log_total):
        coef = info[1] / total_count
        grad = coef[:, None] * (jnp.exp(logits - log_total[:, None]) - is_target)
        return grad.astype(BF16)

    d_far_logits = part_back(far_logits, far_target, far_info, log_total[mid:])
    d_near_logits = part_back(near_logits, near_target, near_info, log_total[:mid])
    d_far = matmul_nt(d_far_logits, head16).astype(BF16)
    d_near = matmul_nt(d_near_logits, head16).astype(BF16)
    to_core = jnp.concatenate([d_near[each:], d_far[each:]], axis=0)
    back = swap(to_core, 1)
    d_far, d_near = added(d_far[:each], back[each:]), added(d_near[:each], back[:each])
    rows_all = jnp.concatenate([near_rows, far_rows], axis=0)
    d_logits = jnp.concatenate([d_near_logits, d_far_logits], axis=0)
    d_far, head16 = tie(d_far, head16)
    d_head_in = added(d_near, swap(d_far, bits_x[-1]), F32)
    for mask in reversed(bits_x[:-1]):
        d_head_in = keep_half(d_head_in.astype(BF16), mask, devices, F32)
    head_far = matmul_tn(rows_all[:, top:], d_logits).astype(BF16)
    head_near = matmul_tn(rows_all[:, :top], d_logits).astype(BF16)
    bias_grad = lax.dynamic_update_slice(
        jnp.zeros((V,), F32), jnp.sum(d_logits.astype(F32), axis=0), (code_start,)
    )
    d_head_in, head_far, head_near = tie(d_head_in, head_far, head_near)

    def cross(one, two):
        return swap(one, bits_x[-1]), swap(two, bits_y[-1])

    def join(one, two, one_back, two_back):
        one, two = added(one, one_back), added(two, two_back)
        for mask in reversed(bits_y[:-1]):
            two = keep_half(two, mask, devices)
        for mask in reversed(bits_x[:-1]):
            one = keep_half(one, mask, devices)
        half = one.shape[0] // 2
        return tuple(
            jnp.concatenate([one[at : at + half], two[at : at + half]], axis=1) for at in (0, half)
        )

    def turn(one, two, one_back, two_back):
        one, one_far = halves_of(one, one_back)
        two, two_far = halves_of(two, two_back)
        for mask in reversed(bits_x[:-1]):
            whole_one = jnp.concatenate([one, one_far], axis=0)
            one, one_far = halves_of(
                whole_one[: whole_one.shape[0] // 2],
                swap(whole_one[whole_one.shape[0] // 2 :], mask),
            )
        for mask in reversed(bits_y[:-1]):
            whole_two = jnp.concatenate([two, two_far], axis=0)
            two, two_far = halves_of(
                whole_two[: whole_two.shape[0] // 2],
                swap(whole_two[whole_two.shape[0] // 2 :], mask),
            )
        return one, one_far, two, two_far

    def cross_back(one_far, two_far):
        return swap(one_far, bits_y[-1]), swap(two_far, bits_x[-1])

    perms = [perm_one, perm_two]
    ones, twos = (0, half_ff), (half_ff, FF)
    q_ones, q_twos = (0, half_qkv), (half_qkv, 3 * width)
    downs, ups = [None, None], [u_mid_one, u_mid_two]
    mixes, ins = [mix_one, mix_two], [u_one, u_two]
    ffs, projs, qkvs = [ones, twos], [(0, top), (top, width)], [q_ones, q_twos]

    active = active[None]
    head_back = swap(head_far, head_masks[-1])
    d_head_in = in_halves_outside(lambda part: matmul(part, perm_head), d_head_in)
    d_resid_out, d_shift_head, d_scale_head, down_bias, d_gate_two, *downs = norm_back(
        resid_out,
        d_head_in,
        hot,
        hot_t,
        mods[7],
        gate=mods[5],
        branch=mlp_out,
        perms=[perm_one_t, perm_two_t],
    )
    down_f = grad_sets(downs, active, ffs)
    downs, down_f = tie(downs, down_f)
    down_b = swap(down_f, 1)
    d_hid, up_bias_sum = times_sets(downs, w_down, hidden=hidden)
    d_hid, down_b = tie(d_hid, down_b)
    d_hid = d_hid[None]
    down_n1, down_f1, down_n2, down_f2 = grad_sets(downs, active, ffs, down_b)
    up_f = grad_sets(ups, d_hid, ffs)
    d_hid, down_f1, down_f2, down_n1, down_n2, up_f = tie(
        d_hid, down_f1, down_f2, down_n1, down_n2, up_f
    )
    down_x1, down_x2 = cross(down_f1, down_f2)
    up_b = swap(up_f, 1)
    d_u = back_sets(d_hid, w_up, perms)
    d_u, up_b = tie(d_u, up_b)
    up_n1, up_f1, up_n2, up_f2 = grad_sets(ups, d_hid, ffs, up_b)
    d_resid_mid, d_shift_two, d_scale_two, proj_bias, d_gate_one, d_low = norm_back(
        resid_mid, d_u, hot, hot_t, mods[4], beyond=d_resid_out, gate=mods[2], branch=attn_out
    )
    d_low, down_x1, down_x2, up_f1, up_f2, up_n1, up_n2, head_back, head_near = tie(
        d_low, down_x1, down_x2, up_f1, up_f2, up_n1, up_n2, head_back, head_near
    )
    down_n1, down_f1, down_n2, down_f2 = turn(down_n1, down_n2, down_x1, down_x2)
    d_low, down_f1, down_f2, up_f1, up_f2, head_back = tie(
        d_low, down_f1, down_f2, up_f1, up_f2, head_back
    )
    head_near, head_far = halves_of(head_near, head_back)
    down_x1, down_x2 = cross_back(down_f1, down_f2)
    up_x1, up_x2 = cross(up_f1, up_f2)
    head_back = swap(head_far, head_masks[-2])
    d_low = d_low[None]
    proj_f = grad_sets(mixes, d_low, projs)
    d_mix = back_sets(d_low, w_proj, perms, out=BF16)
    d_qkv, attn_sums = attend_back(qkv, q_gain, k_gain, mask_rows, d_mix)
    d_qkv, proj_f, down_x1, down_x2, down_n1, down_n2, up_x1, up_x2, head_back, head_near = tie(
        d_qkv, proj_f, down_x1, down_x2, down_n1, down_n2, up_x1, up_x2, head_back, head_near
    )
    up_n1, up_f1, up_n2, up_f2 = turn(up_n1, up_n2, up_x1, up_x2)
    down_near, down_far = join(down_n1, down_n2, down_x1, down_x2)
    d_qkv, up_f1, up_f2, down_far, proj_f = tie(d_qkv, up_f1, up_f2, down_far, proj_f)
    up_x1, up_x2 = cross_back(up_f1, up_f2)
    down_back = swap(down_far, bits_z[-1])
    proj_b = swap(proj_f, 1)
    qkv_f = grad_sets(ins, d_qkv, qkvs)
    d_qkv, qkv_f, proj_b = tie(d_qkv, qkv_f, proj_b)
    qkv_b = swap(qkv_f, 1)
    head_near = added(head_near, head_back)
    head_grad = lend(head_near, head_masks[:-2], devices)
    d_u = back_sets(d_qkv, w_qkv, perms)
    d_u, qkv_b, up_x1, up_x2, down_back, down_near = tie(
        d_u, qkv_b, up_x1, up_x2, down_back, down_near
    )
    down_near, down_far = halves_of(down_near, down_back)
    d_u, down_far, qkv_b, up_x1, up_x2 = tie(d_u, down_far, qkv_b, up_x1, up_x2)
    down_back = swap(down_far, bits_z[-2])
    d_resid_in, d_shift_one, d_scale_one, word_bias, d_res16 = norm_back(
        resid_in, d_u, hot, hot_t, mods[1], beyond=d_resid_mid
    )
    d_mod = jnp.concatenate(
        [
            d_shift_one,
            d_scale_one,
            d_gate_one,
            d_shift_two,
            d_scale_two,
            d_gate_two,
            d_shift_head,
            d_scale_head,
        ],
        axis=1,
    ).astype(BF16)
    ada_sums = jnp.sum(d_mod.astype(F32), axis=0, keepdims=True)
    arrays = [word_bias, attn_sums, proj_bias, down_bias, up_bias_sum, ada_sums, bias_grad[None]]
    plan = [(0, 0), (1, 2), (1, 3), (2, 0), (3, 0), (1, 0), (1, 1), (4, 0), (5, 0), (6, 0)]
    d_slim = slim_back(d_res16, token_hot, arrays, plan, perms, n_embed)
    d_slim, d_mod, qkv_b = tie(d_slim, d_mod, qkv_b)
    slim_b = swap(d_slim[top:], 1)
    qkv_n1, qkv_f1, qkv_n2, qkv_f2 = grad_sets(ins, d_qkv, qkvs, qkv_b)
    proj_n1, proj_f1, proj_n2, proj_f2 = grad_sets(mixes, d_low, projs, proj_b)
    (
        qkv_n1,
        qkv_f1,
        qkv_n2,
        qkv_f2,
        proj_n1,
        proj_f1,
        proj_n2,
        proj_f2,
        slim_b,
        down_back,
        up_x1,
        up_x2,
        head_grad,
    ) = tie(
        qkv_n1,
        qkv_f1,
        qkv_n2,
        qkv_f2,
        proj_n1,
        proj_f1,
        proj_n2,
        proj_f2,
        slim_b,
        down_back,
        up_x1,
        up_x2,
        head_grad,
    )
    head_grad = added(*head_grad, F32)

    def beside(*parts):
        return jnp.concatenate(parts, axis=1)

    far_slim = added(d_slim[quarter:top], slim_b[quarter:])
    qkv_f1 = beside(qkv_f1, proj_f1, far_slim[:, :half_slim])
    qkv_f2 = beside(qkv_f2, proj_f2, far_slim[:, half_slim:])
    up_near, up_far = join(up_n1, up_n2, up_x1, up_x2)
    d_mod, up_far, qkv_f1, qkv_f2 = tie(d_mod, up_far, qkv_f1, qkv_f2)
    qkv_x1, qkv_x2 = cross(qkv_f1, qkv_f2)
    up_back = swap(up_far, bits_z[-1])
    all_mod = widen(d_mod, bits_z, devices)
    near_slim = added(d_slim[:quarter], slim_b[:quarter])
    qkv_n1 = beside(qkv_n1, proj_n1, near_slim[:, :half_slim])
    qkv_n2 = beside(qkv_n2, proj_n2, near_slim[:, half_slim:])
    qkv_x1, qkv_x2, qkv_n1, qkv_n2, all_mod, up_back, up_near = tie(
        qkv_x1, qkv_x2, qkv_n1, qkv_n2, all_mod, up_back, up_near
    )
    qkv_n1, qkv_f1, qkv_n2, qkv_f2 = turn(qkv_n1, qkv_n2, qkv_x1, qkv_x2)
    up_near, up_far = halves_of(up_near, up_back)
    qkv_x1, qkv_x2 = cross_back(qkv_f1, qkv_f2)
    up_back = swap(up_far, bits_z[-2])
    all_mod = stack(all_mod)
    all_first = widen(all_mod[:, : cuts[1]], bits_y, devices)
    all_two = widen(all_mod[:, cuts[1] :], bits_x, devices)
    qkv_x1, qkv_x2, qkv_n1, qkv_n2, up_back, all_first, all_two = tie(
        qkv_x1, qkv_x2, qkv_n1, qkv_n2, up_back, all_first, all_two
    )
    near, far = join(qkv_n1, qkv_n2, qkv_x1, qkv_x2)
    attn_back = swap(far, bits_z[-1])
    all_two = widen(stack(all_two), bits_y, devices)
    all_first = widen(stack(all_first), bits_x, devices)
    attn_back, near, all_two, all_first = tie(attn_back, near, all_two, all_first)
    near, far = halves_of(near, attn_back)
    attn_back = swap(far, bits_z[-2])
    all_two = grown([1], stack(all_two))
    all_first = grown([1], stack(all_first))

    def close(near, back):
        masks = bits_z[:-2]
        near = added(near, back, BF16 if masks else F32)
        return keep_all(near, masks, devices)

    up_rows, down_rows = close(up_near, up_back), close(down_near, down_back)
    mlp_grad = jnp.stack([up_rows, down_rows])
    ada_grad = jnp.concatenate([matmul_tn(class_act, all_first), matmul_tn(act_two, all_two)], axis=1)
    d_class_act = matmul_nt(all_first, ada16[:, : cuts[1]]) + to_one(
        matmul_nt(all_two, ada16[:, cuts[1] :])
    )
    _, silu_back = jax.vjp(jax.nn.silu, class_vec)
    d_class = precise_tn(class_hot.astype(F32), silu_back(d_class_act)[0])
    squares_local = jnp.zeros((), F32)
    for gradient in (mlp_grad, ada_grad, d_class, head_grad):
        squares_local = squares_local + jnp.sum(gradient * gradient)
    squares_local, mlp_grad, ada_grad, d_class, near, attn_back = tie(
        squares_local, mlp_grad, ada_grad, d_class, near, attn_back
    )
    attn_rows = close(near, attn_back)
    squares_local = squares_local + jnp.sum(attn_rows * attn_rows)
    half_attn = half_qkv + top
    half_all = half_attn + half_slim
    attn_grad = jnp.concatenate(
        [
            attn_rows[:, :half_qkv],
            attn_rows[:, half_all : half_all + half_qkv],
            attn_rows[:, half_qkv:half_attn],
            attn_rows[:, half_all + half_qkv : half_all + half_attn],
        ],
        axis=1,
    )
    slim_grad = jnp.concatenate(
        [attn_rows[:, half_attn:half_all], attn_rows[:, half_all + half_attn :]], axis=1
    ).T
    embed_grad = jnp.concatenate(
        [
            d_class,
            slim_grad[:used],
            jnp.zeros((POSITIONS - used, rows), F32),
            slim_grad[used:n_embed],
        ],
        axis=0,
    )
    gains_grad = slim_grad[n_embed : n_embed + n_gains]
    gradients = (attn_grad, mlp_grad, ada_grad, embed_grad, gains_grad, head_grad)
    sums = sum_all(
        jnp.stack([squares_local, loss_part])[None], [1] + bits_x + bits_y + bits_z, devices
    )
    total_sq, loss_sum = sums[0, 0], sums[0, 1]
    grad_norm = jnp.sqrt(total_sq)
    clip_factor = jnp.minimum(1.0, CLIP_NORM / (grad_norm + 1e-06))
    masters = (attn_weight, mlp_weight, ada_weight, embed_weight, gains_weight, head_weight)
    moments = (attn_moment, mlp_moment, ada_moment, embed_moment, gains_moment, head_moment)
    squares = (attn_square, mlp_square, ada_square, embed_square, gains_square, head_square)
    updates = []
    for number in range(6):
        updates.extend(
            adam_step(
                masters[number],
                moments[number],
                squares[number],
                gradients[number],
                clip_factor,
                RATES[number],
            )
        )
    return tuple(updates) + (grad_norm, loss_sum, total_count)


def solution(mesh):
    n_dp, n_vocab = mesh.shape["dp"], mesh.shape["vocab"]
    n_z = 1 << (n_dp.bit_length() // 2)
    devices = n_dp * n_vocab

    def bits(least, top):
        found = []
        while least < top:
            found, least = [least] + found, least * 2
        return found

    ways = {"devices": devices, "n_vocab": n_vocab}
    ways["x"] = bits(2, n_vocab)
    ways["y"] = bits(n_vocab, devices // n_z)
    ways["z"] = bits(devices // n_z, devices)
    every = ("dp", "vocab")
    by_row = P(every, None)
    by_mid = P(None, every, None)
    by_column = P(None, every)
    head = P("dp", "vocab")
    placed = (P(every, None, None), by_row, by_row, by_row, by_row)
    for spec in (by_row, by_mid, by_row, by_column, by_column, head):
        placed = placed + (spec,) * 3
    given = ()
    for spec in (by_row, by_mid, by_row, by_column, by_column, head):
        given = given + (spec,) * 4

    def step(*arrays):
        return per_device(ways, *arrays)

    return jax.shard_map(
        step, mesh=mesh, in_specs=placed, out_specs=given + (P(), P(), P()), check_vma=False
    )
```
